32 devices in a mesh: node: 4 (over y, x), gx: 4 (over z), gy: 2 (over core).
Axes of the slice: x: 2, y: 2, z: 4, core: 2. Of those that a mesh axis runs over, the one named last changes fastest.
Arguments:
- initial: float32 [5, 48, 32, 128], P(None, 'gx', 'gy'), may hold values from -8 to 50, as said below
- guesses: float32 [4, 5, 48, 32, 128], P('node', None, 'gx', 'gy'), may hold values from -8 to 50, as said below
Outputs:
- node_states: float32 [4, 5, 48, 32, 128], P('node', None, 'gx', 'gy')
The draws below stay inside these ranges and needn't reach their ends.
Inputs may be any that keep to these rules, and one draw needn't show every extreme that they name: `initial`: each cell holds density, three momenta and total energy of a gas with ratio of heats 1.4: density 0.5 to 2.5, pressure 0.3 to 9, velocity components at most 3 in magnitude. `guesses`: each cell of each node holds density, three momenta and total energy of a gas with ratio of heats 1.4: density 0.5 to 2.5, pressure 0.3 to 9, velocity components at most 3 in magnitude.
All inputs are finite; a program needn't handle non-finite values.
Results may differ from the reference program's by a relative error of at most 0.0001.
Values sent between devices are 32-bit elements; how exact they have to be, the bound alone decides.
No kernel may reach another device: no remote copies, remote signals or barrier semaphores. Data moves between devices by JAX's collectives and lax.ppermute only.
A program may use at most 64 MiB of HBM per device.

```python
import math
import jax
import jax.numpy as jnp
from jax import lax

NODES = 4
SWEEPS = 2
NX = 48
NY = 32
NZ = 128


def make_states(base_key, count):
    subkeys = jax.random.split(base_key, 3)
    grid_shape = (count, NX, NY, NZ)
    position = jnp.arange(NX, dtype=jnp.float32) / max(NX - 1, 1)
    rising = (9.0 ** position)[None, :, None, None]
    density = jnp.exp(jax.random.uniform(subkeys[0], grid_shape, jnp.float32, math.log(0.5), math.log(2.0)))
    velocity = jnp.clip(jax.random.normal(subkeys[1], (3,) + grid_shape, jnp.float32), -3.0, 3.0)
    base_pressure = jnp.exp(jax.random.uniform(subkeys[2], grid_shape, jnp.float32, math.log(0.3), 0.0))
    pressure = base_pressure * rising
    momentum = density[None] * velocity
    energy = pressure / 0.4 + 0.5 * density * jnp.sum(velocity * velocity, axis=0)
    return jnp.stack([density, momentum[0], momentum[1], momentum[2], energy], axis=1)


def draw_initial(key, part):
    return make_states(jax.random.fold_in(key, 11), 1)[0]


def draw_guesses(key, part):
    return make_states(jax.random.fold_in(key, 23), NODES)


def setup_inputs(seed: int = 0) -> dict:
    arg_keys = jax.random.split(jax.random.key(seed), 3)
    initial = draw_initial(jax.random.fold_in(arg_keys[2], 71), 0)
    guesses = draw_guesses(jax.random.fold_in(arg_keys[2], 71), 0)
    return dict(initial=initial, guesses=guesses)


heat_ratio = 1.4
step_size = 0.025
density_floor = 0.5
pressure_floor = 0.25
epsilon = 1e-06
radau_weights = [[0.112999479323156, -0.040309220723522, 0.025802377420336, -0.009904676507266], [0.2343839957474, 0.206892573935359, -0.047857128048541, 0.016047422806516], [0.21668178462325, 0.406123263867373, 0.189036518170056, -0.024182104899833], [0.220462211176768, 0.388193468843172, 0.32884431998006, 0.0625]]

def primitives(fields):
    density = jnp.maximum(fields[0], density_floor)
    velocity = fields[1:4] / density
    pressure = jnp.maximum(0.4 * (fields[4] - 0.5 * lax.optimization_barrier(jnp.sum(fields[1:4] * velocity, axis=0))), pressure_floor)
    return (density, velocity, pressure)

def wave_speeds(fields):
    density, velocity, pressure = primitives(fields)
    sound = jnp.sqrt(heat_ratio * pressure / density)
    return tuple((jnp.max(jnp.abs(velocity[direction]) + sound) for direction in range(3)))

def reconstruct(first, second, third, fourth, fifth):
    cand_zero = (2.0 * first - 7.0 * second + 11.0 * third) / 6.0
    cand_one = (-second + 5.0 * third + 2.0 * fourth) / 6.0
    cand_two = (2.0 * third + 5.0 * fourth - fifth) / 6.0
    smooth_zero = 13.0 / 12.0 * (first - 2.0 * second + third) ** 2 + 0.25 * (first - 4.0 * second + 3.0 * third) ** 2
    smooth_one = 13.0 / 12.0 * (second - 2.0 * third + fourth) ** 2 + 0.25 * (second - fourth) ** 2
    smooth_two = 13.0 / 12.0 * (third - 2.0 * fourth + fifth) ** 2 + 0.25 * (3.0 * third - 4.0 * fourth + fifth) ** 2
    weight_zero = 0.1 / (epsilon + smooth_zero) ** 2
    weight_one = 0.6 / (epsilon + smooth_one) ** 2
    weight_two = 0.3 / (epsilon + smooth_two) ** 2
    return (weight_zero * cand_zero + weight_one * cand_one + weight_two * cand_two) / (weight_zero + weight_one + weight_two)

def flux_along(extended, spatial_axis, alpha):
    direction = spatial_axis - 1
    density, velocity, pressure = primitives(extended)
    speed = velocity[direction]
    components = [extended[direction + 1], extended[1] * speed, extended[2] * speed, extended[3] * speed, (extended[4] + pressure) * speed]
    components[direction + 1] = components[direction + 1] + pressure
    fluxes = jnp.stack(components)
    right_going = 0.5 * (fluxes + alpha * extended)
    left_going = 0.5 * (fluxes - alpha * extended)
    length = extended.shape[spatial_axis] - 6

    def window(values, begin):
        return lax.slice_in_dim(values, begin, begin + length + 1, axis=spatial_axis)
    interface = reconstruct(window(right_going, 0), window(right_going, 1), window(right_going, 2), window(right_going, 3), window(right_going, 4))
    interface = interface + reconstruct(window(left_going, 5), window(left_going, 4), window(left_going, 3), window(left_going, 2), window(left_going, 1))
    return lax.slice_in_dim(interface, 0, length, axis=spatial_axis) - lax.slice_in_dim(interface, 1, length + 1, axis=spatial_axis)

def wrapped(fields, spatial_axis):
    size_here = fields.shape[spatial_axis]
    lower = lax.slice_in_dim(fields, size_here - 3, size_here, axis=spatial_axis)
    upper = lax.slice_in_dim(fields, 0, 3, axis=spatial_axis)
    return jnp.concatenate([lower, fields, upper], axis=spatial_axis)

def evaluate(fields):
    alphas = wave_speeds(fields)
    summed = flux_along(wrapped(fields, 1), 1, alphas[0])
    summed = summed + flux_along(wrapped(fields, 2), 2, alphas[1])
    summed = summed + flux_along(wrapped(fields, 3), 3, alphas[2])
    return summed

def reference(initial, guesses):
    current = [guesses[node] for node in range(NODES)]
    for sweep_index in range(SWEEPS):
        rates = [evaluate(fields) for fields in current]
        updated = []
        for target in range(NODES):
            combined = jnp.zeros_like(initial)
            for source in range(NODES):
                combined = combined + radau_weights[target][source] * rates[source]
            updated.append(initial + step_size * combined)
        current = updated
    return jnp.stack(current)
```

```python
import functools

import jax
import jax.numpy as jnp
from jax import lax
from jax.experimental import pallas as pl
from jax.experimental.pallas import tpu as pltpu
from jax.sharding import PartitionSpec as P

SWEEPS = 2
HALO = 3
COMPONENTS = 5

heat_ratio = 1.4
step_size = 0.025
density_floor = 0.5
pressure_floor = 0.25
epsilon = 1e-06
radau_weights = [
    [0.112999479323156, -0.040309220723522, 0.025802377420336, -0.009904676507266],
    [0.2343839957474, 0.206892573935359, -0.047857128048541, 0.016047422806516],
    [0.21668178462325, 0.406123263867373, 0.189036518170056, -0.024182104899833],
    [0.220462211176768, 0.388193468843172, 0.32884431998006, 0.0625],
]


def reciprocal(value):
    return pl.reciprocal(value, approx=True)


def primitives(fields):
    inverse = 1.0 / jnp.maximum(fields[0], density_floor)
    velocity = [fields[k] * inverse for k in (1, 2, 3)]
    energy = fields[1] * velocity[0] + fields[2] * velocity[1] + fields[3] * velocity[2]
    pressure = jnp.maximum(0.4 * (fields[4] - 0.5 * energy), pressure_floor)
    return inverse, velocity, pressure


def signal_speeds(fields):
    inverse, velocity, pressure = primitives(fields)
    sound = jnp.sqrt(heat_ratio * pressure * inverse)
    return [jnp.abs(v) + sound for v in velocity]


def half_fluxes(half, speed, half_pressure, direction):
    flux = [half[direction + 1]] + [half[k] * speed for k in (1, 2, 3)]
    flux.append((half[4] + half_pressure) * speed)
    flux[direction + 1] = flux[direction + 1] + half_pressure
    return flux


def splits(fields, alphas, directions=(0, 1, 2)):
    _, velocity, pressure = primitives(fields)
    half = [0.5 * field for field in fields]
    half_pressure = 0.5 * pressure
    out = []
    for direction in directions:
        flux = half_fluxes(half, velocity[direction], half_pressure, direction)
        signal = [alphas[direction] * value for value in half]
        out.append(
            ([f + s for f, s in zip(flux, signal)], [f - s for f, s in zip(flux, signal)])
        )
    return out


def cell_terms(below, above):
    second = above - below
    both = below + above
    square = second * second
    middle = 0.25 * (both * both) + ((13.0 / 12.0) * square + epsilon)
    outer = middle + square
    cross = both * second
    return second, outer + cross, middle, outer - cross


def correction(first, middle, last, third_first, third_last):
    ratio_first = middle * reciprocal(first)
    ratio_last = middle * reciprocal(last)
    weight_first = ratio_first * ratio_first
    weight_last = 1.5 * (ratio_last * ratio_last)
    total = (6.0 + weight_first) + (weight_last + weight_last)
    return (weight_first * third_first + weight_last * third_last) * reciprocal(total)


def stream(load, store, count):
    plus, minus, centre = {}, {}, {}
    terms_plus, terms_minus, third_plus, third_minus, interface = {}, {}, {}, {}, {}
    differences_plus, differences_minus = {}, {}
    plus[0], minus[0] = load(0)
    for j in range(1, count + 2 * HALO):
        plus[j], minus[j] = load(j)
        differences_plus[j] = plus[j] - plus[j - 1]
        differences_minus[j] = minus[j] - minus[j - 1]
        cell = j - 1
        if cell < 1:
            continue
        terms_plus[cell] = cell_terms(differences_plus[cell], differences_plus[j])
        terms_minus[cell] = cell_terms(differences_minus[cell], differences_minus[j])
        if 2 <= cell <= count + 3:
            centre[cell] = 6.0 * (plus[cell] + minus[cell]) - (
                terms_plus[cell][0] + terms_minus[cell][0]
            )
        if cell < 2:
            continue
        third_plus[cell] = terms_plus[cell][0] - terms_plus[cell - 1][0]
        third_minus[cell] = terms_minus[cell][0] - terms_minus[cell - 1][0]
        if cell < 4:
            continue
        at = cell - 2
        right = correction(
            terms_plus[at - 1][1], terms_plus[at][2], terms_plus[at + 1][3], third_plus[at], third_plus[at + 1]
        )
        left = correction(
            terms_minus[at + 2][3], terms_minus[at + 1][2], terms_minus[at][1],
            third_minus[at + 2], third_minus[at + 1],
        )
        interface[at] = (third_plus[at + 1] - third_minus[at + 1]) - 4.0 * (right - left)
        if at >= 3:
            store(at - 3, (centre[at - 1] - centre[at + 1]) + (interface[at - 1] - interface[at]))


def rolled(plus, minus):
    size = plus.shape[-1]

    def nxt(value, by=1):
        return pltpu.roll(value, size - by, value.ndim - 1)

    def prev(value):
        return pltpu.roll(value, 1, value.ndim - 1)

    above = nxt(plus) - plus
    second_plus, first_p, middle_p, last_p = cell_terms(prev(above), above)
    above = nxt(minus) - minus
    second_minus, first_m, middle_m, last_m = cell_terms(prev(above), above)
    centre = 6.0 * (plus + minus) - (second_plus + second_minus)
    third_plus = nxt(second_plus) - second_plus
    third_minus = nxt(second_minus) - second_minus
    right = correction(prev(first_p), middle_p, nxt(last_p), prev(third_plus), third_plus)
    left = correction(nxt(last_m, 2), nxt(middle_m), first_m, nxt(third_minus), third_minus)
    interface = (third_plus - third_minus) - 4.0 * (right - left)
    return (prev(centre) - nxt(centre)) + (prev(interface) - interface)


def rhs_kernel(u_ref, xlo_ref, xhi_ref, yh_ref, al_ref, out_ref, xp, xm, yp, ym, fy):
    comps, nx, ny, nz = u_ref.shape
    rows = yh_ref.shape[1]
    every = range(comps)
    alphas = [al_ref[k : k + 1, :] for k in range(3)]

    def own(i, carry):
        fields = [u_ref[c, i] for c in every]
        along_x, along_y, along_z = splits(fields, alphas)
        for c in every:
            xp[i + HALO, c * ny : (c + 1) * ny, :] = along_x[0][c]
            xm[i + HALO, c * ny : (c + 1) * ny, :] = along_x[1][c]
            for t in range(0, ny, 8):
                at = pl.ds((HALO + t) * rows + c * nx + i, 8, stride=rows)
                yp[at, :] = along_y[0][c][t : t + 8]
                ym[at, :] = along_y[1][c][t : t + 8]
            out_ref[c, i] = rolled(along_z[0][c], along_z[1][c])
        return carry

    lax.fori_loop(0, nx, own, 0)

    for ref, start in ((xlo_ref, 0), (xhi_ref, nx + HALO)):

        def ghost_x(i, carry, ref=ref, start=start):
            ((p, m),) = splits([ref[c, i] for c in every], alphas, (0,))
            for c in every:
                xp[start + i, c * ny : (c + 1) * ny, :] = p[c]
                xm[start + i, c * ny : (c + 1) * ny, :] = m[c]
            return carry

        lax.fori_loop(0, HALO, ghost_x, 0)

    def ghost_y(i, carry):
        row = jnp.where(i < HALO, i, i + ny) * rows
        ((p, m),) = splits([yh_ref[i, c * nx : (c + 1) * nx, :] for c in every], alphas, (1,))
        for c in every:
            yp[pl.ds(row + c * nx, nx), :] = p[c]
            ym[pl.ds(row + c * nx, nx), :] = m[c]
        return carry

    lax.fori_loop(0, 2 * HALO, ghost_y, 0)

    def along_second(b, carry):
        first = pl.multiple_of(b * 8, 8)

        def load(j):
            return yp[pl.ds(j * rows + first, 8), :], ym[pl.ds(j * rows + first, 8), :]

        def store(i, value):
            fy[pl.ds(i * rows + first, 8), :] = value

        stream(load, store, ny)
        return carry

    lax.fori_loop(0, rows // 8, along_second, 0)

    for c in every:

        def along_first(b, carry, c=c):
            first = pl.multiple_of(b * 8, 8)

            def load(j):
                at = pl.ds(c * ny + first, 8)
                return xp[j, at, :], xm[j, at, :]

            def store(i, value):
                cross = fy[pl.ds(first * rows + c * nx + i, 8, stride=rows), :]
                here = pl.ds(first, 8)
                out_ref[c, i, here, :] = out_ref[c, i, here, :] + value + cross

            stream(load, store, nx)
            return carry

        lax.fori_loop(0, ny // 8, along_first, 0)


def right_hand_side(fields, lower, upper, sides, alphas):
    comps, nx, ny, nz = fields.shape
    rows = sides.shape[1]
    vmem = pl.BlockSpec(memory_space=pltpu.VMEM)
    return pl.pallas_call(
        rhs_kernel,
        out_shape=jax.ShapeDtypeStruct(fields.shape, jnp.float32),
        in_specs=[vmem] * 5,
        out_specs=vmem,
        scratch_shapes=[
            pltpu.VMEM((nx + 2 * HALO, comps * ny, nz), jnp.float32),
            pltpu.VMEM((nx + 2 * HALO, comps * ny, nz), jnp.float32),
            pltpu.VMEM(((ny + 2 * HALO) * rows, nz), jnp.float32),
            pltpu.VMEM(((ny + 2 * HALO) * rows, nz), jnp.float32),
            pltpu.VMEM((ny * rows, nz), jnp.float32),
        ],
        compiler_params=pltpu.CompilerParams(vmem_limit_bytes=24 * 1024 * 1024),
        cost_estimate=pl.CostEstimate(flops=30_000_000, bytes_accessed=1_500_000, transcendentals=0),
        name="right_hand_side",
    )(fields, lower, upper, sides, alphas)


def shifted(value, axis, by):
    count = lax.axis_size(axis)
    return lax.ppermute(value, axis, [(i, (i + by) % count) for i in range(count)])


def local_speeds(fields):
    return jnp.stack([jnp.max(s) for s in signal_speeds([fields[c] for c in range(COMPONENTS)])])


def evaluate(fields):
    comps, nx, ny, nz = fields.shape
    speeds = lax.pmax(local_speeds(fields), ("gx", "gy"))
    alphas = jnp.broadcast_to(jnp.pad(speeds, (0, 5))[:, None], (8, nz))
    lower = shifted(fields[:, -HALO:], "gx", 1)
    upper = shifted(fields[:, :HALO], "gx", -1)
    leading = jnp.moveaxis(fields, 2, 0).reshape(ny, comps * nx, nz)
    pad = -(comps * nx) % 8
    leading = jnp.pad(leading, ((0, 0), (0, pad), (0, 0)))
    sides = jnp.concatenate([shifted(leading[-HALO:], "gy", 1), shifted(leading[:HALO], "gy", -1)])
    return right_hand_side(fields, lower, upper, sides, alphas)


def local(initial, guesses):
    weights_table = jnp.array(radau_weights, jnp.float32) * (step_size / 12.0)
    node_index = lax.axis_index("node")
    current = guesses[0]
    for sweep_index in range(SWEEPS):
        rate = evaluate(current)
        own_row = lax.dynamic_index_in_dim(weights_table, node_index, 0, keepdims=False)
        gathered = lax.all_gather(rate[None], "node", axis=0, tiled=True)
        current = initial + jnp.sum(own_row[:, None, None, None, None] * gathered, axis=0)
    return current[None]


def solution(mesh):
    return jax.shard_map(
        local,
        mesh=mesh,
        in_specs=(P(None, "gx", "gy", None), P("node", None, "gx", "gy", None)),
        out_specs=P("node", None, "gx", "gy", None),
        check_vma=False,
    )
```

```python
import functools

import jax
import jax.numpy as jnp
from jax import lax
from jax.experimental import pallas as pl
from jax.experimental.pallas import tpu as pltpu
from jax.sharding import PartitionSpec as P

SWEEPS = 2
HALO = 3
COMPONENTS = 5
TILE = 8

heat_ratio = 1.4
step_size = 0.025
density_floor = 0.5
pressure_floor = 0.25
epsilon = 1e-06
radau_weights = [
    [0.112999479323156, -0.040309220723522, 0.025802377420336, -0.009904676507266],
    [0.2343839957474, 0.206892573935359, -0.047857128048541, 0.016047422806516],
    [0.21668178462325, 0.406123263867373, 0.189036518170056, -0.024182104899833],
    [0.220462211176768, 0.388193468843172, 0.32884431998006, 0.0625],
]


def reciprocal(value):
    return pl.reciprocal(value, approx=True)


def primitives(fields):
    inverse = 1.0 / jnp.maximum(fields[0], density_floor)
    velocity = [fields[k] * inverse for k in (1, 2, 3)]
    energy = fields[1] * velocity[0] + fields[2] * velocity[1] + fields[3] * velocity[2]
    pressure = jnp.maximum(0.4 * (fields[4] - 0.5 * energy), pressure_floor)
    return inverse, velocity, pressure


def signal_speeds(fields):
    inverse, velocity, pressure = primitives(fields)
    sound = jnp.sqrt(heat_ratio * pressure * inverse)
    return [jnp.abs(v) + sound for v in velocity]


def half_fluxes(half, speed, half_pressure, direction):
    flux = [half[direction + 1]] + [half[k] * speed for k in (1, 2, 3)]
    flux.append((half[4] + half_pressure) * speed)
    flux[direction + 1] = flux[direction + 1] + half_pressure
    return flux


def splits(fields, alphas, directions=(0, 1, 2)):
    _, velocity, pressure = primitives(fields)
    half = [0.5 * field for field in fields]
    half_pressure = 0.5 * pressure
    out = []
    for direction in directions:
        flux = half_fluxes(half, velocity[direction], half_pressure, direction)
        signal = [alphas[direction] * value for value in half]
        out.append(
            ([f + s for f, s in zip(flux, signal)], [f - s for f, s in zip(flux, signal)])
        )
    return out


def cell_terms(below, above):
    second = above - below
    both = below + above
    square = second * second
    middle = 0.25 * (both * both) + ((13.0 / 12.0) * square + epsilon)
    outer = middle + square
    cross = both * second
    return second, outer + cross, middle, outer - cross


def correction(first, middle, last, third_first, third_last):
    ratio_first = middle * reciprocal(first)
    ratio_last = middle * reciprocal(last)
    weight_first = ratio_first * ratio_first
    weight_last = 1.5 * (ratio_last * ratio_last)
    total = (6.0 + weight_first) + (weight_last + weight_last)
    return (weight_first * third_first + weight_last * third_last) * reciprocal(total)


def stream(load, store, count):
    plus, minus, centre = {}, {}, {}
    terms_plus, terms_minus, third_plus, third_minus, interface = {}, {}, {}, {}, {}
    differences_plus, differences_minus = {}, {}
    plus[0], minus[0] = load(0)
    for j in range(1, count + 2 * HALO):
        plus[j], minus[j] = load(j)
        differences_plus[j] = plus[j] - plus[j - 1]
        differences_minus[j] = minus[j] - minus[j - 1]
        cell = j - 1
        if cell < 1:
            continue
        terms_plus[cell] = cell_terms(differences_plus[cell], differences_plus[j])
        terms_minus[cell] = cell_terms(differences_minus[cell], differences_minus[j])
        if 2 <= cell <= count + 3:
            centre[cell] = 6.0 * (plus[cell] + minus[cell]) - (
                terms_plus[cell][0] + terms_minus[cell][0]
            )
        if cell < 2:
            continue
        third_plus[cell] = terms_plus[cell][0] - terms_plus[cell - 1][0]
        third_minus[cell] = terms_minus[cell][0] - terms_minus[cell - 1][0]
        if cell < 4:
            continue
        at = cell - 2
        right = correction(
            terms_plus[at - 1][1], terms_plus[at][2], terms_plus[at + 1][3], third_plus[at], third_plus[at + 1]
        )
        left = correction(
            terms_minus[at + 2][3], terms_minus[at + 1][2], terms_minus[at][1],
            third_minus[at + 2], third_minus[at + 1],
        )
        interface[at] = (third_plus[at + 1] - third_minus[at + 1]) - 4.0 * (right - left)
        if at >= 3:
            store(at - 3, (centre[at - 1] - centre[at + 1]) + (interface[at - 1] - interface[at]))


def rolled(plus, minus):
    size = plus.shape[-1]

    def nxt(value, by=1):
        return pltpu.roll(value, size - by, value.ndim - 1)

    def prev(value):
        return pltpu.roll(value, 1, value.ndim - 1)

    above = nxt(plus) - plus
    second_plus, first_p, middle_p, last_p = cell_terms(prev(above), above)
    above = nxt(minus) - minus
    second_minus, first_m, middle_m, last_m = cell_terms(prev(above), above)
    centre = 6.0 * (plus + minus) - (second_plus + second_minus)
    third_plus = nxt(second_plus) - second_plus
    third_minus = nxt(second_minus) - second_minus
    right = correction(prev(first_p), middle_p, nxt(last_p), prev(third_plus), third_plus)
    left = correction(nxt(last_m, 2), nxt(middle_m), first_m, nxt(third_minus), third_minus)
    interface = (third_plus - third_minus) - 4.0 * (right - left)
    return (prev(centre) - nxt(centre)) + (prev(interface) - interface)


def lane_index(shape):
    return lax.broadcasted_iota(jnp.int32, shape, len(shape) - 1)


def turned(value, by):
    size = value.shape[-1]
    if isinstance(by, int):
        by = by % size
        return value if by == 0 else pltpu.roll(value, by, value.ndim - 1)
    return pltpu.roll(value, lax.rem(by + 4 * size, size), value.ndim - 1)


def merged(pieces, slot):
    out = pieces[0]
    for number, piece in enumerate(pieces[1:], 1):
        out = jnp.where(slot == number, piece, out)
    return out


def node_weights(me, count):
    def picked(row, column):
        values = [radau_weights[n ^ row][n ^ column] * (step_size / 12.0) for n in range(count)]
        out = jnp.float32(values[0])
        for n in range(1, count):
            out = jnp.where(me == n, jnp.float32(values[n]), out)
        return out

    return [[picked(row, column) for column in range(count)] for row in range(count)]


class Windows:
    def __init__(self, nx, nz, nodes):
        self.nodes = nodes
        self.width = nz // nodes
        self.pitch = self.width + 8
        self.slots = nz // self.pitch
        assert nx % self.slots == 0 and nz % nodes == 0
        self.rows = nx // self.slots

    def slot(self, shape):
        return lane_index(shape) // self.pitch

    def group(self, shape):
        return lane_index(shape) // self.width

    def cut(self, values, quarter):
        pieces = [
            turned(value, self.pitch * s + HALO - self.width * quarter) for s, value in enumerate(values)
        ]
        return merged(pieces, self.slot(values[0].shape))

    def joined(self, values, s):
        pieces = [
            turned(value, self.width * k - self.pitch * s - HALO) for k, value in enumerate(values)
        ]
        return merged(pieces, self.group(values[0].shape))


def write_edges(read, nx, ny, comps, lo_ref, hi_ref, side_ref):
    rows = side_ref.shape[1] // (2 * HALO)
    for c in range(comps):
        for i in range(HALO):
            lo_ref[0, pl.ds((c * HALO + i) * ny, ny), :] = read(c, i)
            hi_ref[0, pl.ds((c * HALO + i) * ny, ny), :] = read(c, nx - HALO + i)

    def side(i, carry):
        for c in range(comps):
            value = read(c, i)
            side_ref[0, pl.ds(c * nx + i, HALO, stride=rows), :] = value[ny - HALO :]
            side_ref[0, pl.ds(HALO * rows + c * nx + i, HALO, stride=rows), :] = value[:HALO]
        return carry

    lax.fori_loop(0, nx, side, 0)


def speed_rows(read, nx, ny, nz, comps):
    def step(i, best):
        speeds = signal_speeds([read(c, i) for c in range(comps)])
        return tuple(jnp.maximum(b, s) for b, s in zip(best, speeds))

    best = lax.fori_loop(0, nx, step, tuple(jnp.zeros((ny, nz), jnp.float32) for _ in range(3)))
    return [jnp.max(b, axis=0, keepdims=True) for b in best]


def alpha_tile(rows, group):
    nz = rows[0].shape[-1]
    tile = jnp.concatenate(rows + [jnp.zeros((TILE - 3, nz), jnp.float32)], axis=0)
    lane = lane_index(tile.shape)
    by = 1
    while by < group:
        other = jnp.where((lane & by) != 0, turned(tile, by), turned(tile, -by))
        tile = jnp.maximum(tile, other)
        by *= 2
    return tile


def open_kernel(u_ref, lo_ref, hi_ref, side_ref, al_ref):
    comps, nx, ny, nz = u_ref.shape[1:]

    def read(c, i):
        return u_ref[0, c, i]

    write_edges(read, nx, ny, comps, lo_ref, hi_ref, side_ref)
    tile = alpha_tile(speed_rows(read, nx, ny, nz, comps), nz)
    al_ref[...] = tile
    lo_ref[0, pl.ds(comps * HALO * ny, TILE), :] = tile
    hi_ref[0, pl.ds(comps * HALO * ny, TILE), :] = tile


def blend_kernel(init_ref, *refs):
    comps, nx, ny, nz = init_ref.shape
    nodes = len(refs) - 6
    parts, (win_ref, nat_ref, lo_ref, hi_ref, side_ref, al_ref) = refs[:nodes], refs[nodes:]
    windows = Windows(nx, nz, nodes)
    me = lax.axis_index("node")
    weights = node_weights(me, nodes)

    def step(c, carry):
        for r in range(windows.rows):
            at = pl.ds(pl.multiple_of((c * windows.rows + r) * ny, ny), ny)
            start = windows.cut([init_ref[c, s * windows.rows + r] for s in range(windows.slots)], me)
            rates = [part[at, :] for part in parts]
            states = []
            for k in range(nodes):
                value = start
                for j in range(nodes):
                    value = value + weights[k][j] * rates[j]
                win_ref[k, at, :] = value
                states.append(value)
            for s in range(windows.slots):
                nat_ref[c, s * windows.rows + r] = windows.joined(states, s)
        return carry

    lax.fori_loop(0, comps, step, 0)

    def read(c, i):
        return nat_ref[c, i]

    write_edges(read, nx, ny, comps, lo_ref, hi_ref, side_ref)
    tile = alpha_tile(speed_rows(read, nx, ny, nz, comps), windows.width)
    al_ref[...] = tile
    lo_ref[0, pl.ds(comps * HALO * ny, TILE), :] = tile
    hi_ref[0, pl.ds(comps * HALO * ny, TILE), :] = tile


def along_grid(u, alphas, lo_ref, hi_ref, side_ref, out_ref, scratch, depth):
    xp, xm, yp, ym, fy = scratch
    comps, nx, ny, nz = out_ref.shape
    rows = yp.shape[0] // (ny + 2 * HALO)
    every = range(comps)

    def own(i, carry):
        split = splits([u(c, i) for c in every], alphas, (0, 1, 2) if depth else (0, 1))
        along_x, along_y = split[:2]
        for c in every:
            xp[i + HALO, c * ny : (c + 1) * ny, :] = along_x[0][c]
            xm[i + HALO, c * ny : (c + 1) * ny, :] = along_x[1][c]
            for t in range(0, ny, TILE):
                at = pl.ds((HALO + t) * rows + c * nx + i, TILE, stride=rows)
                yp[at, :] = along_y[0][c][t : t + TILE]
                ym[at, :] = along_y[1][c][t : t + TILE]
            if depth:
                out_ref[c, i] = rolled(split[2][0][c], split[2][1][c])
        return carry

    lax.fori_loop(0, nx, own, 0)

    for ref, start in ((lo_ref, 0), (hi_ref, nx + HALO)):

        def ghost_x(i, carry, ref=ref, start=start):
            fields = [ref[0, pl.ds(pl.multiple_of((c * HALO + i) * ny, ny), ny), :] for c in every]
            ((p, m),) = splits(fields, alphas, (0,))
            for c in every:
                xp[start + i, c * ny : (c + 1) * ny, :] = p[c]
                xm[start + i, c * ny : (c + 1) * ny, :] = m[c]
            return carry

        lax.fori_loop(0, HALO, ghost_x, 0)

    def ghost_y(i, carry):
        row = jnp.where(i < HALO, i, i + ny) * rows
        ((p, m),) = splits([side_ref[0, pl.ds(i * rows + c * nx, nx), :] for c in every], alphas, (1,))
        for c in every:
            yp[pl.ds(row + c * nx, nx), :] = p[c]
            ym[pl.ds(row + c * nx, nx), :] = m[c]
        return carry

    lax.fori_loop(0, 2 * HALO, ghost_y, 0)

    def along_second(b, carry):
        first = pl.multiple_of(b * TILE, TILE)

        def load(j):
            at = pl.ds(j * rows + first, TILE)
            return yp[at, :], ym[at, :]

        def store(i, value):
            fy[pl.ds(i * rows + first, TILE), :] = value

        stream(load, store, ny)
        return carry

    lax.fori_loop(0, rows // TILE, along_second, 0)

    for c in every:

        def along_first(b, carry, c=c):
            first = pl.multiple_of(b * TILE, TILE)

            def load(j):
                at = pl.ds(c * ny + first, TILE)
                return xp[j, at, :], xm[j, at, :]

            def store(i, value):
                cross = fy[pl.ds(first * rows + c * nx + i, TILE, stride=rows), :]
                here = pl.ds(first, TILE)
                out_ref[c, i, here, :] = out_ref[c, i, here, :] + value + cross

            stream(load, store, nx)
            return carry

        lax.fori_loop(0, ny // TILE, along_first, 0)


def first_kernel(u_ref, lo_ref, hi_ref, side_ref, al_ref, other_ref, *refs):
    nodes = len(refs) - 6
    parts, rate, scratch = refs[:nodes], refs[nodes], refs[nodes + 1 :]
    comps, nx, ny, nz = u_ref.shape[1:]
    tile = jnp.maximum(al_ref[...], other_ref[...])
    alphas = [tile[k : k + 1, :] for k in range(3)]
    along_grid(lambda c, i: u_ref[0, c, i], alphas, lo_ref, hi_ref, side_ref, rate, scratch, True)
    windows = Windows(nx, nz, nodes)
    me = lax.axis_index("node")

    def cut(c, carry):
        for r in range(windows.rows):
            values = [rate[c, s * windows.rows + r] for s in range(windows.slots)]
            at = pl.ds(pl.multiple_of((c * windows.rows + r) * ny, ny), ny)
            for k in range(nodes):
                parts[k][at, :] = windows.cut(values, me ^ k)
        return carry

    lax.fori_loop(0, comps, cut, 0)


def second_kernel(init_ref, nat_ref, win_ref, lo_ref, hi_ref, side_ref, *refs):
    nodes = win_ref.shape[0]
    tiles, outs, (rate, deep), scratch = refs[:nodes], refs[nodes : 2 * nodes], refs[2 * nodes : 2 * nodes + 2], refs[2 * nodes + 2 :]
    comps, nx, ny, nz = nat_ref.shape
    every = range(comps)
    windows = Windows(nx, nz, nodes)
    me = lax.axis_index("node")
    group = windows.group((TILE, nz))
    tile = tiles[0][...]
    for k in range(1, nodes):
        value = tiles[k][...]
        tile = jnp.maximum(tile, merged([turned(value, windows.width * (g - (g ^ k))) for g in range(nodes)], group))
    alphas = [tile[k : k + 1, :] for k in range(3)]

    for k in range(nodes):
        alpha = jnp.max(jnp.where(group[:1] == k, alphas[2], 0.0))

        def depth(r, carry, k=k, alpha=alpha):
            places = [pl.ds(pl.multiple_of((c * windows.rows + r) * ny, ny), ny) for c in every]
            ((p, m),) = splits([win_ref[k, at, :] for at in places], [None, None, alpha], (2,))
            for c in every:
                deep[k, places[c], :] = rolled(p[c], m[c])
            return carry

        lax.fori_loop(0, windows.rows, depth, 0)

    def join(c, carry):
        for r in range(windows.rows):
            at = pl.ds(pl.multiple_of((c * windows.rows + r) * ny, ny), ny)
            values = [deep[k, at, :] for k in range(nodes)]
            for s in range(windows.slots):
                rate[c, s * windows.rows + r] = windows.joined(values, s)
        return carry

    lax.fori_loop(0, comps, join, 0)
    along_grid(lambda c, i: nat_ref[c, i], alphas, lo_ref, hi_ref, side_ref, rate, scratch, False)

    weights = node_weights(me, nodes)
    lanes = windows.group((ny, nz))

    def finish(c, carry):
        for q in range(nx // nodes):
            at = pl.ds(pl.multiple_of((c * (nx // nodes) + q) * ny, ny), ny)
            start = merged(
                [turned(init_ref[c, q * nodes + i], windows.width * (i - me)) for i in range(nodes)], lanes
            )
            rows = [rate[c, q * nodes + i] for i in range(nodes)]
            rates = [
                merged([turned(rows[i], windows.width * (i - k)) for i in range(nodes)], lanes) for k in range(nodes)
            ]
            for k in range(nodes):
                value = start
                for j in range(nodes):
                    value = value + weights[k][j] * rates[j]
                outs[k][at, :] = value
        return carry

    lax.fori_loop(0, comps, finish, 0)


def close_kernel(*refs):
    parts, out_ref = refs[:-1], refs[-1]
    nodes = len(parts)
    comps, nx, ny, nz = out_ref.shape[1:]
    width = nz // nodes
    me = lax.axis_index("node")
    lanes = lane_index((ny, nz)) // width

    def step(c, carry):
        for q in range(nx // nodes):
            at = pl.ds(pl.multiple_of((c * (nx // nodes) + q) * ny, ny), ny)
            values = [part[at, :] for part in parts]
            for i in range(nodes):
                out = turned(values[0], width * (me - i))
                for k in range(1, nodes):
                    out = jnp.where(lanes == (me ^ k), turned(values[k], width * ((me ^ k) - i)), out)
                out_ref[0, c, q * nodes + i] = out
        return carry

    lax.fori_loop(0, comps, step, 0)


def call(kernel, outs, operands, scratch=(), flops=1_000_000):
    vmem = pl.BlockSpec(memory_space=pltpu.VMEM)
    moved = sum(4 * x.size for x in operands)
    return pl.pallas_call(
        kernel,
        out_shape=[jax.ShapeDtypeStruct(shape, jnp.float32) for shape in outs],
        in_specs=[vmem] * len(operands),
        out_specs=[vmem] * len(outs),
        scratch_shapes=[pltpu.VMEM(shape, jnp.float32) for shape in scratch],
        compiler_params=pltpu.CompilerParams(vmem_limit_bytes=32 * 1024 * 1024),
        cost_estimate=pl.CostEstimate(flops=flops, bytes_accessed=2 * moved, transcendentals=0),
        name=kernel.__name__,
    )(*operands)


def shifted(value, axis, by):
    count = lax.axis_size(axis)
    return lax.ppermute(value, axis, [(i, (i + by) % count) for i in range(count)])


def swapped(value, by):
    return lax.ppermute(value, "node", [(i, i ^ by) for i in range(lax.axis_size("node"))])


def neighbours(lo, hi, side, tile):
    across, beside = lax.axis_size("gx"), lax.axis_size("gy")
    lower, upper = shifted(hi, "gx", 1), shifted(lo, "gx", -1)
    if across <= 4:
        tiles = [tile, lower[0, -TILE:], upper[0, -TILE:]]
        if across == 4:
            tiles.append(shifted(tile, "gx", 2))
        tile = functools.reduce(jnp.maximum, tiles)
    else:
        tile = lax.pmax(tile, "gx")
    if beside == 2:
        return lower, upper, shifted(side, "gy", 1), tile, shifted(tile, "gy", 1)
    half = side.shape[1] // 2
    side = jnp.concatenate([shifted(side[:, :half], "gy", 1), shifted(side[:, half:], "gy", -1)], axis=1)
    tile = lax.pmax(tile, "gy")
    return lower, upper, side, tile, tile


def local(initial, guesses):
    comps, nx, ny, nz = initial.shape
    nodes = lax.axis_size("node")
    rows = -(-comps * nx // TILE) * TILE
    windows = Windows(nx, nz, nodes)
    edge = (1, comps * HALO * ny + TILE, nz)
    edges = [edge, edge, (1, 2 * HALO * rows, nz), (TILE, nz)]
    part = (comps * windows.rows * ny, nz)
    streams = [
        (nx + 2 * HALO, comps * ny, nz),
        (nx + 2 * HALO, comps * ny, nz),
        ((ny + 2 * HALO) * rows, nz),
        ((ny + 2 * HALO) * rows, nz),
        (ny * rows, nz),
    ]
    lo, hi, side, tile = call(open_kernel, edges, [guesses])
    lower, upper, side, tile, other = neighbours(lo, hi, side, tile)
    parts = call(
        first_kernel,
        [part] * nodes,
        [guesses, lower, upper, side, tile, other],
        [initial.shape] + streams,
        30_000_000,
    )
    parts = [parts[0]] + [swapped(parts[k], k) for k in range(1, nodes)]
    win, nat, lo, hi, side, tile = call(
        blend_kernel, [(nodes,) + part, initial.shape] + edges, [initial] + parts
    )
    lower, upper, side, tile, other = neighbours(lo, hi, side, tile)
    tile = jnp.maximum(tile, other)
    tiles = [tile] + [swapped(tile, k) for k in range(1, nodes)]
    outs = call(
        second_kernel,
        [(comps * nx // nodes * ny, nz)] * nodes,
        [initial, nat, win, lower, upper, side] + tiles,
        [initial.shape, (nodes,) + part] + streams,
        30_000_000,
    )
    outs = [outs[0]] + [swapped(outs[k], k) for k in range(1, nodes)]
    (states,) = call(close_kernel, [(1,) + initial.shape], outs)
    return states


def solution(mesh):
    return jax.shard_map(
        local,
        mesh=mesh,
        in_specs=(P(None, "gx", "gy", None), P("node", None, "gx", "gy", None)),
        out_specs=P("node", None, "gx", "gy", None),
        check_vma=False,
    )
```

```python
import functools

import jax
import jax.numpy as jnp
from jax import lax
from jax.experimental import pallas as pl
from jax.experimental.pallas import tpu as pltpu
from jax.sharding import PartitionSpec as P

SWEEPS = 2
HALO = 3
COMPONENTS = 5
TILE = 8

heat_ratio = 1.4
step_size = 0.025
density_floor = 0.5
pressure_floor = 0.25
epsilon = 1e-06
radau_weights = [
    [0.112999479323156, -0.040309220723522, 0.025802377420336, -0.009904676507266],
    [0.2343839957474, 0.206892573935359, -0.047857128048541, 0.016047422806516],
    [0.21668178462325, 0.406123263867373, 0.189036518170056, -0.024182104899833],
    [0.220462211176768, 0.388193468843172, 0.32884431998006, 0.0625],
]


def reciprocal(value):
    return pl.reciprocal(value, approx=True)


def primitives(fields):
    inverse = 1.0 / jnp.maximum(fields[0], density_floor)
    velocity = [fields[k] * inverse for k in (1, 2, 3)]
    energy = fields[1] * velocity[0] + fields[2] * velocity[1] + fields[3] * velocity[2]
    pressure = jnp.maximum(0.4 * (fields[4] - 0.5 * energy), pressure_floor)
    return inverse, velocity, pressure


def signal_speeds(fields):
    inverse, velocity, pressure = primitives(fields)
    sound = jnp.sqrt(heat_ratio * pressure * inverse)
    return [jnp.abs(v) + sound for v in velocity]


def half_fluxes(half, speed, half_pressure, direction):
    flux = [half[direction + 1]] + [half[k] * speed for k in (1, 2, 3)]
    flux.append((half[4] + half_pressure) * speed)
    flux[direction + 1] = flux[direction + 1] + half_pressure
    return flux


def splits(fields, alphas, directions=(0, 1, 2)):
    _, velocity, pressure = primitives(fields)
    half = [0.5 * field for field in fields]
    half_pressure = 0.5 * pressure
    out = []
    for direction in directions:
        flux = half_fluxes(half, velocity[direction], half_pressure, direction)
        signal = [alphas[direction] * value for value in half]
        out.append(
            ([f + s for f, s in zip(flux, signal)], [f - s for f, s in zip(flux, signal)])
        )
    return out


def cell_terms(below, above):
    second = above - below
    both = below + above
    square = second * second
    middle = 0.25 * (both * both) + ((13.0 / 12.0) * square + epsilon)
    outer = middle + square
    cross = both * second
    return second, outer + cross, middle, outer - cross


def correction(first, middle, last, third_first, third_last):
    ratio_first = middle * reciprocal(first)
    ratio_last = middle * reciprocal(last)
    weight_first = ratio_first * ratio_first
    weight_last = 1.5 * (ratio_last * ratio_last)
    total = (6.0 + weight_first) + (weight_last + weight_last)
    return (weight_first * third_first + weight_last * third_last) * reciprocal(total)


def stream(load, store, count):
    plus, minus, centre = {}, {}, {}
    terms_plus, terms_minus, third_plus, third_minus, interface = {}, {}, {}, {}, {}
    differences_plus, differences_minus = {}, {}
    plus[0], minus[0] = load(0)
    for j in range(1, count + 2 * HALO):
        plus[j], minus[j] = load(j)
        differences_plus[j] = plus[j] - plus[j - 1]
        differences_minus[j] = minus[j] - minus[j - 1]
        cell = j - 1
        if cell < 1:
            continue
        terms_plus[cell] = cell_terms(differences_plus[cell], differences_plus[j])
        terms_minus[cell] = cell_terms(differences_minus[cell], differences_minus[j])
        if 2 <= cell <= count + 3:
            centre[cell] = 6.0 * (plus[cell] + minus[cell]) - (
                terms_plus[cell][0] + terms_minus[cell][0]
            )
        if cell < 2:
            continue
        third_plus[cell] = terms_plus[cell][0] - terms_plus[cell - 1][0]
        third_minus[cell] = terms_minus[cell][0] - terms_minus[cell - 1][0]
        if cell < 4:
            continue
        at = cell - 2
        right = correction(
            terms_plus[at - 1][1], terms_plus[at][2], terms_plus[at + 1][3], third_plus[at], third_plus[at + 1]
        )
        left = correction(
            terms_minus[at + 2][3], terms_minus[at + 1][2], terms_minus[at][1],
            third_minus[at + 2], third_minus[at + 1],
        )
        interface[at] = (third_plus[at + 1] - third_minus[at + 1]) - 4.0 * (right - left)
        if at >= 3:
            store(at - 3, (centre[at - 1] - centre[at + 1]) + (interface[at - 1] - interface[at]))


def reconstructed(first, second, third, fourth, fifth):
    one, two, three, four = second - first, third - second, fourth - third, fifth - fourth
    bends = [two - one, three - two, four - three]
    slopes = [two + 0.5 * bends[0], two + 0.5 * bends[1], three - 0.5 * bends[2]]
    smooth = [((13.0 / 12.0) * (b * b) + epsilon) + v * v for b, v in zip(bends, slopes)]
    return bends[1], bends[2], correction(*smooth, bends[1] - bends[0], bends[2] - bends[1])


def rolled(plus, minus):
    p = {k: turned(plus, -k) for k in (-2, -1, 0, 1, 2)}
    m = {k: turned(minus, -k) for k in (-1, 0, 1, 2, 3)}
    plus_here, plus_next, right = reconstructed(p[-2], p[-1], p[0], p[1], p[2])
    minus_next, minus_here, left = reconstructed(m[3], m[2], m[1], m[0], m[-1])
    centre = 6.0 * ((p[0] + m[0]) + (p[1] + m[1])) - ((plus_here + minus_here) + (plus_next + minus_next))
    interface = centre + ((plus_next - plus_here) - (minus_next - minus_here)) - 4.0 * (right + left)
    return turned(interface, 1) - interface


def lane_index(shape):
    return lax.broadcasted_iota(jnp.int32, shape, len(shape) - 1)


def turned(value, by):
    size = value.shape[-1]
    if isinstance(by, int):
        by = by % size
        return value if by == 0 else pltpu.roll(value, by, value.ndim - 1)
    return pltpu.roll(value, lax.rem(by + 4 * size, size), value.ndim - 1)


def merged(pieces, slot):
    out = pieces[0]
    for number, piece in enumerate(pieces[1:], 1):
        out = jnp.where(slot == number, piece, out)
    return out


def node_weights(me, count):
    def picked(row, column):
        values = [radau_weights[n ^ row][n ^ column] * (step_size / 12.0) for n in range(count)]
        out = jnp.float32(values[0])
        for n in range(1, count):
            out = jnp.where(me == n, jnp.float32(values[n]), out)
        return out

    return [[picked(row, column) for column in range(count)] for row in range(count)]


class Windows:
    def __init__(self, nx, nz, nodes):
        self.nodes = nodes
        self.width = nz // nodes
        self.pitch = self.width + 8
        self.slots = nz // self.pitch
        assert nx % self.slots == 0 and nz % nodes == 0
        self.rows = nx // self.slots

    def slot(self, shape):
        return lane_index(shape) // self.pitch

    def group(self, shape):
        return lane_index(shape) // self.width

    def cut(self, values, quarter):
        pieces = [
            turned(value, self.pitch * s + HALO - self.width * quarter) for s, value in enumerate(values)
        ]
        return merged(pieces, self.slot(values[0].shape))

    def joined(self, values, s):
        pieces = [
            turned(value, self.width * k - self.pitch * s - HALO) for k, value in enumerate(values)
        ]
        return merged(pieces, self.group(values[0].shape))


def write_edges(read, nx, ny, comps, lo_ref, hi_ref, side_ref):
    rows = side_ref.shape[1] // (2 * HALO)
    for c in range(comps):
        for i in range(HALO):
            lo_ref[0, pl.ds((c * HALO + i) * ny, ny), :] = read(c, i)
            hi_ref[0, pl.ds((c * HALO + i) * ny, ny), :] = read(c, nx - HALO + i)

    def side(i, carry):
        for c in range(comps):
            value = read(c, i)
            side_ref[0, pl.ds(c * nx + i, HALO, stride=rows), :] = value[ny - HALO :]
            side_ref[0, pl.ds(HALO * rows + c * nx + i, HALO, stride=rows), :] = value[:HALO]
        return carry

    lax.fori_loop(0, nx, side, 0)


def speed_rows(read, nx, ny, nz, comps):
    def step(i, best):
        speeds = signal_speeds([read(c, i) for c in range(comps)])
        return tuple(jnp.maximum(b, s) for b, s in zip(best, speeds))

    best = lax.fori_loop(0, nx, step, tuple(jnp.zeros((ny, nz), jnp.float32) for _ in range(3)))
    return [jnp.max(b, axis=0, keepdims=True) for b in best]


def alpha_tile(rows, group):
    nz = rows[0].shape[-1]
    tile = jnp.concatenate(rows + [jnp.zeros((TILE - 3, nz), jnp.float32)], axis=0)
    lane = lane_index(tile.shape)
    by = 1
    while by < group:
        other = jnp.where((lane & by) != 0, turned(tile, by), turned(tile, -by))
        tile = jnp.maximum(tile, other)
        by *= 2
    return tile


def reordered(tile, me, windows):
    pieces = [turned(tile, windows.width * (g - (g ^ me))) for g in range(windows.nodes)]
    return merged(pieces, windows.group(tile.shape))


def open_kernel(u_ref, lo_ref, hi_ref, side_ref, al_ref):
    comps, nx, ny, nz = u_ref.shape[1:]

    def read(c, i):
        return u_ref[0, c, i]

    write_edges(read, nx, ny, comps, lo_ref, hi_ref, side_ref)
    al_ref[...] = alpha_tile(speed_rows(read, nx, ny, nz, comps), nz)


def blend_kernel(init_ref, *refs):
    comps, nx, ny, nz = init_ref.shape
    nodes = len(refs) - 6
    parts, (win_ref, nat_ref, lo_ref, hi_ref, side_ref, al_ref) = refs[:nodes], refs[nodes:]
    windows = Windows(nx, nz, nodes)
    me = lax.axis_index("node")
    weights = node_weights(me, nodes)

    def step(c, carry):
        for r in range(windows.rows):
            at = pl.ds(pl.multiple_of((c * windows.rows + r) * ny, ny), ny)
            start = windows.cut([init_ref[c, s * windows.rows + r] for s in range(windows.slots)], me)
            rates = [part[at, :] for part in parts]
            states = []
            for k in range(nodes):
                value = start
                for j in range(nodes):
                    value = value + weights[k][j] * rates[j]
                win_ref[k, at, :] = value
                states.append(value)
            for s in range(windows.slots):
                nat_ref[c, s * windows.rows + r] = windows.joined(states, s)
        return carry

    lax.fori_loop(0, comps, step, 0)

    def read(c, i):
        return nat_ref[c, i]

    write_edges(read, nx, ny, comps, lo_ref, hi_ref, side_ref)
    tile = reordered(alpha_tile(speed_rows(read, nx, ny, nz, comps), windows.width), me, windows)

    def spread(i, carry):
        al_ref[i] = tile
        return carry

    lax.fori_loop(0, al_ref.shape[0], spread, 0)


def along_grid(u, alphas, edges, rate, scratch, depth, extra, after):
    xp, xm, yp, ym, zp, zm, fy = scratch
    lo_ref, hi_ref, side_ref = edges
    comps, nx, ny, nz = rate.shape
    rows = yp.shape[0] // (ny + 2 * HALO)
    every = range(comps)

    def own(i, carry):
        along_x, along_y, *rest = splits([u(c, i) for c in every], alphas, (0, 1, 2) if depth else (0, 1))
        for c in every:
            xp[i + HALO, c * ny : (c + 1) * ny, :] = along_x[0][c]
            xm[i + HALO, c * ny : (c + 1) * ny, :] = along_x[1][c]
            for t in range(0, ny, TILE):
                at = pl.ds((HALO + t) * rows + c * nx + i, TILE, stride=rows)
                yp[at, :] = along_y[0][c][t : t + TILE]
                ym[at, :] = along_y[1][c][t : t + TILE]
        if depth:
            depth(i, rest[0])
        return carry

    lax.fori_loop(0, nx, own, 0)

    for ref, start in ((lo_ref, 0), (hi_ref, nx + HALO)):

        def ghost_x(i, carry, ref=ref, start=start):
            fields = [ref[0, pl.ds(pl.multiple_of((c * HALO + i) * ny, ny), ny), :] for c in every]
            ((p, m),) = splits(fields, alphas, (0,))
            for c in every:
                xp[start + i, c * ny : (c + 1) * ny, :] = p[c]
                xm[start + i, c * ny : (c + 1) * ny, :] = m[c]
            return carry

        lax.fori_loop(0, HALO, ghost_x, 0)

    def ghost_y(i, carry):
        row = jnp.where(i < HALO, i, i + ny) * rows
        ((p, m),) = splits([side_ref[0, pl.ds(i * rows + c * nx, nx), :] for c in every], alphas, (1,))
        for c in every:
            yp[pl.ds(row + c * nx, nx), :] = p[c]
            ym[pl.ds(row + c * nx, nx), :] = m[c]
        return carry

    lax.fori_loop(0, 2 * HALO, ghost_y, 0)

    blocks = rows // TILE
    share = zp.shape[0] // blocks
    assert share * blocks == zp.shape[0]
    piece = max(p for p in range(TILE, 41, TILE) if share % p == 0)

    def along_second(b, carry):
        first = pl.multiple_of(b * TILE, TILE)

        def load(j):
            at = pl.ds(j * rows + first, TILE)
            return yp[at, :], ym[at, :]

        def store(i, value):
            fy[pl.ds(i * rows + first, TILE), :] = value

        stream(load, store, ny)
        for n in range(0, share, piece):
            at = pl.ds(pl.multiple_of(b * share + n, TILE), piece)
            zp[at, :] = rolled(zp[at, :], zm[at, :])
        return carry

    lax.fori_loop(0, blocks, along_second, 0)

    tiles = ny // TILE

    def along_first(b, carry):
        c, t = b // tiles, lax.rem(b, tiles) * TILE
        first = pl.multiple_of(b * TILE, TILE)

        def load(j):
            return xp[j, pl.ds(first, TILE), :], xm[j, pl.ds(first, TILE), :]

        def store(i, value):
            cross = fy[pl.ds(t * rows + c * nx + i, TILE, stride=rows), :]
            rate[c, i, pl.ds(pl.multiple_of(t, TILE), TILE), :] = value + (cross + extra(c, i, t))

        stream(load, store, nx)
        done = jnp.maximum(b - 1, 0)
        after(done // tiles, pl.multiple_of(lax.rem(done, tiles) * TILE, TILE))
        return carry

    lax.fori_loop(0, comps * tiles, along_first, 0)
    after(comps - 1, ny - TILE)


def first_kernel(u_ref, lo_ref, hi_ref, side_ref, al_ref, other_ref, *refs):
    nodes = len(refs) - 8
    parts, rate, scratch = refs[:nodes], refs[nodes], refs[nodes + 1 :]
    zp, zm = scratch[4:6]
    comps, nx, ny, nz = u_ref.shape[1:]
    windows = Windows(nx, nz, nodes)
    me = lax.axis_index("node")
    tile = jnp.maximum(al_ref[...], other_ref[...])
    alphas = [tile[k : k + 1, :] for k in range(3)]

    def depth(i, split):
        for c in range(comps):
            at = pl.ds(pl.multiple_of((c * nx + i) * ny, ny), ny)
            zp[at, :] = split[0][c]
            zm[at, :] = split[1][c]

    def extra(c, i, t):
        return zp[pl.ds(pl.multiple_of((c * nx + i) * ny + t, TILE), TILE), :]

    def after(c, t):
        for r in range(windows.rows):
            values = [rate[c, s * windows.rows + r, pl.ds(t, TILE), :] for s in range(windows.slots)]
            at = pl.ds(pl.multiple_of((c * windows.rows + r) * ny + t, TILE), TILE)
            for k in range(nodes):
                parts[k][at, :] = windows.cut(values, me ^ k)

    along_grid(lambda c, i: u_ref[0, c, i], alphas, (lo_ref, hi_ref, side_ref), rate, scratch, depth, extra, after)


def second_kernel(init_ref, nat_ref, win_ref, lo_ref, hi_ref, side_ref, al_ref, *refs):
    nodes = win_ref.shape[0]
    outs, rate, scratch = refs[:nodes], refs[nodes], refs[nodes + 1 :]
    zp, zm = scratch[4:6]
    comps, nx, ny, nz = nat_ref.shape
    every = range(comps)
    windows = Windows(nx, nz, nodes)
    part = comps * windows.rows * ny
    me = lax.axis_index("node")
    tile = lax.fori_loop(
        1, al_ref.shape[0], lambda i, best: jnp.maximum(best, al_ref[i]), al_ref[0], unroll=True if al_ref.shape[0] <= 32 else 1
    )
    tile = reordered(tile, me, windows)
    alphas = [tile[k : k + 1, :] for k in range(3)]
    group = windows.group((1, nz))

    for k in range(nodes):
        alpha = jnp.max(jnp.where(group == k, alphas[2], 0.0))

        def split_depth(r, carry, k=k, alpha=alpha):
            places = [pl.multiple_of((c * windows.rows + r) * ny, ny) for c in every]
            fields = [win_ref[k, pl.ds(place, ny), :] for place in places]
            ((p, m),) = splits(fields, [None, None, alpha], (2,))
            for c in every:
                at = pl.ds(pl.multiple_of(k * part + places[c], TILE), ny)
                zp[at, :] = p[c]
                zm[at, :] = m[c]
            return carry

        lax.fori_loop(0, windows.rows, split_depth, 0)

    def extra(c, i, t):
        s, r = i // windows.rows, i % windows.rows
        place = (c * windows.rows + r) * ny + t
        values = [zp[pl.ds(pl.multiple_of(k * part + place, TILE), TILE), :] for k in range(nodes)]
        return windows.joined(values, s)

    weights = node_weights(me, nodes)
    lanes = windows.group((TILE, nz))

    def after(c, t):
        here = pl.ds(t, TILE)
        for q in range(nx // nodes):
            at = pl.ds(pl.multiple_of((c * (nx // nodes) + q) * ny + t, TILE), TILE)
            start = merged(
                [turned(init_ref[c, q * nodes + i, here, :], windows.width * (i - me)) for i in range(nodes)], lanes
            )
            rows = [rate[c, q * nodes + i, here, :] for i in range(nodes)]
            rates = [
                merged([turned(rows[i], windows.width * (i - k)) for i in range(nodes)], lanes) for k in range(nodes)
            ]
            for k in range(nodes):
                value = start
                for j in range(nodes):
                    value = value + weights[k][j] * rates[j]
                outs[k][at, :] = value

    along_grid(lambda c, i: nat_ref[c, i], alphas, (lo_ref, hi_ref, side_ref), rate, scratch, None, extra, after)


def close_kernel(*refs):
    parts, out_ref = refs[:-1], refs[-1]
    nodes = len(parts)
    nx, ny, nz = out_ref.shape[2:]
    width = nz // nodes
    me = lax.axis_index("node")
    lanes = lane_index((ny, nz)) // width
    for q in range(nx // nodes):
        values = [part[q * ny : (q + 1) * ny, :] for part in parts]
        for i in range(nodes):
            pieces = [turned(values[k], width * ((me ^ k) - i)) for k in range(nodes)]
            out = pieces[0]
            for k in range(1, nodes):
                out = jnp.where(lanes == (me ^ k), pieces[k], out)
            out_ref[0, 0, q * nodes + i] = out


def call(kernel, outs, operands, scratch=(), flops=1_000_000):
    vmem = pl.BlockSpec(memory_space=pltpu.VMEM)
    moved = sum(4 * x.size for x in operands)
    return pl.pallas_call(
        kernel,
        out_shape=[jax.ShapeDtypeStruct(shape, jnp.float32) for shape in outs],
        in_specs=[vmem] * len(operands),
        out_specs=[vmem] * len(outs),
        scratch_shapes=[pltpu.VMEM(shape, jnp.float32) for shape in scratch],
        compiler_params=pltpu.CompilerParams(vmem_limit_bytes=32 * 1024 * 1024),
        cost_estimate=pl.CostEstimate(flops=flops, bytes_accessed=2 * moved, transcendentals=0),
        name=kernel.__name__,
    )(*operands)


def shifted(value, axis, by):
    count = lax.axis_size(axis)
    return lax.ppermute(value, axis, [(i, (i + by) % count) for i in range(count)])


def swapped(value, by):
    return lax.ppermute(value, "node", [(i, i ^ by) for i in range(lax.axis_size("node"))])


def neighbours(lo, hi, side):
    lower, upper = shifted(hi, "gx", 1), shifted(lo, "gx", -1)
    if lax.axis_size("gy") == 2:
        return lower, upper, shifted(side, "gy", 1)
    half = side.shape[1] // 2
    side = jnp.concatenate([shifted(side[:, :half], "gy", 1), shifted(side[:, half:], "gy", -1)], axis=1)
    return lower, upper, side


def largest(tile):
    if lax.axis_size("gx") > 4 or lax.axis_size("gy") > 2:
        tile = lax.pmax(tile, ("gx", "gy"))
        return tile, tile
    others = [shifted(tile, "gx", by) for by in range(1, lax.axis_size("gx"))]
    tile = functools.reduce(jnp.maximum, others, tile)
    return tile, shifted(tile, "gy", 1)


def local(initial, guesses):
    comps, nx, ny, nz = initial.shape
    nodes = lax.axis_size("node")
    devices = nodes * lax.axis_size("gx") * lax.axis_size("gy")
    rows = -(-comps * nx // TILE) * TILE
    windows = Windows(nx, nz, nodes)
    edge = (1, comps * HALO * ny, nz)
    edges = [edge, edge, (1, 2 * HALO * rows, nz)]
    part = (comps * windows.rows * ny, nz)
    streams = [(nx + 2 * HALO, comps * ny, nz)] * 2 + [((ny + 2 * HALO) * rows, nz)] * 2
    across = [(ny * rows, nz)]
    lo, hi, side, tile = call(open_kernel, edges + [(TILE, nz)], [guesses])
    lower, upper, side = neighbours(lo, hi, side)
    tile, other = largest(tile)
    parts = call(
        first_kernel,
        [part] * nodes,
        [guesses, lower, upper, side, tile, other],
        [initial.shape] + streams + [(comps * nx * ny, nz)] * 2 + across,
        30_000_000,
    )
    parts = [parts[0]] + [swapped(parts[k], k) for k in range(1, nodes)]
    win, nat, lo, hi, side, tile = call(
        blend_kernel,
        [(nodes,) + part, initial.shape] + edges + [(devices, TILE, nz)],
        [initial] + parts,
    )
    lower, upper, side = neighbours(lo, hi, side)
    tiles = lax.all_to_all(tile, ("node", "gx", "gy"), 0, 0)
    outs = call(
        second_kernel,
        [(comps * nx // nodes * ny, nz)] * nodes,
        [initial, nat, win, lower, upper, side, tiles],
        [initial.shape] + streams + [(nodes * part[0], nz)] * 2 + across,
        30_000_000,
    )
    outs = [outs[0]] + [swapped(outs[k], k) for k in range(1, nodes)]
    slab = nx // nodes * ny
    return pl.pallas_call(
        close_kernel,
        grid=(comps,),
        out_shape=jax.ShapeDtypeStruct((1,) + initial.shape, jnp.float32),
        in_specs=[pl.BlockSpec((slab, nz), lambda c: (c, 0))] * nodes,
        out_specs=pl.BlockSpec((1, 1, nx, ny, nz), lambda c: (0, c, 0, 0, 0)),
        name="close_kernel",
    )(*outs)


def solution(mesh):
    return jax.shard_map(
        local,
        mesh=mesh,
        in_specs=(P(None, "gx", "gy", None), P("node", None, "gx", "gy", None)),
        out_specs=P("node", None, "gx", "gy", None),
        check_vma=False,
    )
```

```python
import functools

import jax
import jax.numpy as jnp
from jax import lax
from jax.experimental import pallas as pl
from jax.experimental.pallas import tpu as pltpu
from jax.sharding import PartitionSpec as P

SWEEPS = 2
HALO = 3
COMPONENTS = 5
TILE = 8

heat_ratio = 1.4
step_size = 0.025
density_floor = 0.5
pressure_floor = 0.25
epsilon = 1e-06
radau_weights = [
    [0.112999479323156, -0.040309220723522, 0.025802377420336, -0.009904676507266],
    [0.2343839957474, 0.206892573935359, -0.047857128048541, 0.016047422806516],
    [0.21668178462325, 0.406123263867373, 0.189036518170056, -0.024182104899833],
    [0.220462211176768, 0.388193468843172, 0.32884431998006, 0.0625],
]


def reciprocal(value):
    return pl.reciprocal(value, approx=True)


def primitives(fields):
    inverse = 1.0 / jnp.maximum(fields[0], density_floor)
    velocity = [fields[k] * inverse for k in (1, 2, 3)]
    energy = fields[1] * velocity[0] + fields[2] * velocity[1] + fields[3] * velocity[2]
    pressure = jnp.maximum(0.4 * (fields[4] - 0.5 * energy), pressure_floor)
    return inverse, velocity, pressure


def signal_speeds(fields):
    inverse, velocity, pressure = primitives(fields)
    sound = jnp.sqrt(heat_ratio * pressure * inverse)
    return [jnp.abs(v) + sound for v in velocity]


def half_fluxes(half, speed, half_pressure, direction):
    flux = [half[direction + 1]] + [half[k] * speed for k in (1, 2, 3)]
    flux.append((half[4] + half_pressure) * speed)
    flux[direction + 1] = flux[direction + 1] + half_pressure
    return flux


def splits(fields, alphas, directions=(0, 1, 2)):
    _, velocity, pressure = primitives(fields)
    half = [0.5 * field for field in fields]
    half_pressure = 0.5 * pressure
    out = []
    for direction in directions:
        flux = half_fluxes(half, velocity[direction], half_pressure, direction)
        signal = [alphas[direction] * value for value in half]
        out.append(
            ([f + s for f, s in zip(flux, signal)], [f - s for f, s in zip(flux, signal)])
        )
    return out


def cell_terms(below, above):
    second = above - below
    both = below + above
    square = second * second
    middle = 0.25 * (both * both) + ((13.0 / 12.0) * square + epsilon)
    outer = middle + square
    cross = both * second
    return second, outer + cross, middle, outer - cross


def correction(first, middle, last, third_first, third_last):
    ratio_first = middle * reciprocal(first)
    ratio_last = middle * reciprocal(last)
    weight_first = ratio_first * ratio_first
    weight_last = 1.5 * (ratio_last * ratio_last)
    total = (6.0 + weight_first) + (weight_last + weight_last)
    return (weight_first * third_first + weight_last * third_last) * reciprocal(total)


def stream(load, store, count):
    plus, minus, centre = {}, {}, {}
    terms_plus, terms_minus, third_plus, third_minus, interface = {}, {}, {}, {}, {}
    differences_plus, differences_minus = {}, {}
    plus[0], minus[0] = load(0)
    for j in range(1, count + 2 * HALO):
        plus[j], minus[j] = load(j)
        differences_plus[j] = plus[j] - plus[j - 1]
        differences_minus[j] = minus[j] - minus[j - 1]
        cell = j - 1
        if cell < 1:
            continue
        terms_plus[cell] = cell_terms(differences_plus[cell], differences_plus[j])
        terms_minus[cell] = cell_terms(differences_minus[cell], differences_minus[j])
        if 2 <= cell <= count + 3:
            centre[cell] = 6.0 * (plus[cell] + minus[cell]) - (
                terms_plus[cell][0] + terms_minus[cell][0]
            )
        if cell < 2:
            continue
        third_plus[cell] = terms_plus[cell][0] - terms_plus[cell - 1][0]
        third_minus[cell] = terms_minus[cell][0] - terms_minus[cell - 1][0]
        if cell < 4:
            continue
        at = cell - 2
        right = correction(
            terms_plus[at - 1][1], terms_plus[at][2], terms_plus[at + 1][3], third_plus[at], third_plus[at + 1]
        )
        left = correction(
            terms_minus[at + 2][3], terms_minus[at + 1][2], terms_minus[at][1],
            third_minus[at + 2], third_minus[at + 1],
        )
        interface[at] = (third_plus[at + 1] - third_minus[at + 1]) - 4.0 * (right - left)
        if at >= 3:
            store(at - 3, (centre[at - 1] - centre[at + 1]) + (interface[at - 1] - interface[at]))


def reconstructed(first, second, third, fourth, fifth):
    one, two, three, four = second - first, third - second, fourth - third, fifth - fourth
    bends = [two - one, three - two, four - three]
    slopes = [two + 0.5 * bends[0], two + 0.5 * bends[1], three - 0.5 * bends[2]]
    smooth = [((13.0 / 12.0) * (b * b) + epsilon) + v * v for b, v in zip(bends, slopes)]
    return bends[1], bends[2], correction(*smooth, bends[1] - bends[0], bends[2] - bends[1])


def rolled(plus, minus):
    p = {k: turned(plus, -k) for k in (-2, -1, 0, 1, 2)}
    m = {k: turned(minus, -k) for k in (-1, 0, 1, 2, 3)}
    plus_here, plus_next, right = reconstructed(p[-2], p[-1], p[0], p[1], p[2])
    minus_next, minus_here, left = reconstructed(m[3], m[2], m[1], m[0], m[-1])
    centre = 6.0 * ((p[0] + m[0]) + (p[1] + m[1])) - ((plus_here + minus_here) + (plus_next + minus_next))
    interface = centre + ((plus_next - plus_here) - (minus_next - minus_here)) - 4.0 * (right + left)
    return turned(interface, 1) - interface


def lane_index(shape):
    return lax.broadcasted_iota(jnp.int32, shape, len(shape) - 1)


def turned(value, by):
    size = value.shape[-1]
    if isinstance(by, int):
        by = by % size
        return value if by == 0 else pltpu.roll(value, by, value.ndim - 1)
    return pltpu.roll(value, lax.rem(by + 4 * size, size), value.ndim - 1)


def merged(pieces, slot):
    out = pieces[0]
    for number, piece in enumerate(pieces[1:], 1):
        out = jnp.where(slot == number, piece, out)
    return out


def rows_at(start, size):
    return pl.ds(start if isinstance(start, int) else pl.multiple_of(start, TILE), size)


def by_node(me, values):
    out = jnp.float32(values[0])
    for n, value in enumerate(values[1:], 1):
        out = jnp.where(me == n, jnp.float32(value), out)
    return out


def scaled_weight(row, column):
    return radau_weights[row][column] * (step_size / 12.0)


class Windows:
    def __init__(self, nx, nz, nodes):
        self.nodes = nodes
        self.size = nz
        self.width = nz // nodes
        self.pitch = self.width + 8
        self.slots = nz // self.pitch
        assert nx % self.slots == 0 and nx % nodes == 0 and nz % nodes == 0
        self.rows = nx // self.slots

    def cut(self, values, quarter):
        pieces = [
            turned(value, self.pitch * s + HALO - self.width * quarter) for s, value in enumerate(values)
        ]
        return merged(pieces, lane_index(values[0].shape) // self.pitch)

    def joined(self, values, s):
        start = self.pitch * s + HALO
        lane = lane_index(values[0].shape)
        region = jnp.where(lane < start, lane + (self.size - start), lane - start) // self.width
        return turned(merged(values, region), -start)


def write_edges(read, nx, ny, comps, lo_ref, hi_ref, side_ref):
    rows = side_ref.shape[1] // (2 * HALO)
    for c in range(comps):
        for i in range(HALO):
            lo_ref[0, pl.ds((c * HALO + i) * ny, ny), :] = read(c, i)
            hi_ref[0, pl.ds((c * HALO + i) * ny, ny), :] = read(c, nx - HALO + i)

    def side(i, carry):
        for c in range(comps):
            value = read(c, i)
            side_ref[0, pl.ds(c * nx + i, HALO, stride=rows), :] = value[ny - HALO :]
            side_ref[0, pl.ds(HALO * rows + c * nx + i, HALO, stride=rows), :] = value[:HALO]
        return carry

    lax.fori_loop(0, nx, side, 0)


def faster(best, read, first, count, comps):
    def step(i, best):
        speeds = signal_speeds([read(c, i) for c in range(comps)])
        return tuple(jnp.maximum(b, s) for b, s in zip(best, speeds))

    return lax.fori_loop(first, first + count, step, best)


def alpha_tile(best, group):
    nz = best[0].shape[-1]
    rows = [jnp.max(b, axis=0, keepdims=True) for b in best]
    tile = jnp.concatenate(rows + [jnp.zeros((TILE - 3, nz), jnp.float32)], axis=0)
    lane = lane_index(tile.shape)
    by = 1
    while by < group:
        other = jnp.where((lane & by) != 0, turned(tile, by), turned(tile, -by))
        tile = jnp.maximum(tile, other)
        by *= 2
    return tile


def open_kernel(u_hbm, lo_ref, hi_ref, side_ref, al_ref, u_ref, sems):
    comps, nx, ny, nz = u_ref.shape
    chunks = sems.shape[0]
    size = nx // chunks
    copies = []
    for n in range(chunks):
        at = pl.ds(n * size, size)
        copies.append(pltpu.make_async_copy(u_hbm.at[0, :, at], u_ref.at[:, at], sems.at[n]))
        copies[-1].start()

    def read(c, i):
        return u_ref[c, i]

    best = tuple(jnp.zeros((ny, nz), jnp.float32) for _ in range(3))
    for n in range(chunks):
        copies[n].wait()
        best = faster(best, read, n * size, size, comps)
    al_ref[...] = alpha_tile(best, nz)
    write_edges(read, nx, ny, comps, lo_ref, hi_ref, side_ref)


def start_kernel(init_ref, win_ref, pack_ref, *, nodes):
    comps, nx, ny, nz = init_ref.shape
    windows = Windows(nx, nz, nodes)
    me = lax.axis_index("node")
    lanes = lane_index((ny, nz)) // windows.width

    def step(c, carry):
        for r in range(windows.rows):
            values = [init_ref[c, s * windows.rows + r] for s in range(windows.slots)]
            win_ref[rows_at((c * windows.rows + r) * ny, ny), :] = windows.cut(values, me)
        for q in range(nx // nodes):
            pieces = [turned(init_ref[c, q * nodes + i], windows.width * (i - me)) for i in range(nodes)]
            pack_ref[rows_at((c * (nx // nodes) + q) * ny, ny), :] = merged(pieces, lanes)
        return carry

    lax.fori_loop(0, comps, step, 0)


def blend_kernel(start_ref, *refs):
    nodes = len(refs) - 6
    parts, (win_ref, nat_ref, lo_ref, hi_ref, side_ref, al_ref) = refs[:nodes], refs[nodes:]
    comps, nx, ny, nz = nat_ref.shape
    windows = Windows(nx, nz, nodes)
    me = lax.axis_index("node")
    weights = [
        [by_node(me, [scaled_weight(m, n ^ k) for n in range(nodes)]) for k in range(nodes)] for m in range(nodes)
    ]

    def step(c, carry):
        for r in range(windows.rows):
            at = rows_at((c * windows.rows + r) * ny, ny)
            start = start_ref[at, :]
            rates = [part[at, :] for part in parts]
            states = []
            for m in range(nodes):
                value = start
                for k in range(nodes):
                    value = value + weights[m][k] * rates[k]
                value = turned(value, windows.width * m)
                win_ref[m, at, :] = value
                states.append(value)
            for s in range(windows.slots):
                nat_ref[c, s * windows.rows + r] = windows.joined(states, s)
        return carry

    lax.fori_loop(0, comps, step, 0)

    def read(c, i):
        return nat_ref[c, i]

    best = tuple(jnp.zeros((ny, nz), jnp.float32) for _ in range(3))
    tile = alpha_tile(faster(best, read, 0, nx, comps), windows.width)

    def spread(i, carry):
        al_ref[i] = tile
        return carry

    lax.fori_loop(0, al_ref.shape[0], spread, 0)
    write_edges(read, nx, ny, comps, lo_ref, hi_ref, side_ref)


def across_lanes(u, alphas, side_ref, dims, zp, zm, fy, yp, ym, depth):
    comps, nx, ny, nz = dims
    rows = yp.shape[0] // (ny + 2 * HALO)
    every = range(comps)

    def own(i, carry):
        along_y, *rest = splits([u(c, i) for c in every], alphas, (1, 2) if depth else (1,))
        for c in every:
            for t in range(0, ny, TILE):
                at = pl.ds((HALO + t) * rows + c * nx + i, TILE, stride=rows)
                yp[at, :] = along_y[0][c][t : t + TILE]
                ym[at, :] = along_y[1][c][t : t + TILE]
        if depth:
            depth(i, rest[0])
        return carry

    lax.fori_loop(0, nx, own, 0)

    def ghost(i, carry):
        row = jnp.where(i < HALO, i, i + ny) * rows
        ((p, m),) = splits([side_ref[0, pl.ds(i * rows + c * nx, nx), :] for c in every], alphas, (1,))
        for c in every:
            yp[pl.ds(row + c * nx, nx), :] = p[c]
            ym[pl.ds(row + c * nx, nx), :] = m[c]
        return carry

    lax.fori_loop(0, 2 * HALO, ghost, 0)

    blocks = rows // TILE
    share = zp.shape[0] // blocks
    assert share * blocks == zp.shape[0]
    piece = max(p for p in range(TILE, 41, TILE) if share % p == 0)

    def along(b, carry):
        first = pl.multiple_of(b * TILE, TILE)

        def load(j):
            at = pl.ds(j * rows + first, TILE)
            return yp[at, :], ym[at, :]

        def store(i, value):
            fy[pl.ds(i * rows + first, TILE), :] = value

        stream(load, store, ny)
        for n in range(0, share, piece):
            at = rows_at(b * share + n, piece)
            zp[at, :] = rolled(zp[at, :], zm[at, :])
        return carry

    lax.fori_loop(0, blocks, along, 0)


def along_first(u, alphas, lo_ref, hi_ref, fy, rate, xp, xm, extra, after):
    comps, nx, ny, nz = rate.shape
    rows = fy.shape[0] // ny
    every = range(comps)

    def split(fields, at):
        ((p, m),) = splits(fields, alphas, (0,))
        for c in every:
            xp[at, c * ny : (c + 1) * ny, :] = p[c]
            xm[at, c * ny : (c + 1) * ny, :] = m[c]

    def own(i, carry):
        split([u(c, i) for c in every], i + HALO)
        return carry

    lax.fori_loop(0, nx, own, 0)
    for ref, start in ((lo_ref, 0), (hi_ref, nx + HALO)):

        def ghost(i, carry, ref=ref, start=start):
            split([ref[0, rows_at((c * HALO + i) * ny, ny), :] for c in every], start + i)
            return carry

        lax.fori_loop(0, HALO, ghost, 0)

    tiles = ny // TILE

    def along(b, carry):
        c, t = b // tiles, lax.rem(b, tiles) * TILE
        first = pl.multiple_of(b * TILE, TILE)

        def load(j):
            return xp[j, pl.ds(first, TILE), :], xm[j, pl.ds(first, TILE), :]

        def store(i, value):
            cross = fy[pl.ds(t * rows + c * nx + i, TILE, stride=rows), :]
            rate[c, i, rows_at(t, TILE), :] = value + (cross + extra(c, i, t))

        stream(load, store, nx)
        done = jnp.maximum(b - 1, 0)
        after(done // tiles, pl.multiple_of(lax.rem(done, tiles) * TILE, TILE))
        return carry

    lax.fori_loop(0, comps * tiles, along, 0)
    after(comps - 1, ny - TILE)


def tile_rows(tile):
    return [tile[k : k + 1, :] for k in range(3)]


def first_lanes_kernel(u_ref, side_ref, al_ref, other_ref, zp, fy, al_out, zm, yp, ym):
    comps, nx, ny, nz = u_ref.shape[1:]
    tile = jnp.maximum(al_ref[...], other_ref[...])
    al_out[...] = tile

    def depth(i, split):
        for c in range(comps):
            at = rows_at((c * nx + i) * ny, ny)
            zp[at, :] = split[0][c]
            zm[at, :] = split[1][c]

    across_lanes(lambda c, i: u_ref[0, c, i], tile_rows(tile), side_ref, u_ref.shape[1:], zp, zm, fy, yp, ym, depth)


def first_rows_kernel(u_ref, lo_ref, hi_ref, al_ref, zp, fy, *refs):
    parts, (rate, xp, xm) = refs[:-3], refs[-3:]
    nodes = len(parts)
    comps, nx, ny, nz = u_ref.shape[1:]
    windows = Windows(nx, nz, nodes)
    me = lax.axis_index("node")

    def extra(c, i, t):
        return zp[rows_at((c * nx + i) * ny + t, TILE), :]

    def after(c, t):
        for r in range(windows.rows):
            values = [rate[c, s * windows.rows + r, pl.ds(t, TILE), :] for s in range(windows.slots)]
            at = rows_at((c * windows.rows + r) * ny + t, TILE)
            for k in range(nodes):
                parts[k][at, :] = windows.cut(values, me ^ k)

    along_first(lambda c, i: u_ref[0, c, i], tile_rows(al_ref), lo_ref, hi_ref, fy, rate, xp, xm, extra, after)


def second_lanes_kernel(nat_ref, win_ref, side_ref, al_ref, zp, fy, al_out, zm, yp, ym):
    nodes = win_ref.shape[0]
    comps, nx, ny, nz = nat_ref.shape
    windows = Windows(nx, nz, nodes)
    part = comps * windows.rows * ny
    tiles = al_ref.shape[0]
    tile = lax.fori_loop(
        1, tiles, lambda i, best: jnp.maximum(best, al_ref[i]), al_ref[0], unroll=True if tiles <= 32 else 1
    )
    al_out[...] = tile
    alphas = tile_rows(tile)
    group = lane_index((1, nz)) // windows.width

    for m in range(nodes):
        alpha = jnp.max(jnp.where(group == m, alphas[2], 0.0))

        def depth(r, carry, m=m, alpha=alpha):
            places = [(c * windows.rows + r) * ny for c in range(comps)]
            fields = [win_ref[m, rows_at(place, ny), :] for place in places]
            ((plus, minus),) = splits(fields, [None, None, alpha], (2,))
            for c in range(comps):
                at = rows_at(m * part + places[c], ny)
                zp[at, :] = plus[c]
                zm[at, :] = minus[c]
            return carry

        lax.fori_loop(0, windows.rows, depth, 0)

    across_lanes(lambda c, i: nat_ref[c, i], alphas, side_ref, nat_ref.shape, zp, zm, fy, yp, ym, None)


def second_rows_kernel(nat_ref, lo_ref, hi_ref, al_ref, zp, fy, pack_ref, *refs):
    outs, (rate, xp, xm) = refs[:-3], refs[-3:]
    nodes = len(outs)
    comps, nx, ny, nz = nat_ref.shape
    windows = Windows(nx, nz, nodes)
    part = comps * windows.rows * ny
    me = lax.axis_index("node")
    weights = [
        [by_node(me, [scaled_weight(n ^ k, j) for n in range(nodes)]) for j in range(nodes)] for k in range(nodes)
    ]
    lanes = lane_index((TILE, nz)) // windows.width

    def extra(c, i, t):
        s, r = i // windows.rows, i % windows.rows
        place = (c * windows.rows + r) * ny + t
        return windows.joined([zp[rows_at(m * part + place, TILE), :] for m in range(nodes)], s)

    def after(c, t):
        for q in range(nx // nodes):
            at = rows_at((c * (nx // nodes) + q) * ny + t, TILE)
            start = pack_ref[at, :]
            rows = [rate[c, q * nodes + i, pl.ds(t, TILE), :] for i in range(nodes)]
            rates = [
                merged([turned(rows[i], windows.width * (i - j)) for i in range(nodes)], lanes) for j in range(nodes)
            ]
            for k in range(nodes):
                value = start
                for j in range(nodes):
                    value = value + weights[k][j] * rates[j]
                outs[k][at, :] = turned(value, windows.width * me)

    along_first(lambda c, i: nat_ref[c, i], tile_rows(al_ref), lo_ref, hi_ref, fy, rate, xp, xm, extra, after)


def close_kernel(*refs):
    parts, (out_hbm, out_ref, sems) = refs[:-3], refs[-3:]
    nodes = len(parts)
    comps, nx, ny, nz = out_ref.shape
    width = nz // nodes
    me = lax.axis_index("node")
    lanes = lane_index((ny, nz)) // width
    copies = []
    for c in range(comps):
        for q in range(nx // nodes):
            at = pl.ds((c * (nx // nodes) + q) * ny, ny)
            values = [part[at, :] for part in parts]
            for i in range(nodes):
                out = values[0]
                for k in range(1, nodes):
                    out = jnp.where(lanes == lax.rem((me ^ k) + i, nodes), values[k], out)
                out_ref[c, q * nodes + i] = turned(out, -width * i)
        copies.append(pltpu.make_async_copy(out_ref.at[c], out_hbm.at[0, c], sems.at[c]))
        copies[-1].start()
    for copy in copies:
        copy.wait()


def call(kernel, name, outs, operands, scratch=(), flops=1_000_000, anywhere=False, outside=False):
    vmem, hbm = pl.BlockSpec(memory_space=pltpu.VMEM), pl.BlockSpec(memory_space=pl.ANY)
    moved = sum(4 * x.size for x in operands)
    scratch = [pltpu.VMEM(x, jnp.float32) if isinstance(x, tuple) else x for x in scratch]
    return pl.pallas_call(
        kernel,
        out_shape=[jax.ShapeDtypeStruct(shape, jnp.float32) for shape in outs],
        in_specs=[hbm if anywhere else vmem] * len(operands),
        out_specs=[hbm if outside else vmem] * len(outs),
        scratch_shapes=scratch,
        compiler_params=pltpu.CompilerParams(vmem_limit_bytes=32 * 1024 * 1024),
        cost_estimate=pl.CostEstimate(flops=flops, bytes_accessed=2 * moved, transcendentals=0),
        name=name,
    )(*operands)


def shifted(value, axis, by):
    count = lax.axis_size(axis)
    return lax.ppermute(value, axis, [(i, (i + by) % count) for i in range(count)])


def swapped(value, by):
    return lax.ppermute(value, "node", [(i, i ^ by) for i in range(lax.axis_size("node"))])


def neighbours(lo, hi, side):
    lower, upper = shifted(hi, "gx", 1), shifted(lo, "gx", -1)
    if lax.axis_size("gy") == 2:
        return lower, upper, shifted(side, "gy", 1)
    half = side.shape[1] // 2
    side = jnp.concatenate([shifted(side[:, :half], "gy", 1), shifted(side[:, half:], "gy", -1)], axis=1)
    return lower, upper, side


def largest(tile):
    if lax.axis_size("gx") > 4 or lax.axis_size("gy") > 2:
        tile = lax.pmax(tile, ("gx", "gy"))
        return tile, tile
    others = [shifted(tile, "gx", by) for by in range(1, lax.axis_size("gx"))]
    tile = functools.reduce(jnp.maximum, others, tile)
    return tile, shifted(tile, "gy", 1)


def exchanged(parts):
    moved = {k: swapped(parts[k], k) for k in sorted(range(1, len(parts)), reverse=True)}
    return [parts[0]] + [moved[k] for k in range(1, len(parts))]


def local(initial, guesses):
    comps, nx, ny, nz = initial.shape
    nodes = lax.axis_size("node")
    devices = nodes * lax.axis_size("gx") * lax.axis_size("gy")
    rows = -(-comps * nx // TILE) * TILE
    windows = Windows(nx, nz, nodes)
    edge = (1, comps * HALO * ny, nz)
    edges = [edge, edge, (1, 2 * HALO * rows, nz)]
    tile_shape = (TILE, nz)
    part = (comps * windows.rows * ny, nz)
    pack = (comps * nx // nodes * ny, nz)
    second = (ny * rows, nz)
    padded = [((ny + 2 * HALO) * rows, nz)] * 2
    slabs = [initial.shape] + [(nx + 2 * HALO, comps * ny, nz)] * 2
    chunks = 4 if nx % 4 == 0 else 1

    lo, hi, side, tile = call(
        open_kernel,
        "open_kernel",
        edges + [tile_shape],
        [guesses],
        [initial.shape, pltpu.SemaphoreType.DMA((chunks,))],
        anywhere=True,
    )
    lower, upper, side = neighbours(lo, hi, side)
    tile, other = largest(tile)
    start, start_pack = call(
        functools.partial(start_kernel, nodes=nodes), "start_kernel", [part, pack], [initial]
    )
    whole = (comps * nx * ny, nz)
    depth, across, tile = call(
        first_lanes_kernel,
        "first_lanes_kernel",
        [whole, second, tile_shape],
        [guesses, side, tile, other],
        [whole] + padded,
        20_000_000,
    )
    parts = call(
        first_rows_kernel, "first_rows_kernel", [part] * nodes, [guesses, lower, upper, tile, depth, across], slabs, 10_000_000
    )
    win, nat, lo, hi, side, tile = call(
        blend_kernel,
        "blend_kernel",
        [(nodes,) + part, initial.shape] + edges + [(devices,) + tile_shape],
        [start] + exchanged(parts),
    )
    lower, upper, side = neighbours(lo, hi, side)
    tiles = lax.all_to_all(tile, ("node", "gx", "gy"), 0, 0)
    whole = (nodes * part[0], nz)
    depth, across, tile = call(
        second_lanes_kernel,
        "second_lanes_kernel",
        [whole, second, tile_shape],
        [nat, win, side, tiles],
        [whole] + padded,
        20_000_000,
    )
    outs = call(
        second_rows_kernel,
        "second_rows_kernel",
        [pack] * nodes,
        [nat, lower, upper, tile, depth, across, start_pack],
        slabs,
        10_000_000,
    )
    (states,) = call(
        close_kernel,
        "close_kernel",
        [(1,) + initial.shape],
        exchanged(outs),
        [initial.shape, pltpu.SemaphoreType.DMA((comps,))],
        outside=True,
    )
    return states


def solution(mesh):
    return jax.shard_map(
        local,
        mesh=mesh,
        in_specs=(P(None, "gx", "gy", None), P("node", None, "gx", "gy", None)),
        out_specs=P("node", None, "gx", "gy", None),
        check_vma=False,
    )
```

```python
import functools

import jax
import jax.numpy as jnp
from jax import lax
from jax.experimental import pallas as pl
from jax.experimental.pallas import tpu as pltpu
from jax.sharding import PartitionSpec as P

SWEEPS = 2
HALO = 3
COMPONENTS = 5
TILE = 8
CHUNK = 16

heat_ratio = 1.4
step_size = 0.025
density_floor = 0.5
pressure_floor = 0.25
epsilon = 1e-06
radau_weights = [
    [0.112999479323156, -0.040309220723522, 0.025802377420336, -0.009904676507266],
    [0.2343839957474, 0.206892573935359, -0.047857128048541, 0.016047422806516],
    [0.21668178462325, 0.406123263867373, 0.189036518170056, -0.024182104899833],
    [0.220462211176768, 0.388193468843172, 0.32884431998006, 0.0625],
]


def reciprocal(value):
    return pl.reciprocal(value, approx=True)


def primitives(fields):
    inverse = 1.0 / jnp.maximum(fields[0], density_floor)
    velocity = [fields[k] * inverse for k in (1, 2, 3)]
    energy = fields[1] * velocity[0] + fields[2] * velocity[1] + fields[3] * velocity[2]
    pressure = jnp.maximum(0.4 * (fields[4] - 0.5 * energy), pressure_floor)
    return inverse, velocity, pressure


def signal_speeds(fields):
    inverse, velocity, pressure = primitives(fields)
    sound = jnp.sqrt(heat_ratio * pressure * inverse)
    return [jnp.abs(v) + sound for v in velocity]


def half_fluxes(half, speed, half_pressure, direction):
    flux = [half[direction + 1]] + [half[k] * speed for k in (1, 2, 3)]
    flux.append((half[4] + half_pressure) * speed)
    flux[direction + 1] = flux[direction + 1] + half_pressure
    return flux


def splits(fields, alphas, directions=(0, 1, 2)):
    _, velocity, pressure = primitives(fields)
    half = [0.5 * field for field in fields]
    half_pressure = 0.5 * pressure
    out = []
    for direction in directions:
        flux = half_fluxes(half, velocity[direction], half_pressure, direction)
        signal = [alphas[direction] * value for value in half]
        out.append(
            ([f + s for f, s in zip(flux, signal)], [f - s for f, s in zip(flux, signal)])
        )
    return out


def cell_terms(below, above):
    second = above - below
    both = below + above
    square = second * second
    middle = 0.25 * (both * both) + ((13.0 / 12.0) * square + epsilon)
    outer = middle + square
    cross = both * second
    return second, outer + cross, middle, outer - cross


def correction(first, middle, last, third_first, third_last):
    ratio_first = middle * reciprocal(first)
    ratio_last = middle * reciprocal(last)
    weight_first = ratio_first * ratio_first
    weight_last = 1.5 * (ratio_last * ratio_last)
    total = (6.0 + weight_first) + (weight_last + weight_last)
    return (weight_first * third_first + weight_last * third_last) * reciprocal(total)


def stream(load, store, count):
    plus, minus, centre = {}, {}, {}
    terms_plus, terms_minus, third_plus, third_minus, interface = {}, {}, {}, {}, {}
    differences_plus, differences_minus = {}, {}
    plus[0], minus[0] = load(0)
    for j in range(1, count + 2 * HALO):
        plus[j], minus[j] = load(j)
        differences_plus[j] = plus[j] - plus[j - 1]
        differences_minus[j] = minus[j] - minus[j - 1]
        cell = j - 1
        if cell < 1:
            continue
        terms_plus[cell] = cell_terms(differences_plus[cell], differences_plus[j])
        terms_minus[cell] = cell_terms(differences_minus[cell], differences_minus[j])
        if 2 <= cell <= count + 3:
            centre[cell] = 6.0 * (plus[cell] + minus[cell]) - (
                terms_plus[cell][0] + terms_minus[cell][0]
            )
        if cell < 2:
            continue
        third_plus[cell] = terms_plus[cell][0] - terms_plus[cell - 1][0]
        third_minus[cell] = terms_minus[cell][0] - terms_minus[cell - 1][0]
        if cell < 4:
            continue
        at = cell - 2
        right = correction(
            terms_plus[at - 1][1], terms_plus[at][2], terms_plus[at + 1][3], third_plus[at], third_plus[at + 1]
        )
        left = correction(
            terms_minus[at + 2][3], terms_minus[at + 1][2], terms_minus[at][1],
            third_minus[at + 2], third_minus[at + 1],
        )
        interface[at] = (third_plus[at + 1] - third_minus[at + 1]) - 4.0 * (right - left)
        if at >= 3:
            store(at - 3, (centre[at - 1] - centre[at + 1]) + (interface[at - 1] - interface[at]))


def lane_index(shape):
    return lax.broadcasted_iota(jnp.int32, shape, len(shape) - 1)


def turned(value, by):
    size = value.shape[-1]
    if isinstance(by, int):
        by = by % size
        return value if by == 0 else pltpu.roll(value, by, value.ndim - 1)
    return pltpu.roll(value, lax.rem(by + 4 * size, size), value.ndim - 1)


def merged(pieces, slot):
    out = pieces[0]
    for number, piece in enumerate(pieces[1:], 1):
        out = jnp.where(slot == number, piece, out)
    return out


def rows_at(start, size):
    return pl.ds(start if isinstance(start, int) else pl.multiple_of(start, TILE), size)


def by_node(me, values):
    out = jnp.float32(values[0])
    for n, value in enumerate(values[1:], 1):
        out = jnp.where(me == n, jnp.float32(value), out)
    return out


def scaled_weight(row, column):
    return radau_weights[row][column] * (step_size / 12.0)


class Blocks:
    def __init__(self, comps, nx, ny, nz):
        self.comps, self.nx, self.ny, self.nz = comps, nx, ny, nz
        self.per = nz // ny
        self.left = nx - self.per
        assert nz % ny == 0 and ny % TILE == 0 and 2 * self.left == self.per
        self.half = nz // 2
        self.count = comps + (comps + 1) // 2
        self.step = CHUNK + 8

    def pair(self, b):
        first = 2 * (b - self.comps)
        return first, min(first + 1, self.comps - 1) if isinstance(b, int) else jnp.minimum(first + 1, self.comps - 1)

    def whole(self, ref, c):
        return ref[c, pl.ds(0, self.per)].reshape(self.nz, self.nz)

    def leftovers(self, ref, first, second):
        at = pl.ds(self.per, self.left)
        shape = (self.half, self.nz)
        return jnp.concatenate([ref[first, at].reshape(shape), ref[second, at].reshape(shape)], axis=0)

    def natural(self, ref, b):
        return self.whole(ref, b) if b < self.comps else self.leftovers(ref, *self.pair(b))

    def put_natural(self, ref, b, value):
        if b < self.comps:
            ref[b, pl.ds(0, self.per)] = value.reshape(self.per, self.ny, self.nz)
            return
        at = pl.ds(self.per, self.left)
        shape = (self.left, self.ny, self.nz)
        first, second = self.pair(b)
        ref[first, at] = value[: self.half].reshape(shape)
        if second != first:
            ref[second, at] = value[self.half :].reshape(shape)

    def row(self, c, i, t):
        if i < self.per:
            return c * self.nz + (i * self.ny + t)
        return (self.comps + c // 2) * self.nz + lax.rem(c, 2) * self.half + ((i - self.per) * self.ny + t)


def split_depth(blocks, read, alpha, write):
    comps = blocks.comps
    ((plus, minus),) = splits([read(c) for c in range(comps)], [None, None, alpha], (2,))
    for c in range(comps):
        write(c, plus[c], minus[c])
    shared = [read(b) for b in range(comps, blocks.count)]
    fields = [shared[c // 2] if c % 2 == 0 else turned(shared[c // 2], blocks.half) for c in range(comps)]
    ((plus, minus),) = splits(fields, [None, None, alpha], (2,))
    lower = lane_index(fields[0].shape) < blocks.half
    for b in range(comps, blocks.count):
        first, second = blocks.pair(b)
        write(b, *[jnp.where(lower, v[first], turned(v[second], blocks.half)) for v in (plus, minus)])


def write_edges(read, nx, ny, comps, lo_ref, hi_ref, side_ref):
    rows = side_ref.shape[1] // (2 * HALO)
    for c in range(comps):
        for i in range(HALO):
            lo_ref[0, pl.ds((c * HALO + i) * ny, ny), :] = read(c, i)
            hi_ref[0, pl.ds((c * HALO + i) * ny, ny), :] = read(c, nx - HALO + i)

    def side(i, carry):
        for c in range(comps):
            value = read(c, i)
            side_ref[0, pl.ds(c * nx + i, HALO, stride=rows), :] = value[ny - HALO :]
            side_ref[0, pl.ds(HALO * rows + c * nx + i, HALO, stride=rows), :] = value[:HALO]
        return carry

    lax.fori_loop(0, nx, side, 0)


def faster(best, read, first, count, comps):
    def step(i, best):
        speeds = signal_speeds([read(c, i) for c in range(comps)])
        return tuple(jnp.maximum(b, s) for b, s in zip(best, speeds))

    return lax.fori_loop(first, first + count, step, best)


def alpha_tile(best, group):
    nz = best[0].shape[-1]
    rows = [jnp.max(b, axis=0, keepdims=True) for b in best]
    tile = jnp.concatenate(rows + [jnp.zeros((TILE - 3, nz), jnp.float32)], axis=0)
    lane = lane_index(tile.shape)
    by = 1
    while by < group:
        other = jnp.where((lane & by) != 0, turned(tile, by), turned(tile, -by))
        tile = jnp.maximum(tile, other)
        by *= 2
    return tile


def open_kernel(u_hbm, u_ref, lo_ref, hi_ref, side_ref, al_ref, sems):
    comps, nx, ny, nz = u_ref.shape
    chunks = sems.shape[0]
    size = nx // chunks
    copies = []
    for n in range(chunks):
        at = pl.ds(n * size, size)
        copies.append(pltpu.make_async_copy(u_hbm.at[0, :, at], u_ref.at[:, at], sems.at[n]))
        copies[-1].start()

    def read(c, i):
        return u_ref[c, i]

    best = tuple(jnp.zeros((ny, nz), jnp.float32) for _ in range(3))
    for n in range(chunks):
        copies[n].wait()
        best = faster(best, read, n * size, size, comps)
    al_ref[...] = alpha_tile(best, nz)
    write_edges(read, nx, ny, comps, lo_ref, hi_ref, side_ref)


def turn_kernel(u_ref, rows_ref):
    blocks = Blocks(*u_ref.shape)
    nz = blocks.nz
    for b in range(blocks.count):
        value = blocks.natural(u_ref, b).T
        rows_ref[b, pl.ds(HALO, nz), :] = value
        rows_ref[b, pl.ds(0, HALO), :] = value[nz - HALO :]
        rows_ref[b, pl.ds(HALO + nz, HALO), :] = value[:HALO]


def start_kernel(init_ref, rows_ref, pack_ref, turned_ref, *, nodes):
    comps, nx, ny, nz = init_ref.shape
    blocks = Blocks(comps, nx, ny, nz)
    width = nz // nodes
    me = lax.axis_index("node")
    lanes = lane_index((ny, nz)) // width
    for b in range(blocks.count):
        send_quarter(blocks.natural(init_ref, b).T, turned_ref, b, [rows_ref], [me], width)

    def step(c, carry):
        for q in range(nx // nodes):
            pieces = [turned(init_ref[c, q * nodes + i], width * (i - me)) for i in range(nodes)]
            pack_ref[rows_at((c * (nx // nodes) + q) * ny, ny), :] = merged(pieces, lanes)
        return carry

    lax.fori_loop(0, comps, step, 0)


def send_quarter(value, ring_ref, b, parts, quarters, width):
    nz = value.shape[0]
    base = b * (nz + 2 * TILE)
    ring_ref[rows_at(base + TILE, nz), :] = value
    ring_ref[rows_at(base, TILE), :] = value[nz - TILE :]
    ring_ref[rows_at(base + TILE + nz, TILE), :] = value[:TILE]
    size = width + 8
    for part, quarter in zip(parts, quarters):
        part[rows_at(b * size, size), :] = ring_ref[pl.ds(base + (TILE - HALO) + quarter * width, size), :]


def blend_kernel(start_ref, *refs):
    nodes = len(refs) - 6
    parts, (rows_ref, nat_ref, lo_ref, hi_ref, side_ref, al_ref) = refs[:nodes], refs[nodes:]
    comps, nx, ny, nz = nat_ref.shape
    blocks = Blocks(comps, nx, ny, nz)
    width = nz // nodes
    size = width + 8
    me = lax.axis_index("node")
    weights = [
        [by_node(me, [scaled_weight(m, n ^ k) for n in range(nodes)]) for k in range(nodes)] for m in range(nodes)
    ]
    for b in range(blocks.count):
        at = pl.ds(b * size, size)
        start = start_ref[at, :]
        rates = [part[at, :] for part in parts]
        for m in range(nodes):
            value = start
            for k in range(nodes):
                value = value + weights[m][k] * rates[k]
            rows_ref[m, at, :] = value
        own = pl.ds(b * size + HALO, width)
        state = jnp.concatenate([rows_ref[m, own, :] for m in range(nodes)], axis=0)
        blocks.put_natural(nat_ref, b, state.T)

    def read(c, i):
        return nat_ref[c, i]

    best = tuple(jnp.zeros((ny, nz), jnp.float32) for _ in range(3))
    tile = alpha_tile(faster(best, read, 0, nx, comps), width)

    def spread(i, carry):
        al_ref[i] = tile
        return carry

    lax.fori_loop(0, al_ref.shape[0], spread, 0)
    write_edges(read, nx, ny, comps, lo_ref, hi_ref, side_ref)


def along_second(u, alphas, side_ref, dims, fy, yp, ym):
    comps, nx, ny, nz = dims
    rows = yp.shape[0] // (ny + 2 * HALO)
    every = range(comps)

    def own(i, carry):
        ((p, m),) = splits([u(c, i) for c in every], alphas, (1,))
        for c in every:
            for t in range(0, ny, TILE):
                at = pl.ds((HALO + t) * rows + c * nx + i, TILE, stride=rows)
                yp[at, :] = p[c][t : t + TILE]
                ym[at, :] = m[c][t : t + TILE]
        return carry

    lax.fori_loop(0, nx, own, 0)

    def ghost(i, carry):
        row = jnp.where(i < HALO, i, i + ny) * rows
        ((p, m),) = splits([side_ref[0, pl.ds(i * rows + c * nx, nx), :] for c in every], alphas, (1,))
        for c in every:
            yp[pl.ds(row + c * nx, nx), :] = p[c]
            ym[pl.ds(row + c * nx, nx), :] = m[c]
        return carry

    lax.fori_loop(0, 2 * HALO, ghost, 0)

    def along(b, carry):
        first = pl.multiple_of(b * TILE, TILE)

        def load(j):
            at = pl.ds(j * rows + first, TILE)
            return yp[at, :], ym[at, :]

        def store(i, value):
            fy[pl.ds(i * rows + first, TILE), :] = value

        stream(load, store, ny)
        return carry

    lax.fori_loop(0, rows // TILE, along, 0)


def along_last(blocks, zp, zm, fz, after):
    size = blocks.step * TILE

    def along(b, carry):
        def load(j):
            at = pl.ds(b * size + j, TILE, stride=blocks.step)
            return zp[at, :], zm[at, :]

        def store(i, value):
            fz[pl.ds(b * blocks.nz + i, TILE, stride=CHUNK), :] = value

        stream(load, store, CHUNK)
        after(jnp.maximum(b - 1, 0))
        return carry

    lax.fori_loop(0, blocks.count, along, 0)
    after(blocks.count - 1)


def along_first(u, alphas, lo_ref, hi_ref, fy, rate, xp, xm, extra, after):
    comps, nx, ny, nz = rate.shape
    rows = fy.shape[0] // ny
    every = range(comps)

    def split(fields, at):
        ((p, m),) = splits(fields, alphas, (0,))
        for c in every:
            xp[at, c * ny : (c + 1) * ny, :] = p[c]
            xm[at, c * ny : (c + 1) * ny, :] = m[c]

    def own(i, carry):
        split([u(c, i) for c in every], i + HALO)
        return carry

    lax.fori_loop(0, nx, own, 0)
    for ref, start in ((lo_ref, 0), (hi_ref, nx + HALO)):

        def ghost(i, carry, ref=ref, start=start):
            split([ref[0, rows_at((c * HALO + i) * ny, ny), :] for c in every], start + i)
            return carry

        lax.fori_loop(0, HALO, ghost, 0)

    def along(c, carry):
        for t in range(0, ny, TILE):

            def load(j, t=t):
                at = rows_at(c * ny + t, TILE)
                return xp[j, at, :], xm[j, at, :]

            def store(i, value, t=t):
                value = value + fy[pl.ds(t * rows + c * nx + i, TILE, stride=rows), :]
                rate[c, i, pl.ds(t, TILE), :] = value if extra is None else value + extra(c, i, t)

            stream(load, store, nx)
        after(jnp.maximum(c - 1, 0))
        return carry

    lax.fori_loop(0, comps, along, 0)
    after(jnp.int32(comps - 1))


def tile_rows(tile):
    return [tile[k : k + 1, :] for k in range(3)]


def first_lanes_kernel(u_ref, rows_ref, side_ref, al_ref, other_ref, fz, fy, al_out, zp, zm, yp, ym):
    dims = u_ref.shape
    blocks = Blocks(*dims)
    tile = jnp.maximum(al_ref[...], other_ref[...])
    al_out[...] = tile
    alphas = tile_rows(tile)
    along_second(lambda c, i: u_ref[c, i], alphas, side_ref, dims, fy, yp, ym)

    def depth(n, carry):
        at = rows_at(n * CHUNK, blocks.step)

        def write(b, plus, minus):
            to = rows_at((b * TILE + n) * blocks.step, blocks.step)
            zp[to, :] = plus
            zm[to, :] = minus

        split_depth(blocks, lambda b: rows_ref[b, at, :], alphas[2], write)
        return carry

    lax.fori_loop(0, TILE, depth, 0)
    along_last(blocks, zp, zm, fz, lambda b: None)


def first_rows_kernel(u_ref, lo_ref, hi_ref, al_ref, fz, fy, *refs):
    parts, (rate, xp, xm, ring) = refs[:-4], refs[-4:]
    nodes = len(parts)
    blocks = Blocks(*u_ref.shape)
    nz = blocks.nz
    me = lax.axis_index("node")
    quarters = [me ^ k for k in range(nodes)]

    def send(value, b):
        value = value.T + fz[rows_at(b * nz, nz), :]
        send_quarter(value, ring, b, parts, quarters, nz // nodes)

    def after(c):
        send(blocks.whole(rate, c), c)
        b = blocks.comps + c // 2
        send(blocks.leftovers(rate, *blocks.pair(b)), b)

    along_first(lambda c, i: u_ref[c, i], tile_rows(al_ref), lo_ref, hi_ref, fy, rate, xp, xm, None, after)


def second_lanes_kernel(nat_ref, rows_ref, side_ref, al_ref, fz, fy, al_out, zp, zm, yp, ym, back):
    nodes = rows_ref.shape[0]
    dims = nat_ref.shape
    blocks = Blocks(*dims)
    nz = blocks.nz
    width = nz // nodes
    tiles = al_ref.shape[0]
    tile = lax.fori_loop(
        1, tiles, lambda i, best: jnp.maximum(best, al_ref[i]), al_ref[0], unroll=True if tiles <= 32 else 1
    )
    al_out[...] = tile
    alphas = tile_rows(tile)
    along_second(lambda c, i: nat_ref[c, i], alphas, side_ref, dims, fy, yp, ym)
    group = lane_index((1, nz)) // width
    each = width // CHUNK
    for m in range(nodes):
        alpha = jnp.max(jnp.where(group == m, alphas[2], 0.0))

        def depth(n, carry, m=m, alpha=alpha):
            def read(b):
                return rows_ref[m, rows_at(b * (width + 8) + n * CHUNK, blocks.step), :]

            def write(b, plus, minus):
                to = rows_at((b * TILE + m * each + n) * blocks.step, blocks.step)
                zp[to, :] = plus
                zm[to, :] = minus

            split_depth(blocks, read, alpha, write)
            return carry

        lax.fori_loop(0, each, depth, 0)

    def after(b):
        at = rows_at(b * nz, nz)
        fz[at, :] = back[at, :].T

    along_last(blocks, zp, zm, back, after)


def second_rows_kernel(nat_ref, lo_ref, hi_ref, al_ref, fz, fy, pack_ref, *refs):
    outs, (rate, xp, xm) = refs[:-3], refs[-3:]
    nodes = len(outs)
    comps, nx, ny, nz = nat_ref.shape
    blocks = Blocks(comps, nx, ny, nz)
    width = nz // nodes
    me = lax.axis_index("node")
    weights = [
        [by_node(me, [scaled_weight(n ^ k, j) for n in range(nodes)]) for j in range(nodes)] for k in range(nodes)
    ]
    lanes = lane_index((TILE, nz)) // width

    def extra(c, i, t):
        return fz[rows_at(blocks.row(c, i, t), TILE), :]

    def after(c):
        for t in range(0, ny, TILE):
            for q in range(nx // nodes):
                at = rows_at((c * (nx // nodes) + q) * ny + t, TILE)
                start = pack_ref[at, :]
                rows = [rate[c, q * nodes + i, pl.ds(t, TILE), :] for i in range(nodes)]
                rates = [
                    merged([turned(rows[i], width * (i - j)) for i in range(nodes)], lanes) for j in range(nodes)
                ]
                for k in range(nodes):
                    value = start
                    for j in range(nodes):
                        value = value + weights[k][j] * rates[j]
                    outs[k][at, :] = turned(value, width * me)

    along_first(lambda c, i: nat_ref[c, i], tile_rows(al_ref), lo_ref, hi_ref, fy, rate, xp, xm, extra, after)


def close_kernel(*refs):
    parts, (out_hbm, out_ref, sems) = refs[:-3], refs[-3:]
    nodes = len(parts)
    comps, nx, ny, nz = out_ref.shape
    width = nz // nodes
    me = lax.axis_index("node")
    lanes = lane_index((ny, nz)) // width
    copies = []
    for c in range(comps):
        for q in range(nx // nodes):
            at = pl.ds((c * (nx // nodes) + q) * ny, ny)
            values = [part[at, :] for part in parts]
            for i in range(nodes):
                out = values[0]
                for k in range(1, nodes):
                    out = jnp.where(lanes == lax.rem((me ^ k) + i, nodes), values[k], out)
                out_ref[c, q * nodes + i] = turned(out, -width * i)
        copies.append(pltpu.make_async_copy(out_ref.at[c], out_hbm.at[0, c], sems.at[c]))
        copies[-1].start()
    for copy in copies:
        copy.wait()


def call(kernel, name, outs, operands, scratch=(), flops=1_000_000, anywhere=False, outside=False):
    vmem, hbm = pl.BlockSpec(memory_space=pltpu.VMEM), pl.BlockSpec(memory_space=pl.ANY)
    moved = sum(4 * x.size for x in operands)
    scratch = [pltpu.VMEM(x, jnp.float32) if isinstance(x, tuple) else x for x in scratch]
    return pl.pallas_call(
        kernel,
        out_shape=[jax.ShapeDtypeStruct(shape, jnp.float32) for shape in outs],
        in_specs=[hbm if anywhere else vmem] * len(operands),
        out_specs=[hbm if outside else vmem] * len(outs),
        scratch_shapes=scratch,
        compiler_params=pltpu.CompilerParams(vmem_limit_bytes=32 * 1024 * 1024),
        cost_estimate=pl.CostEstimate(flops=flops, bytes_accessed=2 * moved, transcendentals=0),
        name=name,
    )(*operands)


def shifted(value, axis, by):
    count = lax.axis_size(axis)
    return lax.ppermute(value, axis, [(i, (i + by) % count) for i in range(count)])


def swapped(value, by):
    return lax.ppermute(value, "node", [(i, i ^ by) for i in range(lax.axis_size("node"))])


def neighbours(lo, hi, side):
    lower, upper = shifted(hi, "gx", 1), shifted(lo, "gx", -1)
    if lax.axis_size("gy") == 2:
        return lower, upper, shifted(side, "gy", 1)
    half = side.shape[1] // 2
    side = jnp.concatenate([shifted(side[:, :half], "gy", 1), shifted(side[:, half:], "gy", -1)], axis=1)
    return lower, upper, side


def largest(tile):
    if lax.axis_size("gx") > 4 or lax.axis_size("gy") > 2:
        tile = lax.pmax(tile, ("gx", "gy"))
        return tile, tile
    others = [shifted(tile, "gx", by) for by in range(1, lax.axis_size("gx"))]
    tile = functools.reduce(jnp.maximum, others, tile)
    return tile, shifted(tile, "gy", 1)


def exchanged(parts):
    moved = {k: swapped(parts[k], k) for k in sorted(range(1, len(parts)), reverse=True)}
    return [parts[0]] + [moved[k] for k in range(1, len(parts))]


def local(initial, guesses):
    comps, nx, ny, nz = initial.shape
    nodes = lax.axis_size("node")
    devices = nodes * lax.axis_size("gx") * lax.axis_size("gy")
    rows = -(-comps * nx // TILE) * TILE
    blocks = Blocks(comps, nx, ny, nz)
    width = nz // nodes
    assert nz == CHUNK * TILE and width % CHUNK == 0 and nx % nodes == 0
    edge = (1, comps * HALO * ny, nz)
    edges = [edge, edge, (1, 2 * HALO * rows, nz)]
    tile_shape = (TILE, nz)
    part = (blocks.count * (width + 8), nz)
    pack = (comps * nx // nodes * ny, nz)
    across_shape = (ny * rows, nz)
    depth_shape = (blocks.count * nz, nz)
    padded = [(blocks.count * TILE * blocks.step, nz)] * 2 + [((ny + 2 * HALO) * rows, nz)] * 2
    slabs = [initial.shape] + [(nx + 2 * HALO, comps * ny, nz)] * 2
    ring = (blocks.count * (nz + 2 * TILE), nz)
    chunks = 4 if nx % 4 == 0 else 1

    field, lo, hi, side, tile = call(
        open_kernel,
        "open_kernel",
        [initial.shape] + edges + [tile_shape],
        [guesses],
        [pltpu.SemaphoreType.DMA((chunks,))],
        anywhere=True,
    )
    lower, upper, side = neighbours(lo, hi, side)
    tile, other = largest(tile)
    (turned_field,) = call(turn_kernel, "turn_kernel", [(blocks.count, nz + 8, nz)], [field])
    start, start_pack = call(
        functools.partial(start_kernel, nodes=nodes), "start_kernel", [part, pack], [initial], [ring]
    )
    depth, across, tile = call(
        first_lanes_kernel,
        "first_lanes_kernel",
        [depth_shape, across_shape, tile_shape],
        [field, turned_field, side, tile, other],
        padded,
        20_000_000,
    )
    parts = call(
        first_rows_kernel,
        "first_rows_kernel",
        [part] * nodes,
        [field, lower, upper, tile, depth, across],
        slabs + [ring],
        10_000_000,
    )
    turned_field, field, lo, hi, side, tile = call(
        blend_kernel,
        "blend_kernel",
        [(nodes,) + part, initial.shape] + edges + [(devices,) + tile_shape],
        [start] + exchanged(parts),
    )
    lower, upper, side = neighbours(lo, hi, side)
    tiles = lax.all_to_all(tile, ("node", "gx", "gy"), 0, 0)
    depth, across, tile = call(
        second_lanes_kernel,
        "second_lanes_kernel",
        [depth_shape, across_shape, tile_shape],
        [field, turned_field, side, tiles],
        padded + [depth_shape],
        20_000_000,
    )
    outs = call(
        second_rows_kernel,
        "second_rows_kernel",
        [pack] * nodes,
        [field, lower, upper, tile, depth, across, start_pack],
        slabs,
        10_000_000,
    )
    (states,) = call(
        close_kernel,
        "close_kernel",
        [(1,) + initial.shape],
        exchanged(outs),
        [initial.shape, pltpu.SemaphoreType.DMA((comps,))],
        outside=True,
    )
    return states


def solution(mesh):
    return jax.shard_map(
        local,
        mesh=mesh,
        in_specs=(P(None, "gx", "gy", None), P("node", None, "gx", "gy", None)),
        out_specs=P("node", None, "gx", "gy", None),
        check_vma=False,
    )
```

```python
import functools

import jax
import jax.numpy as jnp
from jax import lax
from jax.experimental import pallas as pl
from jax.experimental.pallas import tpu as pltpu
from jax.sharding import PartitionSpec as P

SWEEPS = 2
HALO = 3
COMPONENTS = 5
TILE = 8
CHUNK = 16

heat_ratio = 1.4
step_size = 0.025
density_floor = 0.5
pressure_floor = 0.25
epsilon = 1e-06
radau_weights = [
    [0.112999479323156, -0.040309220723522, 0.025802377420336, -0.009904676507266],
    [0.2343839957474, 0.206892573935359, -0.047857128048541, 0.016047422806516],
    [0.21668178462325, 0.406123263867373, 0.189036518170056, -0.024182104899833],
    [0.220462211176768, 0.388193468843172, 0.32884431998006, 0.0625],
]


def reciprocal(value):
    return pl.reciprocal(value, approx=True)


def primitives(fields):
    inverse = 1.0 / jnp.maximum(fields[0], density_floor)
    velocity = [fields[k] * inverse for k in (1, 2, 3)]
    energy = fields[1] * velocity[0] + fields[2] * velocity[1] + fields[3] * velocity[2]
    pressure = jnp.maximum(0.4 * (fields[4] - 0.5 * energy), pressure_floor)
    return inverse, velocity, pressure


def signal_speeds(fields):
    inverse, velocity, pressure = primitives(fields)
    sound = jnp.sqrt(heat_ratio * pressure * inverse)
    return [jnp.abs(v) + sound for v in velocity]


def half_fluxes(half, speed, half_pressure, direction):
    flux = [half[direction + 1]] + [half[k] * speed for k in (1, 2, 3)]
    flux.append((half[4] + half_pressure) * speed)
    flux[direction + 1] = flux[direction + 1] + half_pressure
    return flux


def splits(fields, alphas, directions=(0, 1, 2)):
    _, velocity, pressure = primitives(fields)
    half = [0.5 * field for field in fields]
    half_pressure = 0.5 * pressure
    out = []
    for direction in directions:
        flux = half_fluxes(half, velocity[direction], half_pressure, direction)
        signal = [alphas[direction] * value for value in half]
        out.append(
            ([f + s for f, s in zip(flux, signal)], [f - s for f, s in zip(flux, signal)])
        )
    return out


def cell_terms(below, above):
    second = above - below
    both = below + above
    square = second * second
    middle = 0.25 * (both * both) + ((13.0 / 12.0) * square + epsilon)
    outer = middle + square
    cross = both * second
    return second, outer + cross, middle, outer - cross


def correction(first, middle, last, third_first, third_last):
    ratio_first = middle * reciprocal(first)
    ratio_last = middle * reciprocal(last)
    weight_first = ratio_first * ratio_first
    weight_last = 1.5 * (ratio_last * ratio_last)
    total = (6.0 + weight_first) + (weight_last + weight_last)
    return (weight_first * third_first + weight_last * third_last) * reciprocal(total)


def stream(load, store, count):
    plus, minus, centre = {}, {}, {}
    terms_plus, terms_minus, third_plus, third_minus, interface = {}, {}, {}, {}, {}
    differences_plus, differences_minus = {}, {}
    plus[0], minus[0] = load(0)
    for j in range(1, count + 2 * HALO):
        plus[j], minus[j] = load(j)
        differences_plus[j] = plus[j] - plus[j - 1]
        differences_minus[j] = minus[j] - minus[j - 1]
        cell = j - 1
        if cell < 1:
            continue
        terms_plus[cell] = cell_terms(differences_plus[cell], differences_plus[j])
        terms_minus[cell] = cell_terms(differences_minus[cell], differences_minus[j])
        if 2 <= cell <= count + 3:
            centre[cell] = 6.0 * (plus[cell] + minus[cell]) - (
                terms_plus[cell][0] + terms_minus[cell][0]
            )
        if cell < 2:
            continue
        third_plus[cell] = terms_plus[cell][0] - terms_plus[cell - 1][0]
        third_minus[cell] = terms_minus[cell][0] - terms_minus[cell - 1][0]
        if cell < 4:
            continue
        at = cell - 2
        right = correction(
            terms_plus[at - 1][1], terms_plus[at][2], terms_plus[at + 1][3], third_plus[at], third_plus[at + 1]
        )
        left = correction(
            terms_minus[at + 2][3], terms_minus[at + 1][2], terms_minus[at][1],
            third_minus[at + 2], third_minus[at + 1],
        )
        interface[at] = (third_plus[at + 1] - third_minus[at + 1]) - 4.0 * (right - left)
        if at >= 3:
            store(at - 3, (centre[at - 1] - centre[at + 1]) + (interface[at - 1] - interface[at]))


def lane_index(shape):
    return lax.broadcasted_iota(jnp.int32, shape, len(shape) - 1)


def turned(value, by):
    size = value.shape[-1]
    if isinstance(by, int):
        by = by % size
        return value if by == 0 else pltpu.roll(value, by, value.ndim - 1)
    return pltpu.roll(value, lax.rem(by + 4 * size, size), value.ndim - 1)


def merged(pieces, slot):
    out = pieces[0]
    for number, piece in enumerate(pieces[1:], 1):
        out = jnp.where(slot == number, piece, out)
    return out


def rows_at(start, size):
    return pl.ds(start if isinstance(start, int) else pl.multiple_of(start, TILE), size)


def by_node(me, values):
    out = jnp.float32(values[0])
    for n, value in enumerate(values[1:], 1):
        out = jnp.where(me == n, jnp.float32(value), out)
    return out


def scaled_weight(row, column):
    return radau_weights[row][column] * (step_size / 12.0)


class Blocks:
    def __init__(self, comps, nx, ny, nz):
        self.comps, self.nx, self.ny, self.nz = comps, nx, ny, nz
        self.per = nz // ny
        self.left = nx - self.per
        assert nz % ny == 0 and ny % TILE == 0 and 2 * self.left == self.per
        self.half = nz // 2
        self.count = comps + (comps + 1) // 2
        self.step = CHUNK + 8

    def pair(self, b):
        first = 2 * (b - self.comps)
        return first, min(first + 1, self.comps - 1) if isinstance(b, int) else jnp.minimum(first + 1, self.comps - 1)

    def whole(self, ref, c):
        return ref[c, pl.ds(0, self.per)].reshape(self.nz, self.nz)

    def leftovers(self, ref, first, second):
        at = pl.ds(self.per, self.left)
        shape = (self.half, self.nz)
        return jnp.concatenate([ref[first, at].reshape(shape), ref[second, at].reshape(shape)], axis=0)

    def natural(self, ref, b):
        return self.whole(ref, b) if b < self.comps else self.leftovers(ref, *self.pair(b))

    def put_natural(self, ref, b, value):
        if b < self.comps:
            ref[b, pl.ds(0, self.per)] = value.reshape(self.per, self.ny, self.nz)
            return
        at = pl.ds(self.per, self.left)
        shape = (self.left, self.ny, self.nz)
        first, second = self.pair(b)
        ref[first, at] = value[: self.half].reshape(shape)
        if second != first:
            ref[second, at] = value[self.half :].reshape(shape)

    def row(self, c, i, t):
        if i < self.per:
            return c * self.nz + (i * self.ny + t)
        return (self.comps + c // 2) * self.nz + lax.rem(c, 2) * self.half + ((i - self.per) * self.ny + t)


def split_depth(blocks, read, alpha, write):
    comps = blocks.comps
    ((plus, minus),) = splits([read(c) for c in range(comps)], [None, None, alpha], (2,))
    for c in range(comps):
        write(c, plus[c], minus[c])
    shared = [read(b) for b in range(comps, blocks.count)]
    fields = [shared[c // 2] if c % 2 == 0 else turned(shared[c // 2], blocks.half) for c in range(comps)]
    ((plus, minus),) = splits(fields, [None, None, alpha], (2,))
    lower = lane_index(fields[0].shape) < blocks.half
    for b in range(comps, blocks.count):
        first, second = blocks.pair(b)
        write(b, *[jnp.where(lower, v[first], turned(v[second], blocks.half)) for v in (plus, minus)])


def write_edges(read, nx, ny, comps, lo_ref, hi_ref, side_ref):
    rows = side_ref.shape[1] // (2 * HALO)
    for c in range(comps):
        for i in range(HALO):
            lo_ref[0, pl.ds((c * HALO + i) * ny, ny), :] = read(c, i)
            hi_ref[0, pl.ds((c * HALO + i) * ny, ny), :] = read(c, nx - HALO + i)

    def side(i, carry):
        for c in range(comps):
            value = read(c, i)
            side_ref[0, pl.ds(c * nx + i, HALO, stride=rows), :] = value[ny - HALO :]
            side_ref[0, pl.ds(HALO * rows + c * nx + i, HALO, stride=rows), :] = value[:HALO]
        return carry

    lax.fori_loop(0, nx, side, 0)


def faster(best, read, first, count, comps):
    def step(i, best):
        speeds = signal_speeds([read(c, i) for c in range(comps)])
        return tuple(jnp.maximum(b, s) for b, s in zip(best, speeds))

    return lax.fori_loop(first, first + count, step, best)


def alpha_tile(best, group):
    nz = best[0].shape[-1]
    rows = [jnp.max(b, axis=0, keepdims=True) for b in best]
    tile = jnp.concatenate(rows + [jnp.zeros((TILE - 3, nz), jnp.float32)], axis=0)
    lane = lane_index(tile.shape)
    by = 1
    while by < group:
        other = jnp.where((lane & by) != 0, turned(tile, by), turned(tile, -by))
        tile = jnp.maximum(tile, other)
        by *= 2
    return tile


def open_kernel(u_hbm, u_ref, lo_ref, hi_ref, side_ref, al_ref, sems):
    comps, nx, ny, nz = u_ref.shape
    chunks = sems.shape[0]
    size = nx // chunks
    copies = []
    for n in range(chunks):
        at = pl.ds(n * size, size)
        copies.append(pltpu.make_async_copy(u_hbm.at[0, :, at], u_ref.at[:, at], sems.at[n]))
        copies[-1].start()

    def read(c, i):
        return u_ref[c, i]

    best = tuple(jnp.zeros((ny, nz), jnp.float32) for _ in range(3))
    for n in range(chunks):
        copies[n].wait()
        best = faster(best, read, n * size, size, comps)
    al_ref[...] = alpha_tile(best, nz)
    write_edges(read, nx, ny, comps, lo_ref, hi_ref, side_ref)


def turn_kernel(u_ref, rows_ref):
    blocks = Blocks(*u_ref.shape)
    nz = blocks.nz
    for b in range(blocks.count):
        value = blocks.natural(u_ref, b).T
        rows_ref[b, pl.ds(HALO, nz), :] = value
        rows_ref[b, pl.ds(0, HALO), :] = value[nz - HALO :]
        rows_ref[b, pl.ds(HALO + nz, HALO), :] = value[:HALO]


def start_kernel(init_ref, rows_ref, pack_ref, turned_ref, *, nodes):
    comps, nx, ny, nz = init_ref.shape
    blocks = Blocks(comps, nx, ny, nz)
    width = nz // nodes
    me = lax.axis_index("node")
    lanes = lane_index((ny, nz)) // width
    for b in range(blocks.count):
        send_quarter(blocks.natural(init_ref, b).T, turned_ref, b, [rows_ref], [me], width)

    def step(c, carry):
        for q in range(nx // nodes):
            pieces = [turned(init_ref[c, q * nodes + i], width * (i - me)) for i in range(nodes)]
            pack_ref[rows_at((c * (nx // nodes) + q) * ny, ny), :] = merged(pieces, lanes)
        return carry

    lax.fori_loop(0, comps, step, 0)


def send_quarter(value, ring_ref, b, parts, quarters, width):
    nz = value.shape[0]
    base = b * (nz + 2 * TILE)
    ring_ref[rows_at(base + TILE, nz), :] = value
    ring_ref[rows_at(base, TILE), :] = value[nz - TILE :]
    ring_ref[rows_at(base + TILE + nz, TILE), :] = value[:TILE]
    size = width + 8
    for part, quarter in zip(parts, quarters):
        part[rows_at(b * size, size), :] = ring_ref[pl.ds(base + (TILE - HALO) + quarter * width, size), :]


def blend_kernel(start_ref, *refs):
    nodes = len(refs) - 6
    parts, (rows_ref, nat_ref, lo_ref, hi_ref, side_ref, al_ref) = refs[:nodes], refs[nodes:]
    comps, nx, ny, nz = nat_ref.shape
    blocks = Blocks(comps, nx, ny, nz)
    width = nz // nodes
    size = width + 8
    me = lax.axis_index("node")
    weights = [
        [by_node(me, [scaled_weight(m, n ^ k) for n in range(nodes)]) for k in range(nodes)] for m in range(nodes)
    ]
    for b in range(blocks.count):
        at = pl.ds(b * size, size)
        start = start_ref[at, :]
        rates = [part[at, :] for part in parts]
        for m in range(nodes):
            value = start
            for k in range(nodes):
                value = value + weights[m][k] * rates[k]
            rows_ref[m, at, :] = value
        own = pl.ds(b * size + HALO, width)
        state = jnp.concatenate([rows_ref[m, own, :] for m in range(nodes)], axis=0)
        blocks.put_natural(nat_ref, b, state.T)

    def read(c, i):
        return nat_ref[c, i]

    best = tuple(jnp.zeros((ny, nz), jnp.float32) for _ in range(3))
    tile = alpha_tile(faster(best, read, 0, nx, comps), width)

    def spread(i, carry):
        al_ref[i] = tile
        return carry

    lax.fori_loop(0, al_ref.shape[0], spread, 0)
    write_edges(read, nx, ny, comps, lo_ref, hi_ref, side_ref)


def along_second(u, alphas, side_ref, dims, fy, yp, ym, gp, gm):
    comps, nx, ny, nz = dims
    rows = gp.shape[0] // (2 * HALO)
    every = range(comps)

    def own(i, carry):
        ((p, m),) = splits([u(c, i) for c in every], alphas, (1,))
        for c in every:
            at = rows_at((c * nx + i) * ny, ny)
            yp[at, :] = p[c]
            ym[at, :] = m[c]
        return carry

    lax.fori_loop(0, nx, own, 0, unroll=4)

    def ghost(i, carry):
        ((p, m),) = splits([side_ref[0, pl.ds(i * rows + c * nx, nx), :] for c in every], alphas, (1,))
        for c in every:
            gp[pl.ds(i * rows + c * nx, nx), :] = p[c]
            gm[pl.ds(i * rows + c * nx, nx), :] = m[c]
        return carry

    lax.fori_loop(0, 2 * HALO, ghost, 0, unroll=HALO)

    def along(b, carry):
        first = pl.multiple_of(b * TILE, TILE)

        def load(j):
            if HALO <= j < HALO + ny:
                at = pl.ds(first * ny + (j - HALO), TILE, stride=ny)
                return yp[at, :], ym[at, :]
            at = pl.ds((j if j < HALO else j - ny) * rows + first, TILE)
            return gp[at, :], gm[at, :]

        def store(i, value):
            fy[pl.ds(i * rows + first, TILE), :] = value

        stream(load, store, ny)
        return carry

    lax.fori_loop(0, rows // TILE, along, 0)


def along_last(blocks, zp, zm, fz, after):
    size = blocks.step * TILE

    def along(b, carry):
        def load(j):
            at = pl.ds(b * size + j, TILE, stride=blocks.step)
            return zp[at, :], zm[at, :]

        def store(i, value):
            fz[pl.ds(b * blocks.nz + i, TILE, stride=CHUNK), :] = value

        after(jnp.maximum(b - 1, 0))
        stream(load, store, CHUNK)
        return carry

    lax.fori_loop(0, blocks.count, along, 0)
    after(blocks.count - 1)


def along_first(u, alphas, lo_ref, hi_ref, fy, rate, xp, xm, extra, after):
    comps, nx, ny, nz = rate.shape
    rows = fy.shape[0] // ny
    every = range(comps)

    def split(fields, at):
        ((p, m),) = splits(fields, alphas, (0,))
        for c in every:
            xp[at, c * ny : (c + 1) * ny, :] = p[c]
            xm[at, c * ny : (c + 1) * ny, :] = m[c]

    def own(i, carry):
        split([u(c, i) for c in every], i + HALO)
        return carry

    lax.fori_loop(0, nx, own, 0, unroll=4)
    for ref, start in ((lo_ref, 0), (hi_ref, nx + HALO)):

        def ghost(i, carry, ref=ref, start=start):
            split([ref[0, rows_at((c * HALO + i) * ny, ny), :] for c in every], start + i)
            return carry

        lax.fori_loop(0, HALO, ghost, 0, unroll=HALO)

    def along(c, carry):
        after(jnp.maximum(c - 1, 0))
        for t in range(0, ny, TILE):

            def load(j, t=t):
                at = rows_at(c * ny + t, TILE)
                return xp[j, at, :], xm[j, at, :]

            def store(i, value, t=t):
                value = value + fy[pl.ds(t * rows + c * nx + i, TILE, stride=rows), :]
                rate[c, i, pl.ds(t, TILE), :] = value if extra is None else value + extra(c, i, t)

            stream(load, store, nx)
        return carry

    lax.fori_loop(0, comps, along, 0)
    after(jnp.int32(comps - 1))


def tile_rows(tile):
    return [tile[k : k + 1, :] for k in range(3)]


def first_lanes_kernel(u_ref, rows_ref, side_ref, al_ref, other_ref, fz, fy, al_out, zp, zm, yp, ym, gp, gm):
    dims = u_ref.shape
    blocks = Blocks(*dims)
    tile = jnp.maximum(al_ref[...], other_ref[...])
    al_out[...] = tile
    alphas = tile_rows(tile)
    along_second(lambda c, i: u_ref[c, i], alphas, side_ref, dims, fy, yp, ym, gp, gm)

    def depth(n, carry):
        at = rows_at(n * CHUNK, blocks.step)

        def write(b, plus, minus):
            to = rows_at((b * TILE + n) * blocks.step, blocks.step)
            zp[to, :] = plus
            zm[to, :] = minus

        split_depth(blocks, lambda b: rows_ref[b, at, :], alphas[2], write)
        return carry

    lax.fori_loop(0, TILE, depth, 0, unroll=4)
    along_last(blocks, zp, zm, fz, lambda b: None)


def first_rows_kernel(u_ref, lo_ref, hi_ref, al_ref, fz, fy, *refs):
    parts, (rate, xp, xm, ring) = refs[:-4], refs[-4:]
    nodes = len(parts)
    blocks = Blocks(*u_ref.shape)
    nz = blocks.nz
    me = lax.axis_index("node")
    quarters = [me ^ k for k in range(nodes)]

    def send(value, b):
        value = value.T + fz[rows_at(b * nz, nz), :]
        send_quarter(value, ring, b, parts, quarters, nz // nodes)

    def after(c):
        send(blocks.whole(rate, c), c)
        b = blocks.comps + c // 2
        send(blocks.leftovers(rate, *blocks.pair(b)), b)

    along_first(lambda c, i: u_ref[c, i], tile_rows(al_ref), lo_ref, hi_ref, fy, rate, xp, xm, None, after)


def second_lanes_kernel(nat_ref, rows_ref, side_ref, al_ref, fz, fy, al_out, zp, zm, yp, ym, gp, gm, back):
    nodes = rows_ref.shape[0]
    dims = nat_ref.shape
    blocks = Blocks(*dims)
    nz = blocks.nz
    width = nz // nodes
    tiles = al_ref.shape[0]
    tile = lax.fori_loop(
        1, tiles, lambda i, best: jnp.maximum(best, al_ref[i]), al_ref[0], unroll=True if tiles <= 32 else 1
    )
    al_out[...] = tile
    alphas = tile_rows(tile)
    along_second(lambda c, i: nat_ref[c, i], alphas, side_ref, dims, fy, yp, ym, gp, gm)
    group = lane_index((1, nz)) // width
    each = width // CHUNK
    for m in range(nodes):
        alpha = jnp.max(jnp.where(group == m, alphas[2], 0.0))

        def depth(n, carry, m=m, alpha=alpha):
            def read(b):
                return rows_ref[m, rows_at(b * (width + 8) + n * CHUNK, blocks.step), :]

            def write(b, plus, minus):
                to = rows_at((b * TILE + m * each + n) * blocks.step, blocks.step)
                zp[to, :] = plus
                zm[to, :] = minus

            split_depth(blocks, read, alpha, write)
            return carry

        lax.fori_loop(0, each, depth, 0, unroll=True)

    def after(b):
        at = rows_at(b * nz, nz)
        fz[at, :] = back[at, :].T

    along_last(blocks, zp, zm, back, after)


def second_rows_kernel(nat_ref, lo_ref, hi_ref, al_ref, fz, fy, pack_ref, *refs):
    outs, (rate, xp, xm) = refs[:-3], refs[-3:]
    nodes = len(outs)
    comps, nx, ny, nz = nat_ref.shape
    blocks = Blocks(comps, nx, ny, nz)
    width = nz // nodes
    me = lax.axis_index("node")
    weights = [
        [by_node(me, [scaled_weight(n ^ k, j) for n in range(nodes)]) for j in range(nodes)] for k in range(nodes)
    ]
    lanes = lane_index((TILE, nz)) // width

    def extra(c, i, t):
        return fz[rows_at(blocks.row(c, i, t), TILE), :]

    def after(c):
        for t in range(0, ny, TILE):
            for q in range(nx // nodes):
                at = rows_at((c * (nx // nodes) + q) * ny + t, TILE)
                start = pack_ref[at, :]
                rows = [rate[c, q * nodes + i, pl.ds(t, TILE), :] for i in range(nodes)]
                rates = [
                    merged([turned(rows[i], width * (i - j)) for i in range(nodes)], lanes) for j in range(nodes)
                ]
                for k in range(nodes):
                    value = start
                    for j in range(nodes):
                        value = value + weights[k][j] * rates[j]
                    outs[k][at, :] = turned(value, width * me)

    along_first(lambda c, i: nat_ref[c, i], tile_rows(al_ref), lo_ref, hi_ref, fy, rate, xp, xm, extra, after)


def close_kernel(*refs):
    parts, (out_hbm, out_ref, sems) = refs[:-3], refs[-3:]
    nodes = len(parts)
    comps, nx, ny, nz = out_ref.shape
    width = nz // nodes
    me = lax.axis_index("node")
    lanes = lane_index((ny, nz)) // width
    copies = []
    for c in range(comps):
        for q in range(nx // nodes):
            at = pl.ds((c * (nx // nodes) + q) * ny, ny)
            values = [part[at, :] for part in parts]
            for i in range(nodes):
                out = values[0]
                for k in range(1, nodes):
                    out = jnp.where(lanes == lax.rem((me ^ k) + i, nodes), values[k], out)
                out_ref[c, q * nodes + i] = turned(out, -width * i)
        copies.append(pltpu.make_async_copy(out_ref.at[c], out_hbm.at[0, c], sems.at[c]))
        copies[-1].start()
    for copy in copies:
        copy.wait()


def call(kernel, name, outs, operands, scratch=(), flops=1_000_000, anywhere=False, outside=False):
    vmem, hbm = pl.BlockSpec(memory_space=pltpu.VMEM), pl.BlockSpec(memory_space=pltpu.HBM)
    moved = sum(4 * x.size for x in operands)
    scratch = [pltpu.VMEM(x, jnp.float32) if isinstance(x, tuple) else x for x in scratch]
    return pl.pallas_call(
        kernel,
        out_shape=[jax.ShapeDtypeStruct(shape, jnp.float32) for shape in outs],
        in_specs=[hbm if anywhere else vmem] * len(operands),
        out_specs=[hbm if outside else vmem] * len(outs),
        scratch_shapes=scratch,
        compiler_params=pltpu.CompilerParams(vmem_limit_bytes=32 * 1024 * 1024),
        cost_estimate=pl.CostEstimate(flops=flops, bytes_accessed=2 * moved, transcendentals=0),
        name=name,
    )(*operands)


def shifted(value, axis, by):
    count = lax.axis_size(axis)
    return lax.ppermute(value, axis, [(i, (i + by) % count) for i in range(count)])


def swapped(value, by):
    return lax.ppermute(value, "node", [(i, i ^ by) for i in range(lax.axis_size("node"))])


def neighbours(lo, hi, side):
    lower, upper = shifted(hi, "gx", 1), shifted(lo, "gx", -1)
    if lax.axis_size("gy") == 2:
        return lower, upper, shifted(side, "gy", 1)
    half = side.shape[1] // 2
    side = jnp.concatenate([shifted(side[:, :half], "gy", 1), shifted(side[:, half:], "gy", -1)], axis=1)
    return lower, upper, side


def largest(tile):
    if lax.axis_size("gx") > 4 or lax.axis_size("gy") > 2:
        tile = lax.pmax(tile, ("gx", "gy"))
        return tile, tile
    others = [shifted(tile, "gx", by) for by in range(1, lax.axis_size("gx"))]
    tile = functools.reduce(jnp.maximum, others, tile)
    return tile, shifted(tile, "gy", 1)


def exchanged(parts):
    moved = {k: swapped(parts[k], k) for k in sorted(range(1, len(parts)), reverse=True)}
    return [parts[0]] + [moved[k] for k in range(1, len(parts))]


def local(initial, guesses):
    comps, nx, ny, nz = initial.shape
    nodes = lax.axis_size("node")
    devices = nodes * lax.axis_size("gx") * lax.axis_size("gy")
    rows = -(-comps * nx // TILE) * TILE
    blocks = Blocks(comps, nx, ny, nz)
    width = nz // nodes
    assert nz == CHUNK * TILE and width % CHUNK == 0 and nx % nodes == 0
    edge = (1, comps * HALO * ny, nz)
    edges = [edge, edge, (1, 2 * HALO * rows, nz)]
    tile_shape = (TILE, nz)
    part = (blocks.count * (width + 8), nz)
    pack = (comps * nx // nodes * ny, nz)
    across_shape = (ny * rows, nz)
    depth_shape = (blocks.count * nz, nz)
    padded = [(blocks.count * TILE * blocks.step, nz)] * 2 + [(ny * rows, nz)] * 2 + [(2 * HALO * rows, nz)] * 2
    slabs = [initial.shape] + [(nx + 2 * HALO, comps * ny, nz)] * 2
    ring = (blocks.count * (nz + 2 * TILE), nz)
    chunks = 4 if nx % 4 == 0 else 1

    field, lo, hi, side, tile = call(
        open_kernel,
        "open_kernel",
        [initial.shape] + edges + [tile_shape],
        [guesses],
        [pltpu.SemaphoreType.DMA((chunks,))],
        anywhere=True,
    )
    lower, upper, side = neighbours(lo, hi, side)
    tile, other = largest(tile)
    (turned_field,) = call(turn_kernel, "turn_kernel", [(blocks.count, nz + 8, nz)], [field])
    start, start_pack = call(
        functools.partial(start_kernel, nodes=nodes), "start_kernel", [part, pack], [initial], [ring]
    )
    depth, across, tile = call(
        first_lanes_kernel,
        "first_lanes_kernel",
        [depth_shape, across_shape, tile_shape],
        [field, turned_field, side, tile, other],
        padded,
        20_000_000,
    )
    parts = call(
        first_rows_kernel,
        "first_rows_kernel",
        [part] * nodes,
        [field, lower, upper, tile, depth, across],
        slabs + [ring],
        10_000_000,
    )
    turned_field, field, lo, hi, side, tile = call(
        blend_kernel,
        "blend_kernel",
        [(nodes,) + part, initial.shape] + edges + [(devices,) + tile_shape],
        [start] + exchanged(parts),
    )
    lower, upper, side = neighbours(lo, hi, side)
    tiles = lax.all_to_all(tile, ("node", "gx", "gy"), 0, 0)
    depth, across, tile = call(
        second_lanes_kernel,
        "second_lanes_kernel",
        [depth_shape, across_shape, tile_shape],
        [field, turned_field, side, tiles],
        padded + [depth_shape],
        20_000_000,
    )
    outs = call(
        second_rows_kernel,
        "second_rows_kernel",
        [pack] * nodes,
        [field, lower, upper, tile, depth, across, start_pack],
        slabs,
        10_000_000,
    )
    (states,) = call(
        close_kernel,
        "close_kernel",
        [(1,) + initial.shape],
        exchanged(outs),
        [initial.shape, pltpu.SemaphoreType.DMA((comps,))],
        outside=True,
    )
    return states


def solution(mesh):
    return jax.shard_map(
        local,
        mesh=mesh,
        in_specs=(P(None, "gx", "gy", None), P("node", None, "gx", "gy", None)),
        out_specs=P("node", None, "gx", "gy", None),
        check_vma=False,
    )
```

```python
import functools

import jax
import jax.numpy as jnp
from jax import lax
from jax.experimental import pallas as pl
from jax.experimental.pallas import tpu as pltpu
from jax.sharding import PartitionSpec as P

SWEEPS = 2
HALO = 3
COMPONENTS = 5
TILE = 8
CHUNK = 16

heat_ratio = 1.4
step_size = 0.025
density_floor = 0.5
pressure_floor = 0.25
epsilon = 1e-06
radau_weights = [
    [0.112999479323156, -0.040309220723522, 0.025802377420336, -0.009904676507266],
    [0.2343839957474, 0.206892573935359, -0.047857128048541, 0.016047422806516],
    [0.21668178462325, 0.406123263867373, 0.189036518170056, -0.024182104899833],
    [0.220462211176768, 0.388193468843172, 0.32884431998006, 0.0625],
]


def reciprocal(value):
    return pl.reciprocal(value, approx=True)


def primitives(fields):
    inverse = 1.0 / jnp.maximum(fields[0], density_floor)
    velocity = [fields[k] * inverse for k in (1, 2, 3)]
    energy = fields[1] * velocity[0] + fields[2] * velocity[1] + fields[3] * velocity[2]
    pressure = jnp.maximum(0.4 * (fields[4] - 0.5 * energy), pressure_floor)
    return inverse, velocity, pressure


def signal_speeds(fields):
    inverse, velocity, pressure = primitives(fields)
    sound = jnp.sqrt(heat_ratio * pressure * inverse)
    return [jnp.abs(v) + sound for v in velocity]


def half_fluxes(half, speed, half_pressure, direction):
    flux = [half[direction + 1]] + [half[k] * speed for k in (1, 2, 3)]
    flux.append((half[4] + half_pressure) * speed)
    flux[direction + 1] = flux[direction + 1] + half_pressure
    return flux


def splits(fields, alphas, directions=(0, 1, 2)):
    _, velocity, pressure = primitives(fields)
    half = [0.5 * field for field in fields]
    half_pressure = 0.5 * pressure
    out = []
    for direction in directions:
        flux = half_fluxes(half, velocity[direction], half_pressure, direction)
        signal = [alphas[direction] * value for value in half]
        out.append(
            ([f + s for f, s in zip(flux, signal)], [f - s for f, s in zip(flux, signal)])
        )
    return out


def cell_terms(below, above):
    second = above - below
    both = below + above
    square = second * second
    middle = 0.25 * (both * both) + ((13.0 / 12.0) * square + epsilon)
    outer = middle + square
    cross = both * second
    return second, outer + cross, middle, outer - cross


def correction(first, middle, last, third_first, third_last):
    ratio_first = middle * reciprocal(first)
    ratio_last = middle * reciprocal(last)
    weight_first = ratio_first * ratio_first
    weight_last = 1.5 * (ratio_last * ratio_last)
    total = (6.0 + weight_first) + (weight_last + weight_last)
    return (weight_first * third_first + weight_last * third_last) * reciprocal(total)


def stream(load, store, count):
    plus, minus, centre = {}, {}, {}
    terms_plus, terms_minus, third_plus, third_minus, interface = {}, {}, {}, {}, {}
    differences_plus, differences_minus = {}, {}
    plus[0], minus[0] = load(0)
    for j in range(1, count + 2 * HALO):
        plus[j], minus[j] = load(j)
        differences_plus[j] = plus[j] - plus[j - 1]
        differences_minus[j] = minus[j] - minus[j - 1]
        cell = j - 1
        if cell < 1:
            continue
        terms_plus[cell] = cell_terms(differences_plus[cell], differences_plus[j])
        terms_minus[cell] = cell_terms(differences_minus[cell], differences_minus[j])
        if 2 <= cell <= count + 3:
            centre[cell] = 6.0 * (plus[cell] + minus[cell]) - (
                terms_plus[cell][0] + terms_minus[cell][0]
            )
        if cell < 2:
            continue
        third_plus[cell] = terms_plus[cell][0] - terms_plus[cell - 1][0]
        third_minus[cell] = terms_minus[cell][0] - terms_minus[cell - 1][0]
        if cell < 4:
            continue
        at = cell - 2
        right = correction(
            terms_plus[at - 1][1], terms_plus[at][2], terms_plus[at + 1][3], third_plus[at], third_plus[at + 1]
        )
        left = correction(
            terms_minus[at + 2][3], terms_minus[at + 1][2], terms_minus[at][1],
            third_minus[at + 2], third_minus[at + 1],
        )
        interface[at] = (third_plus[at + 1] - third_minus[at + 1]) - 4.0 * (right - left)
        if at >= 3:
            store(at - 3, (centre[at - 1] - centre[at + 1]) + (interface[at - 1] - interface[at]))


def lane_index(shape):
    return lax.broadcasted_iota(jnp.int32, shape, len(shape) - 1)


def turned(value, by):
    size = value.shape[-1]
    if isinstance(by, int):
        by = by % size
        return value if by == 0 else pltpu.roll(value, by, value.ndim - 1)
    return pltpu.roll(value, lax.rem(by + 4 * size, size), value.ndim - 1)


def merged(pieces, slot):
    out = pieces[0]
    for number, piece in enumerate(pieces[1:], 1):
        out = jnp.where(slot == number, piece, out)
    return out


def rows_at(start, size):
    return pl.ds(start if isinstance(start, int) else pl.multiple_of(start, TILE), size)


def by_node(me, values):
    out = jnp.float32(values[0])
    for n, value in enumerate(values[1:], 1):
        out = jnp.where(me == n, jnp.float32(value), out)
    return out


def scaled_weight(row, column):
    return radau_weights[row][column] * (step_size / 12.0)


class Blocks:
    def __init__(self, comps, nx, ny, nz):
        self.comps, self.nx, self.ny, self.nz = comps, nx, ny, nz
        self.per = nz // ny
        self.left = nx - self.per
        assert nz % ny == 0 and ny % TILE == 0 and 2 * self.left == self.per
        self.half = nz // 2
        self.count = comps + (comps + 1) // 2
        self.step = CHUNK + 8

    def pair(self, b):
        first = 2 * (b - self.comps)
        return first, min(first + 1, self.comps - 1) if isinstance(b, int) else jnp.minimum(first + 1, self.comps - 1)

    def whole(self, ref, c):
        return ref[c, pl.ds(0, self.per)].reshape(self.nz, self.nz)

    def leftovers(self, ref, first, second):
        at = pl.ds(self.per, self.left)
        shape = (self.half, self.nz)
        return jnp.concatenate([ref[first, at].reshape(shape), ref[second, at].reshape(shape)], axis=0)

    def natural(self, ref, b):
        return self.whole(ref, b) if b < self.comps else self.leftovers(ref, *self.pair(b))

    def put_whole(self, ref, c, value):
        ref[c, pl.ds(0, self.per)] = value.reshape(self.per, self.ny, self.nz)

    def put_leftovers(self, ref, b, value):
        at = pl.ds(self.per, self.left)
        shape = (self.left, self.ny, self.nz)
        first, second = self.pair(b)
        ref[second, at] = value[self.half :].reshape(shape)
        ref[first, at] = value[: self.half].reshape(shape)

    def put_natural(self, ref, b, value):
        if b < self.comps:
            self.put_whole(ref, b, value)
        else:
            self.put_leftovers(ref, b, value)

    def row(self, c, i, t):
        if i < self.per:
            return c * self.nz + (i * self.ny + t)
        return (self.comps + c // 2) * self.nz + lax.rem(c, 2) * self.half + ((i - self.per) * self.ny + t)


def split_depth(blocks, read, alpha, write):
    comps = blocks.comps
    ((plus, minus),) = splits([read(c) for c in range(comps)], [None, None, alpha], (2,))
    for c in range(comps):
        write(c, plus[c], minus[c])
    shared = [read(b) for b in range(comps, blocks.count)]
    fields = [shared[c // 2] if c % 2 == 0 else turned(shared[c // 2], blocks.half) for c in range(comps)]
    ((plus, minus),) = splits(fields, [None, None, alpha], (2,))
    lower = lane_index(fields[0].shape) < blocks.half
    for b in range(comps, blocks.count):
        first, second = blocks.pair(b)
        write(b, *[jnp.where(lower, v[first], turned(v[second], blocks.half)) for v in (plus, minus)])


def write_edges(read, nx, ny, comps, lo_ref, hi_ref, side_ref):
    rows = side_ref.shape[1] // (2 * HALO)
    for c in range(comps):
        for i in range(HALO):
            lo_ref[0, pl.ds((c * HALO + i) * ny, ny), :] = read(c, i)
            hi_ref[0, pl.ds((c * HALO + i) * ny, ny), :] = read(c, nx - HALO + i)

    def side(i, carry):
        for c in range(comps):
            value = read(c, i)
            side_ref[0, pl.ds(c * nx + i, HALO, stride=rows), :] = value[ny - HALO :]
            side_ref[0, pl.ds(HALO * rows + c * nx + i, HALO, stride=rows), :] = value[:HALO]
        return carry

    lax.fori_loop(0, nx, side, 0)


def faster(best, read, first, count, comps):
    def step(i, best):
        speeds = signal_speeds([read(c, i) for c in range(comps)])
        return tuple(jnp.maximum(b, s) for b, s in zip(best, speeds))

    return lax.fori_loop(first, first + count, step, best)


def alpha_tile(best, group):
    nz = best[0].shape[-1]
    rows = [jnp.max(b, axis=0, keepdims=True) for b in best]
    tile = jnp.concatenate(rows + [jnp.zeros((TILE - 3, nz), jnp.float32)], axis=0)
    lane = lane_index(tile.shape)
    by = 1
    while by < group:
        other = jnp.where((lane & by) != 0, turned(tile, by), turned(tile, -by))
        tile = jnp.maximum(tile, other)
        by *= 2
    return tile


def spread(tile, al_ref):
    def step(i, carry):
        al_ref[i] = tile
        return carry

    lax.fori_loop(0, al_ref.shape[0], step, 0)


def open_kernel(u_hbm, *refs):
    parts, (al_ref, u_ref, ring, sems) = refs[:-4], refs[-4:]
    nodes = len(parts)
    comps, nx, ny, nz = u_ref.shape
    blocks = Blocks(comps, nx, ny, nz)
    width = nz // nodes
    me = lax.axis_index("node")
    chunks = sems.shape[0]
    size = nx // chunks
    copies = []
    for n in range(chunks):
        at = pl.ds(n * size, size)
        copies.append(pltpu.make_async_copy(u_hbm.at[0, :, at], u_ref.at[:, at], sems.at[n]))
        copies[-1].start()

    def read(c, i):
        return u_ref[c, i]

    best = tuple(jnp.zeros((ny, nz), jnp.float32) for _ in range(3))
    for n in range(chunks):
        copies[n].wait()
        best = faster(best, read, n * size, size, comps)
    tile = alpha_tile(best, nz)
    spread(jnp.where(lane_index(tile.shape) // width == me, tile, 0.0), al_ref)
    quarters = [me ^ k for k in range(nodes)]
    for b in range(blocks.count):
        send_quarter(blocks.natural(u_ref, b).T, ring, b, parts, quarters, width)


def send_quarter(value, ring_ref, b, parts, quarters, width):
    nz = value.shape[0]
    base = b * (nz + 2 * TILE)
    ring_ref[rows_at(base + TILE, nz), :] = value
    ring_ref[rows_at(base, TILE), :] = value[nz - TILE :]
    ring_ref[rows_at(base + TILE + nz, TILE), :] = value[:TILE]
    size = width + 8
    for part, quarter in zip(parts, quarters):
        part[rows_at(b * size, size), :] = ring_ref[pl.ds(base + (TILE - HALO) + quarter * width, size), :]


def start_kernel(init_ref, rows_ref, pack_ref, turned_ref, *, nodes):
    comps, nx, ny, nz = init_ref.shape
    blocks = Blocks(comps, nx, ny, nz)
    width = nz // nodes
    me = lax.axis_index("node")
    lanes = lane_index((ny, nz)) // width
    for b in range(blocks.count):
        turned_ref[rows_at(b * nz, nz), :] = blocks.natural(init_ref, b).T
        rows_ref[rows_at(b * width, width), :] = turned_ref[rows_at(b * nz + me * width, width), :]

    def step(c, carry):
        for q in range(nx // nodes):
            pieces = [turned(init_ref[c, q * nodes + i], width * (i - me)) for i in range(nodes)]
            pack_ref[rows_at((c * (nx // nodes) + q) * ny, ny), :] = merged(pieces, lanes)
        return carry

    lax.fori_loop(0, comps, step, 0)


def gather_kernel(*refs):
    parts, (rows_ref, nat_ref, lo_ref, hi_ref, side_ref) = refs[:-5], refs[-5:]
    nodes = len(parts)
    comps, nx, ny, nz = nat_ref.shape
    blocks = Blocks(comps, nx, ny, nz)
    width = nz // nodes
    size = width + 8
    me = lax.axis_index("node")
    for k in range(nodes):
        rows_ref[me ^ k] = parts[k][...]
    for b in range(blocks.count):
        own = pl.ds(b * size + HALO, width)
        state = jnp.concatenate([rows_ref[m, own, :] for m in range(nodes)], axis=0)
        blocks.put_natural(nat_ref, b, state.T)
    write_edges(lambda c, i: nat_ref[c, i], nx, ny, comps, lo_ref, hi_ref, side_ref)


def along_second(u, alphas, side_ref, dims, fy, yp, ym, gp, gm):
    comps, nx, ny, nz = dims
    rows = gp.shape[0] // (2 * HALO)
    every = range(comps)

    def own(i, carry):
        ((p, m),) = splits([u(c, i) for c in every], alphas, (1,))
        for c in every:
            at = rows_at((c * nx + i) * ny, ny)
            yp[at, :] = p[c]
            ym[at, :] = m[c]
        return carry

    lax.fori_loop(0, nx, own, 0, unroll=4)

    def ghost(i, carry):
        ((p, m),) = splits([side_ref[0, pl.ds(i * rows + c * nx, nx), :] for c in every], alphas, (1,))
        for c in every:
            gp[pl.ds(i * rows + c * nx, nx), :] = p[c]
            gm[pl.ds(i * rows + c * nx, nx), :] = m[c]
        return carry

    lax.fori_loop(0, 2 * HALO, ghost, 0, unroll=HALO)

    def along(b, carry):
        first = pl.multiple_of(b * TILE, TILE)

        def load(j):
            if HALO <= j < HALO + ny:
                at = pl.ds(first * ny + (j - HALO), TILE, stride=ny)
                return yp[at, :], ym[at, :]
            at = pl.ds((j if j < HALO else j - ny) * rows + first, TILE)
            return gp[at, :], gm[at, :]

        def store(i, value):
            fy[pl.ds(i * rows + first, TILE), :] = value

        stream(load, store, ny)
        return carry

    lax.fori_loop(0, rows // TILE, along, 0)


def along_last(blocks, zp, zm, fz, after):
    size = blocks.step * TILE

    def along(b, carry):
        def load(j):
            at = pl.ds(b * size + j, TILE, stride=blocks.step)
            return zp[at, :], zm[at, :]

        def store(i, value):
            fz[pl.ds(b * blocks.nz + i, TILE, stride=CHUNK), :] = value

        after(jnp.maximum(b - 1, 0))
        stream(load, store, CHUNK)
        return carry

    lax.fori_loop(0, blocks.count, along, 0)
    after(blocks.count - 1)


def along_first(u, alphas, lo_ref, hi_ref, fy, rate, xp, xm, extra, after):
    comps, nx, ny, nz = rate.shape
    rows = fy.shape[0] // ny
    every = range(comps)

    def split(fields, at):
        ((p, m),) = splits(fields, alphas, (0,))
        for c in every:
            xp[at, c * ny : (c + 1) * ny, :] = p[c]
            xm[at, c * ny : (c + 1) * ny, :] = m[c]

    def own(i, carry):
        split([u(c, i) for c in every], i + HALO)
        return carry

    lax.fori_loop(0, nx, own, 0, unroll=4)
    for ref, start in ((lo_ref, 0), (hi_ref, nx + HALO)):

        def ghost(i, carry, ref=ref, start=start):
            split([ref[0, rows_at((c * HALO + i) * ny, ny), :] for c in every], start + i)
            return carry

        lax.fori_loop(0, HALO, ghost, 0, unroll=HALO)

    def along(c, carry):
        after(jnp.maximum(c - 1, 0))
        for t in range(0, ny, TILE):

            def load(j, t=t):
                at = rows_at(c * ny + t, TILE)
                return xp[j, at, :], xm[j, at, :]

            def store(i, value, t=t):
                value = value + fy[pl.ds(t * rows + c * nx + i, TILE, stride=rows), :]
                rate[c, i, pl.ds(t, TILE), :] = value if extra is None else value + extra(c, i, t)

            stream(load, store, nx)
        return carry

    lax.fori_loop(0, comps, along, 0)
    after(jnp.int32(comps - 1))


def tile_rows(tile):
    return [tile[k : k + 1, :] for k in range(3)]


def along_lanes(nat_ref, rows_ref, side_ref, al_ref, fz, fy, al_out, scratch, after):
    zp, zm, yp, ym, gp, gm = scratch
    nodes = rows_ref.shape[0]
    dims = nat_ref.shape
    blocks = Blocks(*dims)
    nz = blocks.nz
    width = nz // nodes
    tiles = al_ref.shape[0]
    tile = lax.fori_loop(
        1, tiles, lambda i, best: jnp.maximum(best, al_ref[i]), al_ref[0], unroll=True if tiles <= 32 else 1
    )
    al_out[...] = tile
    alphas = tile_rows(tile)
    along_second(lambda c, i: nat_ref[c, i], alphas, side_ref, dims, fy, yp, ym, gp, gm)
    group = lane_index((1, nz)) // width
    each = width // CHUNK
    for m in range(nodes):
        alpha = jnp.max(jnp.where(group == m, alphas[2], 0.0))

        def depth(n, carry, m=m, alpha=alpha):
            def read(b):
                return rows_ref[m, rows_at(b * (width + 8) + n * CHUNK, blocks.step), :]

            def write(b, plus, minus):
                to = rows_at((b * TILE + m * each + n) * blocks.step, blocks.step)
                zp[to, :] = plus
                zm[to, :] = minus

            split_depth(blocks, read, alpha, write)
            return carry

        lax.fori_loop(0, each, depth, 0, unroll=True)
    along_last(blocks, zp, zm, fz, after)


def first_lanes_kernel(nat_ref, rows_ref, side_ref, al_ref, fz, fy, al_out, *scratch):
    along_lanes(nat_ref, rows_ref, side_ref, al_ref, fz, fy, al_out, scratch, lambda b: None)


def second_lanes_kernel(
    nat_ref, own_ref, before_ref, behind_ref, side_ref, al_ref, fz, fy, al_out, back, rows_ref, *scratch
):
    nodes = own_ref.shape[0]
    blocks = Blocks(*nat_ref.shape)
    nz = blocks.nz
    width = nz // nodes
    size = width + 8
    for m in range(nodes):
        rows_ref[m] = own_ref[m]
        for b in range(blocks.count):
            ghost = pl.ds((m * blocks.count + b) * 4, HALO)
            rows_ref[m, pl.ds(b * size, HALO), :] = before_ref[ghost, :]
            rows_ref[m, pl.ds(b * size + HALO + width, HALO), :] = behind_ref[ghost, :]

    def after(b):
        at = rows_at(b * nz, nz)
        fz[at, :] = back[at, :].T

    along_lanes(nat_ref, rows_ref, side_ref, al_ref, back, fy, al_out, scratch, after)


def first_rows_kernel(nat_in, lo_in, hi_in, al_in, fz, fy, start_ref, *refs):
    rows_ref, nat_ref, lo_ref, hi_ref, side_ref, first_ref, last_ref, al_ref, rate, xp, xm = refs
    nodes = rows_ref.shape[0]
    comps, nx, ny, nz = nat_ref.shape
    blocks = Blocks(comps, nx, ny, nz)
    width = nz // nodes
    size = width + 8

    def state(value, b):
        rates = value.T + fz[rows_at(b * nz, nz), :]
        start = start_ref[rows_at(b * width, width), :]
        states = []
        for m in range(nodes):
            new = start
            for n in range(nodes):
                new = new + scaled_weight(m, n) * rates[n * width : (n + 1) * width]
            rows_ref[m, pl.ds(b * size + HALO, width), :] = new
            ghost = pl.ds((m * blocks.count + b) * 4, HALO)
            first_ref[ghost, :] = new[:HALO]
            last_ref[ghost, :] = new[width - HALO :]
            states.append(new)
        return jnp.concatenate(states, axis=0).T

    def after(c):
        blocks.put_whole(nat_ref, c, state(blocks.whole(rate, c), c))
        b = blocks.comps + c // 2
        blocks.put_leftovers(nat_ref, b, state(blocks.leftovers(rate, *blocks.pair(b)), b))

    along_first(lambda c, i: nat_in[c, i], tile_rows(al_in), lo_in, hi_in, fy, rate, xp, xm, None, after)

    def read(c, i):
        return nat_ref[c, i]

    best = tuple(jnp.zeros((ny, nz), jnp.float32) for _ in range(3))
    spread(alpha_tile(faster(best, read, 0, nx, comps), width), al_ref)
    write_edges(read, nx, ny, comps, lo_ref, hi_ref, side_ref)


def second_rows_kernel(nat_ref, lo_ref, hi_ref, al_ref, fz, fy, pack_ref, *refs):
    outs, (rate, xp, xm) = refs[:-3], refs[-3:]
    nodes = len(outs)
    comps, nx, ny, nz = nat_ref.shape
    blocks = Blocks(comps, nx, ny, nz)
    width = nz // nodes
    me = lax.axis_index("node")
    weights = [
        [by_node(me, [scaled_weight(n ^ k, j) for n in range(nodes)]) for j in range(nodes)] for k in range(nodes)
    ]
    lanes = lane_index((TILE, nz)) // width

    def extra(c, i, t):
        return fz[rows_at(blocks.row(c, i, t), TILE), :]

    def after(c):
        for t in range(0, ny, TILE):
            for q in range(nx // nodes):
                at = rows_at((c * (nx // nodes) + q) * ny + t, TILE)
                start = pack_ref[at, :]
                rows = [rate[c, q * nodes + i, pl.ds(t, TILE), :] for i in range(nodes)]
                rates = [
                    merged([turned(rows[i], width * (i - j)) for i in range(nodes)], lanes) for j in range(nodes)
                ]
                for k in range(nodes):
                    value = start
                    for j in range(nodes):
                        value = value + weights[k][j] * rates[j]
                    outs[k][at, :] = turned(value, width * me)

    along_first(lambda c, i: nat_ref[c, i], tile_rows(al_ref), lo_ref, hi_ref, fy, rate, xp, xm, extra, after)


def close_kernel(*refs):
    parts, (out_hbm, out_ref, sems) = refs[:-3], refs[-3:]
    nodes = len(parts)
    comps, nx, ny, nz = out_ref.shape
    width = nz // nodes
    me = lax.axis_index("node")
    lanes = lane_index((ny, nz)) // width
    copies = []
    for c in range(comps):
        for q in range(nx // nodes):
            at = pl.ds((c * (nx // nodes) + q) * ny, ny)
            values = [part[at, :] for part in parts]
            for i in range(nodes):
                out = values[0]
                for k in range(1, nodes):
                    out = jnp.where(lanes == lax.rem((me ^ k) + i, nodes), values[k], out)
                out_ref[c, q * nodes + i] = turned(out, -width * i)
        copies.append(pltpu.make_async_copy(out_ref.at[c], out_hbm.at[0, c], sems.at[c]))
        copies[-1].start()
    for copy in copies:
        copy.wait()


def call(kernel, name, outs, operands, scratch=(), flops=1_000_000, anywhere=False, outside=False):
    vmem, hbm = pl.BlockSpec(memory_space=pltpu.VMEM), pl.BlockSpec(memory_space=pltpu.HBM)
    moved = sum(4 * x.size for x in operands)
    scratch = [pltpu.VMEM(x, jnp.float32) if isinstance(x, tuple) else x for x in scratch]
    return pl.pallas_call(
        kernel,
        out_shape=[jax.ShapeDtypeStruct(shape, jnp.float32) for shape in outs],
        in_specs=[hbm if anywhere else vmem] * len(operands),
        out_specs=[hbm if outside else vmem] * len(outs),
        scratch_shapes=scratch,
        compiler_params=pltpu.CompilerParams(vmem_limit_bytes=32 * 1024 * 1024),
        cost_estimate=pl.CostEstimate(flops=flops, bytes_accessed=2 * moved, transcendentals=0),
        name=name,
    )(*operands)


def shifted(value, axis, by):
    count = lax.axis_size(axis)
    return lax.ppermute(value, axis, [(i, (i + by) % count) for i in range(count)])


def swapped(value, by):
    return lax.ppermute(value, "node", [(i, i ^ by) for i in range(lax.axis_size("node"))])


def neighbours(lo, hi, side):
    lower, upper = shifted(hi, "gx", 1), shifted(lo, "gx", -1)
    if lax.axis_size("gy") == 2:
        return lower, upper, shifted(side, "gy", 1)
    half = side.shape[1] // 2
    side = jnp.concatenate([shifted(side[:, :half], "gy", 1), shifted(side[:, half:], "gy", -1)], axis=1)
    return lower, upper, side


def exchanged(parts):
    moved = {k: swapped(parts[k], k) for k in sorted(range(1, len(parts)), reverse=True)}
    return [parts[0]] + [moved[k] for k in range(1, len(parts))]


def local(initial, guesses):
    comps, nx, ny, nz = initial.shape
    nodes = lax.axis_size("node")
    everyone = ("node", "gx", "gy")
    devices = nodes * lax.axis_size("gx") * lax.axis_size("gy")
    rows = -(-comps * nx // TILE) * TILE
    blocks = Blocks(comps, nx, ny, nz)
    width = nz // nodes
    assert nz == CHUNK * TILE and width % CHUNK == 0 and nx % nodes == 0
    edge = (1, comps * HALO * ny, nz)
    edges = [edge, edge, (1, 2 * HALO * rows, nz)]
    tile_shape = (TILE, nz)
    tiles_shape = (devices,) + tile_shape
    part = (blocks.count * (width + 8), nz)
    pack = (comps * nx // nodes * ny, nz)
    ghost = (nodes * blocks.count * 4, nz)
    depth_shape = (blocks.count * nz, nz)
    lanes_out = [depth_shape, (ny * rows, nz), tile_shape]
    lanes_scratch = [(blocks.count * TILE * blocks.step, nz)] * 2 + [(ny * rows, nz)] * 2 + [(2 * HALO * rows, nz)] * 2
    slabs = [initial.shape] + [(nx + 2 * HALO, comps * ny, nz)] * 2
    ring = (blocks.count * (nz + 2 * TILE), nz)
    chunks = 4 if nx % 4 == 0 else 1

    *parts, tile = call(
        open_kernel,
        "open_kernel",
        [part] * nodes + [tiles_shape],
        [guesses],
        [initial.shape, ring, pltpu.SemaphoreType.DMA((chunks,))],
        anywhere=True,
    )
    tiles = lax.all_to_all(tile, everyone, 0, 0)
    start, start_pack = call(
        functools.partial(start_kernel, nodes=nodes),
        "start_kernel",
        [(blocks.count * width, nz), pack],
        [initial],
        [depth_shape],
    )
    turned_field, field, lo, hi, side = call(
        gather_kernel, "gather_kernel", [(nodes,) + part, initial.shape] + edges, exchanged(parts)
    )
    lower, upper, side = neighbours(lo, hi, side)
    depth, across, tile = call(
        first_lanes_kernel,
        "first_lanes_kernel",
        lanes_out,
        [field, turned_field, side, tiles],
        lanes_scratch,
        20_000_000,
    )
    turned_field, field, lo, hi, side, first, last, tile = call(
        first_rows_kernel,
        "first_rows_kernel",
        [(nodes,) + part, initial.shape] + edges + [ghost, ghost, tiles_shape],
        [field, lower, upper, tile, depth, across, start],
        slabs,
        10_000_000,
    )
    tiles = lax.all_to_all(tile, everyone, 0, 0)
    lower, upper, side = neighbours(lo, hi, side)
    before, behind = shifted(last, "node", 1), shifted(first, "node", -1)
    depth, across, tile = call(
        second_lanes_kernel,
        "second_lanes_kernel",
        lanes_out,
        [field, turned_field, before, behind, side, tiles],
        [depth_shape, (nodes,) + part] + lanes_scratch,
        20_000_000,
    )
    outs = call(
        second_rows_kernel,
        "second_rows_kernel",
        [pack] * nodes,
        [field, lower, upper, tile, depth, across, start_pack],
        slabs,
        10_000_000,
    )
    (states,) = call(
        close_kernel,
        "close_kernel",
        [(1,) + initial.shape],
        exchanged(outs),
        [initial.shape, pltpu.SemaphoreType.DMA((comps,))],
        outside=True,
    )
    return states


def solution(mesh):
    return jax.shard_map(
        local,
        mesh=mesh,
        in_specs=(P(None, "gx", "gy", None), P("node", None, "gx", "gy", None)),
        out_specs=P("node", None, "gx", "gy", None),
        check_vma=False,
    )
```

```python
import functools

import jax
import jax.numpy as jnp
from jax import lax
from jax.experimental import pallas as pl
from jax.experimental.pallas import tpu as pltpu
from jax.sharding import PartitionSpec as P

SWEEPS = 2
HALO = 3
COMPONENTS = 5
TILE = 8
CHUNK = 16

heat_ratio = 1.4
step_size = 0.025
density_floor = 0.5
pressure_floor = 0.25
epsilon = 1e-06
radau_weights = [
    [0.112999479323156, -0.040309220723522, 0.025802377420336, -0.009904676507266],
    [0.2343839957474, 0.206892573935359, -0.047857128048541, 0.016047422806516],
    [0.21668178462325, 0.406123263867373, 0.189036518170056, -0.024182104899833],
    [0.220462211176768, 0.388193468843172, 0.32884431998006, 0.0625],
]


def reciprocal(value):
    return pl.reciprocal(value, approx=True)


def primitives(fields):
    inverse = 1.0 / jnp.maximum(fields[0], density_floor)
    velocity = [fields[k] * inverse for k in (1, 2, 3)]
    energy = fields[1] * velocity[0] + fields[2] * velocity[1] + fields[3] * velocity[2]
    pressure = jnp.maximum(0.4 * (fields[4] - 0.5 * energy), pressure_floor)
    return inverse, velocity, pressure


def signal_speeds(fields):
    inverse, velocity, pressure = primitives(fields)
    sound = jnp.sqrt(heat_ratio * pressure * inverse)
    return [jnp.abs(v) + sound for v in velocity]


def half_fluxes(half, speed, half_pressure, direction):
    flux = [half[direction + 1]] + [half[k] * speed for k in (1, 2, 3)]
    flux.append((half[4] + half_pressure) * speed)
    flux[direction + 1] = flux[direction + 1] + half_pressure
    return flux


def splits(fields, alphas, directions=(0, 1, 2)):
    _, velocity, pressure = primitives(fields)
    half = [0.5 * field for field in fields]
    half_pressure = 0.5 * pressure
    out = []
    for direction in directions:
        flux = half_fluxes(half, velocity[direction], half_pressure, direction)
        signal = [alphas[direction] * value for value in half]
        out.append(
            ([f + s for f, s in zip(flux, signal)], [f - s for f, s in zip(flux, signal)])
        )
    return out


def cell_terms(below, above):
    second = above - below
    both = below + above
    square = second * second
    middle = 0.25 * (both * both) + ((13.0 / 12.0) * square + epsilon)
    outer = middle + square
    cross = both * second
    return second, outer + cross, middle, outer - cross


def correction(first, middle, last, third_first, third_last):
    ratio_first = middle * reciprocal(first)
    ratio_last = middle * reciprocal(last)
    weight_first = ratio_first * ratio_first
    weight_last = 1.5 * (ratio_last * ratio_last)
    total = (6.0 + weight_first) + (weight_last + weight_last)
    return (weight_first * third_first + weight_last * third_last) * reciprocal(total)


def stream(load, store, count):
    plus, minus, centre = {}, {}, {}
    terms_plus, terms_minus, third_plus, third_minus, interface = {}, {}, {}, {}, {}
    differences_plus, differences_minus = {}, {}
    plus[0], minus[0] = load(0)
    for j in range(1, count + 2 * HALO):
        plus[j], minus[j] = load(j)
        differences_plus[j] = plus[j] - plus[j - 1]
        differences_minus[j] = minus[j] - minus[j - 1]
        cell = j - 1
        if cell < 1:
            continue
        terms_plus[cell] = cell_terms(differences_plus[cell], differences_plus[j])
        terms_minus[cell] = cell_terms(differences_minus[cell], differences_minus[j])
        if 2 <= cell <= count + 3:
            centre[cell] = 6.0 * (plus[cell] + minus[cell]) - (
                terms_plus[cell][0] + terms_minus[cell][0]
            )
        if cell < 2:
            continue
        third_plus[cell] = terms_plus[cell][0] - terms_plus[cell - 1][0]
        third_minus[cell] = terms_minus[cell][0] - terms_minus[cell - 1][0]
        if cell < 4:
            continue
        at = cell - 2
        right = correction(
            terms_plus[at - 1][1], terms_plus[at][2], terms_plus[at + 1][3], third_plus[at], third_plus[at + 1]
        )
        left = correction(
            terms_minus[at + 2][3], terms_minus[at + 1][2], terms_minus[at][1],
            third_minus[at + 2], third_minus[at + 1],
        )
        interface[at] = (third_plus[at + 1] - third_minus[at + 1]) - 4.0 * (right - left)
        if at >= 3:
            store(at - 3, (centre[at - 1] - centre[at + 1]) + (interface[at - 1] - interface[at]))


def lane_index(shape):
    return lax.broadcasted_iota(jnp.int32, shape, len(shape) - 1)


def turned(value, by):
    size = value.shape[-1]
    if isinstance(by, int):
        by = by % size
        return value if by == 0 else pltpu.roll(value, by, value.ndim - 1)
    return pltpu.roll(value, lax.rem(by + 4 * size, size), value.ndim - 1)


def merged(pieces, slot):
    out = pieces[0]
    for number, piece in enumerate(pieces[1:], 1):
        out = jnp.where(slot == number, piece, out)
    return out


def rows_at(start, size):
    return pl.ds(start if isinstance(start, int) else pl.multiple_of(start, TILE), size)


def by_node(me, values):
    out = jnp.float32(values[0])
    for n, value in enumerate(values[1:], 1):
        out = jnp.where(me == n, jnp.float32(value), out)
    return out


def scaled_weight(row, column):
    return radau_weights[row][column] * (step_size / 12.0)


class Blocks:
    def __init__(self, comps, nx, ny, nz):
        self.comps, self.nx, self.ny, self.nz = comps, nx, ny, nz
        self.per = nz // ny
        self.left = nx - self.per
        assert nz % ny == 0 and ny % TILE == 0 and 2 * self.left == self.per
        self.half = nz // 2
        self.count = comps + (comps + 1) // 2
        self.step = CHUNK + 8

    def pair(self, b):
        first = 2 * (b - self.comps)
        return first, min(first + 1, self.comps - 1) if isinstance(b, int) else jnp.minimum(first + 1, self.comps - 1)

    def whole(self, ref, c):
        return ref[c, pl.ds(0, self.per)].reshape(self.nz, self.nz)

    def leftovers(self, ref, first, second):
        at = pl.ds(self.per, self.left)
        shape = (self.half, self.nz)
        return jnp.concatenate([ref[first, at].reshape(shape), ref[second, at].reshape(shape)], axis=0)

    def natural(self, ref, b):
        return self.whole(ref, b) if b < self.comps else self.leftovers(ref, *self.pair(b))

    def put_whole(self, ref, c, value):
        ref[c, pl.ds(0, self.per)] = value.reshape(self.per, self.ny, self.nz)

    def put_leftovers(self, ref, b, value):
        at = pl.ds(self.per, self.left)
        shape = (self.left, self.ny, self.nz)
        first, second = self.pair(b)
        ref[second, at] = value[self.half :].reshape(shape)
        ref[first, at] = value[: self.half].reshape(shape)

    def put_natural(self, ref, b, value):
        if b < self.comps:
            self.put_whole(ref, b, value)
        else:
            self.put_leftovers(ref, b, value)

    def row(self, c, i, t):
        if i < self.per:
            return c * self.nz + (i * self.ny + t)
        return (self.comps + c // 2) * self.nz + lax.rem(c, 2) * self.half + ((i - self.per) * self.ny + t)


def split_depth(blocks, read, alpha, write):
    comps = blocks.comps
    ((plus, minus),) = splits([read(c) for c in range(comps)], [None, None, alpha], (2,))
    for c in range(comps):
        write(c, plus[c], minus[c])
    shared = [read(b) for b in range(comps, blocks.count)]
    fields = [shared[c // 2] if c % 2 == 0 else turned(shared[c // 2], blocks.half) for c in range(comps)]
    ((plus, minus),) = splits(fields, [None, None, alpha], (2,))
    lower = lane_index(fields[0].shape) < blocks.half
    for b in range(comps, blocks.count):
        first, second = blocks.pair(b)
        write(b, *[jnp.where(lower, v[first], turned(v[second], blocks.half)) for v in (plus, minus)])


def write_edges(read, nx, ny, comps, lo_ref, hi_ref, side_ref):
    rows = side_ref.shape[1] // (2 * HALO)
    for c in range(comps):
        for i in range(HALO):
            lo_ref[0, pl.ds((c * HALO + i) * ny, ny), :] = read(c, i)
            hi_ref[0, pl.ds((c * HALO + i) * ny, ny), :] = read(c, nx - HALO + i)

    def side(i, carry):
        for c in range(comps):
            value = read(c, i)
            side_ref[0, pl.ds(c * nx + i, HALO, stride=rows), :] = value[ny - HALO :]
            side_ref[0, pl.ds(HALO * rows + c * nx + i, HALO, stride=rows), :] = value[:HALO]
        return carry

    lax.fori_loop(0, nx, side, 0, unroll=4)


def faster(best, read, first, count, comps):
    def step(i, best):
        speeds = signal_speeds([read(c, i) for c in range(comps)])
        return tuple(jnp.maximum(b, s) for b, s in zip(best, speeds))

    return lax.fori_loop(first, first + count, step, best, unroll=4 if count % 4 == 0 else count)


def speed_row(best, width):
    rows = [jnp.max(b, axis=0, keepdims=True) for b in best]
    size = width
    while size > TILE:
        size //= 2
        rows = [jnp.maximum(r, turned(r, -size)) for r in rows]
    rows = [turned(r, TILE * k) for k, r in enumerate(rows)]
    return merged(rows, lane_index(rows[0].shape) % width // TILE)


def speed_tile(row, nodes):
    nz = row.shape[-1]
    width = nz // nodes
    shape = (3 * nodes, nz)
    lane = lane_index(shape)
    place = lax.broadcasted_iota(jnp.int32, shape, 0)
    mine = (lane // width == place % nodes) & (lane % width // TILE == place // nodes)
    spots = jnp.max(jnp.where(mine, row, 0.0), axis=1, keepdims=True)
    group = lane_index((1, nz)) // width
    rows = [merged([spots[k * nodes + m : k * nodes + m + 1] for m in range(nodes)], group) for k in range(3)]
    return jnp.concatenate(rows + [jnp.zeros((TILE - 3, nz), jnp.float32)], axis=0)


def open_kernel(u_hbm, u_ref, al_ref, sems, *, nodes):
    comps, nx, ny, nz = u_ref.shape
    me = lax.axis_index("node")
    chunks = sems.shape[0]
    size = nx // chunks
    copies = []
    for n in range(chunks):
        at = pl.ds(n * size, size)
        copies.append(pltpu.make_async_copy(u_hbm.at[0, :, at], u_ref.at[:, at], sems.at[n]))
        copies[-1].start()

    def read(c, i):
        return u_ref[c, i]

    best = tuple(jnp.zeros((ny, nz), jnp.float32) for _ in range(3))
    for n in range(chunks):
        copies[n].wait()
        best = faster(best, read, n * size, size, comps)
    width = nz // nodes
    rows = [jnp.max(b, axis=0, keepdims=True) for b in best]
    rows = [functools.reduce(jnp.maximum, [turned(r, width * k) for k in range(nodes)]) for r in rows]
    row = speed_row(rows, width)
    row = jnp.where(lane_index(row.shape) // width == me, row, 0.0)
    al_ref[...] = jnp.broadcast_to(row[None], al_ref.shape)


def quarters_kernel(u_ref, *refs):
    parts, ring = refs[:-1], refs[-1]
    nodes = len(parts)
    blocks = Blocks(*u_ref.shape)
    me = lax.axis_index("node")
    quarters = [me ^ k for k in range(nodes)]
    for b in range(blocks.count):
        send_quarter(blocks.natural(u_ref, b).T, ring, b, parts, quarters, blocks.nz // nodes)


def send_quarter(value, ring_ref, b, parts, quarters, width):
    nz = value.shape[0]
    base = b * (nz + 2 * TILE)
    ring_ref[rows_at(base + TILE, nz), :] = value
    ring_ref[rows_at(base, TILE), :] = value[nz - TILE :]
    ring_ref[rows_at(base + TILE + nz, TILE), :] = value[:TILE]
    size = width + 8
    for part, quarter in zip(parts, quarters):
        part[rows_at(b * size, size), :] = ring_ref[pl.ds(base + (TILE - HALO) + quarter * width, size), :]


def start_kernel(init_ref, rows_ref, pack_ref, turned_ref, *, nodes):
    comps, nx, ny, nz = init_ref.shape
    blocks = Blocks(comps, nx, ny, nz)
    width = nz // nodes
    me = lax.axis_index("node")
    lanes = lane_index((ny, nz)) // width
    for b in range(blocks.count):
        turned_ref[rows_at(b * nz, nz), :] = blocks.natural(init_ref, b).T
        rows_ref[rows_at(b * width, width), :] = turned_ref[rows_at(b * nz + me * width, width), :]

    def step(c, carry):
        for q in range(nx // nodes):
            pieces = [turned(init_ref[c, q * nodes + i], width * (i - me)) for i in range(nodes)]
            pack_ref[rows_at((c * (nx // nodes) + q) * ny, ny), :] = merged(pieces, lanes)
        return carry

    lax.fori_loop(0, comps, step, 0)


def gather_kernel(*refs):
    parts, (rows_ref, nat_ref, lo_ref, hi_ref, side_ref) = refs[:-5], refs[-5:]
    nodes = len(parts)
    comps, nx, ny, nz = nat_ref.shape
    blocks = Blocks(comps, nx, ny, nz)
    width = nz // nodes
    size = width + 8
    me = lax.axis_index("node")
    for k in range(nodes):
        rows_ref[me ^ k] = parts[k][...]
    for b in range(blocks.count):
        own = pl.ds(b * size + HALO, width)
        state = jnp.concatenate([rows_ref[m, own, :] for m in range(nodes)], axis=0)
        blocks.put_natural(nat_ref, b, state.T)
    write_edges(lambda c, i: nat_ref[c, i], nx, ny, comps, lo_ref, hi_ref, side_ref)


def along_second(u, alphas, side_ref, dims, fy, yp, ym, gp, gm):
    comps, nx, ny, nz = dims
    rows = gp.shape[0] // (2 * HALO)
    every = range(comps)

    def own(i, carry):
        ((p, m),) = splits([u(c, i) for c in every], alphas, (1,))
        for c in every:
            at = rows_at((c * nx + i) * ny, ny)
            yp[at, :] = p[c]
            ym[at, :] = m[c]
        return carry

    lax.fori_loop(0, nx, own, 0, unroll=4)

    def ghost(i, carry):
        ((p, m),) = splits([side_ref[0, pl.ds(i * rows + c * nx, nx), :] for c in every], alphas, (1,))
        for c in every:
            gp[pl.ds(i * rows + c * nx, nx), :] = p[c]
            gm[pl.ds(i * rows + c * nx, nx), :] = m[c]
        return carry

    lax.fori_loop(0, 2 * HALO, ghost, 0, unroll=HALO)

    def along(b, carry):
        first = pl.multiple_of(b * TILE, TILE)

        def load(j):
            if HALO <= j < HALO + ny:
                at = pl.ds(first * ny + (j - HALO), TILE, stride=ny)
                return yp[at, :], ym[at, :]
            at = pl.ds((j if j < HALO else j - ny) * rows + first, TILE)
            return gp[at, :], gm[at, :]

        def store(i, value):
            fy[pl.ds(i * rows + first, TILE), :] = value

        stream(load, store, ny)
        return carry

    lax.fori_loop(0, rows // TILE, along, 0)


def along_last(blocks, zp, zm, fz, after):
    size = blocks.step * TILE

    def along(b, carry):
        def load(j):
            at = pl.ds(b * size + j, TILE, stride=blocks.step)
            return zp[at, :], zm[at, :]

        def store(i, value):
            fz[pl.ds(b * blocks.nz + i, TILE, stride=CHUNK), :] = value

        after(jnp.maximum(b - 1, 0))
        stream(load, store, CHUNK)
        return carry

    lax.fori_loop(0, blocks.count, along, 0)
    after(blocks.count - 1)


def along_first(u, alphas, lo_ref, hi_ref, fy, rate, xp, xm, extra, after):
    comps, nx, ny, nz = rate.shape
    rows = fy.shape[0] // ny
    every = range(comps)

    def split(fields, at):
        ((p, m),) = splits(fields, alphas, (0,))
        for c in every:
            xp[at, c * ny : (c + 1) * ny, :] = p[c]
            xm[at, c * ny : (c + 1) * ny, :] = m[c]

    def own(i, carry):
        split([u(c, i) for c in every], i + HALO)
        return carry

    lax.fori_loop(0, nx, own, 0, unroll=4)
    for ref, start in ((lo_ref, 0), (hi_ref, nx + HALO)):

        def ghost(i, carry, ref=ref, start=start):
            split([ref[0, rows_at((c * HALO + i) * ny, ny), :] for c in every], start + i)
            return carry

        lax.fori_loop(0, HALO, ghost, 0, unroll=HALO)

    def along(c, carry):
        after(jnp.maximum(c - 1, 0))
        for t in range(0, ny, TILE):

            def load(j, t=t):
                at = rows_at(c * ny + t, TILE)
                return xp[j, at, :], xm[j, at, :]

            def store(i, value, t=t):
                value = value + fy[pl.ds(t * rows + c * nx + i, TILE, stride=rows), :]
                rate[c, i, pl.ds(t, TILE), :] = value if extra is None else value + extra(c, i, t)

            stream(load, store, nx)
        return carry

    lax.fori_loop(0, comps, along, 0)
    after(jnp.int32(comps - 1))


def tile_rows(tile):
    return [tile[k : k + 1, :] for k in range(3)]


def along_lanes(nat_ref, rows_ref, side_ref, al_ref, fz, fy, al_out, scratch, after):
    zp, zm, yp, ym, gp, gm = scratch
    nodes = rows_ref.shape[0]
    dims = nat_ref.shape
    blocks = Blocks(*dims)
    nz = blocks.nz
    width = nz // nodes
    tile = speed_tile(jnp.max(al_ref[...], axis=0)[:1], nodes)
    al_out[...] = tile
    alphas = tile_rows(tile)
    along_second(lambda c, i: nat_ref[c, i], alphas, side_ref, dims, fy, yp, ym, gp, gm)
    group = lane_index((1, nz)) // width
    each = width // CHUNK
    for m in range(nodes):
        alpha = jnp.max(jnp.where(group == m, alphas[2], 0.0))

        def depth(n, carry, m=m, alpha=alpha):
            def read(b):
                return rows_ref[m, rows_at(b * (width + 8) + n * CHUNK, blocks.step), :]

            def write(b, plus, minus):
                to = rows_at((b * TILE + m * each + n) * blocks.step, blocks.step)
                zp[to, :] = plus
                zm[to, :] = minus

            split_depth(blocks, read, alpha, write)
            return carry

        lax.fori_loop(0, each, depth, 0, unroll=True)
    along_last(blocks, zp, zm, fz, after)


def first_lanes_kernel(nat_ref, rows_ref, side_ref, al_ref, fz, fy, al_out, *scratch):
    along_lanes(nat_ref, rows_ref, side_ref, al_ref, fz, fy, al_out, scratch, lambda b: None)


def second_lanes_kernel(
    nat_ref, own_ref, before_ref, behind_ref, side_ref, al_ref, fz, fy, al_out, back, rows_ref, *scratch
):
    nodes = own_ref.shape[0]
    blocks = Blocks(*nat_ref.shape)
    nz = blocks.nz
    width = nz // nodes
    size = width + 8
    for m in range(nodes):
        rows_ref[m] = own_ref[m]
        for b in range(blocks.count):
            ghost = pl.ds((m * blocks.count + b) * 4, HALO)
            rows_ref[m, pl.ds(b * size, HALO), :] = before_ref[ghost, :]
            rows_ref[m, pl.ds(b * size + HALO + width, HALO), :] = behind_ref[ghost, :]

    def after(b):
        at = rows_at(b * nz, nz)
        fz[at, :] = back[at, :].T

    along_lanes(nat_ref, rows_ref, side_ref, al_ref, back, fy, al_out, scratch, after)


def first_rows_kernel(nat_in, lo_in, hi_in, al_in, fz, fy, start_ref, *refs):
    rows_ref, nat_ref, lo_ref, hi_ref, side_ref, first_ref, last_ref, al_ref, rate, xp, xm = refs
    nodes = rows_ref.shape[0]
    comps, nx, ny, nz = nat_ref.shape
    blocks = Blocks(comps, nx, ny, nz)
    width = nz // nodes
    size = width + 8

    def state(value, b):
        rates = value.T + fz[rows_at(b * nz, nz), :]
        start = start_ref[rows_at(b * width, width), :]
        states = []
        for m in range(nodes):
            new = start
            for n in range(nodes):
                new = new + scaled_weight(m, n) * rates[n * width : (n + 1) * width]
            rows_ref[m, pl.ds(b * size + HALO, width), :] = new
            ghost = pl.ds((m * blocks.count + b) * 4, HALO)
            first_ref[ghost, :] = new[:HALO]
            last_ref[ghost, :] = new[width - HALO :]
            states.append(new)
        return jnp.concatenate(states, axis=0).T

    def after(c):
        blocks.put_whole(nat_ref, c, state(blocks.whole(rate, c), c))
        b = blocks.comps + c // 2
        blocks.put_leftovers(nat_ref, b, state(blocks.leftovers(rate, *blocks.pair(b)), b))

    along_first(lambda c, i: nat_in[c, i], tile_rows(al_in), lo_in, hi_in, fy, rate, xp, xm, None, after)

    def read(c, i):
        return nat_ref[c, i]

    best = tuple(jnp.zeros((ny, nz), jnp.float32) for _ in range(3))
    row = speed_row(faster(best, read, 0, nx, comps), width)
    al_ref[...] = jnp.broadcast_to(row[None], al_ref.shape)
    write_edges(read, nx, ny, comps, lo_ref, hi_ref, side_ref)


def second_rows_kernel(nat_ref, lo_ref, hi_ref, al_ref, fz, fy, pack_ref, *refs):
    outs, (rate, xp, xm) = refs[:-3], refs[-3:]
    nodes = len(outs)
    comps, nx, ny, nz = nat_ref.shape
    blocks = Blocks(comps, nx, ny, nz)
    width = nz // nodes
    me = lax.axis_index("node")
    weights = [
        [by_node(me, [scaled_weight(n ^ k, j) for n in range(nodes)]) for j in range(nodes)] for k in range(nodes)
    ]
    lanes = lane_index((TILE, nz)) // width

    def extra(c, i, t):
        return fz[rows_at(blocks.row(c, i, t), TILE), :]

    def after(c):
        for t in range(0, ny, TILE):
            for q in range(nx // nodes):
                at = rows_at((c * (nx // nodes) + q) * ny + t, TILE)
                start = pack_ref[at, :]
                rows = [rate[c, q * nodes + i, pl.ds(t, TILE), :] for i in range(nodes)]
                rates = [
                    merged([turned(rows[i], width * (i - j)) for i in range(nodes)], lanes) for j in range(nodes)
                ]
                for k in range(nodes):
                    value = start
                    for j in range(nodes):
                        value = value + weights[k][j] * rates[j]
                    outs[k][at, :] = turned(value, width * me)

    along_first(lambda c, i: nat_ref[c, i], tile_rows(al_ref), lo_ref, hi_ref, fy, rate, xp, xm, extra, after)


def close_kernel(*refs):
    parts, (out_hbm, out_ref, sems) = refs[:-3], refs[-3:]
    nodes = len(parts)
    comps, nx, ny, nz = out_ref.shape
    width = nz // nodes
    me = lax.axis_index("node")
    lanes = lane_index((ny, nz)) // width
    copies = []
    for c in range(comps):
        for q in range(nx // nodes):
            at = pl.ds((c * (nx // nodes) + q) * ny, ny)
            values = [part[at, :] for part in parts]
            for i in range(nodes):
                out = values[0]
                for k in range(1, nodes):
                    out = jnp.where(lanes == lax.rem((me ^ k) + i, nodes), values[k], out)
                out_ref[c, q * nodes + i] = turned(out, -width * i)
        copies.append(pltpu.make_async_copy(out_ref.at[c], out_hbm.at[0, c], sems.at[c]))
        copies[-1].start()
    for copy in copies:
        copy.wait()


def call(kernel, name, outs, operands, scratch=(), flops=500_000_000, anywhere=False, outside=False):
    vmem, hbm = pl.BlockSpec(memory_space=pltpu.VMEM), pl.BlockSpec(memory_space=pltpu.HBM)
    moved = sum(4 * x.size for x in operands)
    scratch = [pltpu.VMEM(x, jnp.float32) if isinstance(x, tuple) else x for x in scratch]
    return pl.pallas_call(
        kernel,
        out_shape=[jax.ShapeDtypeStruct(shape, jnp.float32) for shape in outs],
        in_specs=[hbm if anywhere else vmem] * len(operands),
        out_specs=[hbm if outside else vmem] * len(outs),
        scratch_shapes=scratch,
        compiler_params=pltpu.CompilerParams(vmem_limit_bytes=32 * 1024 * 1024),
        cost_estimate=pl.CostEstimate(flops=flops, bytes_accessed=2 * moved, transcendentals=0),
        name=name,
    )(*operands)


def shifted(value, axis, by):
    count = lax.axis_size(axis)
    return lax.ppermute(value, axis, [(i, (i + by) % count) for i in range(count)])


def swapped(value, by):
    return lax.ppermute(value, "node", [(i, i ^ by) for i in range(lax.axis_size("node"))])


def beside(side):
    if lax.axis_size("gy") == 2:
        return shifted(side, "gy", 1)
    half = side.shape[1] // 2
    return jnp.concatenate([shifted(side[:, :half], "gy", 1), shifted(side[:, half:], "gy", -1)], axis=1)


def across(lo, hi):
    return shifted(hi, "gx", 1), shifted(lo, "gx", -1)


def exchanged(parts):
    moved = {k: swapped(parts[k], k) for k in sorted(range(1, len(parts)), reverse=True)}
    return [parts[0]] + [moved[k] for k in range(1, len(parts))]


def local(initial, guesses):
    comps, nx, ny, nz = initial.shape
    nodes = lax.axis_size("node")
    everyone = ("node", "gx", "gy")
    devices = nodes * lax.axis_size("gx") * lax.axis_size("gy")
    rows = -(-comps * nx // TILE) * TILE
    blocks = Blocks(comps, nx, ny, nz)
    width = nz // nodes
    assert nz == CHUNK * TILE and width % CHUNK == 0 and nx % nodes == 0
    edge = (1, comps * HALO * ny, nz)
    edges = [edge, edge, (1, 2 * HALO * rows, nz)]
    tile_shape = (TILE, nz)
    speeds_shape = (devices, TILE, nz)
    part = (blocks.count * (width + 8), nz)
    pack = (comps * nx // nodes * ny, nz)
    ghost = (nodes * blocks.count * 4, nz)
    depth_shape = (blocks.count * nz, nz)
    lanes_out = [depth_shape, (ny * rows, nz), tile_shape]
    lanes_scratch = [(blocks.count * TILE * blocks.step, nz)] * 2 + [(ny * rows, nz)] * 2 + [(2 * HALO * rows, nz)] * 2
    slabs = [initial.shape] + [(nx + 2 * HALO, comps * ny, nz)] * 2
    ring = (blocks.count * (nz + 2 * TILE), nz)
    chunks = 4 if nx % 4 == 0 else 1

    field, speeds = call(
        functools.partial(open_kernel, nodes=nodes),
        "open_kernel",
        [initial.shape, speeds_shape],
        [guesses],
        [pltpu.SemaphoreType.DMA((chunks,))],
        anywhere=True,
    )
    speeds = lax.all_to_all(speeds, everyone, 0, 0)
    parts = call(quarters_kernel, "quarters_kernel", [part] * nodes, [field], [ring])
    start, start_pack = call(
        functools.partial(start_kernel, nodes=nodes),
        "start_kernel",
        [(blocks.count * width, nz), pack],
        [initial],
        [depth_shape],
    )
    start, start_pack, *parts = lax.optimization_barrier((start, start_pack, *exchanged(parts)))
    turned_field, field, lo, hi, side = call(
        gather_kernel, "gather_kernel", [(nodes,) + part, initial.shape] + edges, parts
    )
    side = beside(side)
    lower, upper = across(lo, hi)
    depth, rates, tile = call(
        first_lanes_kernel,
        "first_lanes_kernel",
        lanes_out,
        [field, turned_field, side, speeds],
        lanes_scratch,
        4_000_000_000,
    )
    turned_field, field, lo, hi, side, first, last, speeds = call(
        first_rows_kernel,
        "first_rows_kernel",
        [(nodes,) + part, initial.shape] + edges + [ghost, ghost, speeds_shape],
        [field, lower, upper, tile, depth, rates, start],
        slabs,
        2_500_000_000,
    )
    speeds = lax.all_to_all(speeds, everyone, 0, 0)
    before, behind = shifted(last, "node", 1), shifted(first, "node", -1)
    side = beside(side)
    lower, upper = across(lo, hi)
    depth, rates, tile = call(
        second_lanes_kernel,
        "second_lanes_kernel",
        lanes_out,
        [field, turned_field, before, behind, side, speeds],
        [depth_shape, (nodes,) + part] + lanes_scratch,
        4_000_000_000,
    )
    outs = call(
        second_rows_kernel,
        "second_rows_kernel",
        [pack] * nodes,
        [field, lower, upper, tile, depth, rates, start_pack],
        slabs,
        2_500_000_000,
    )
    (states,) = call(
        close_kernel,
        "close_kernel",
        [(1,) + initial.shape],
        exchanged(outs),
        [initial.shape, pltpu.SemaphoreType.DMA((comps,))],
        outside=True,
    )
    return states


def solution(mesh):
    return jax.shard_map(
        local,
        mesh=mesh,
        in_specs=(P(None, "gx", "gy", None), P("node", None, "gx", "gy", None)),
        out_specs=P("node", None, "gx", "gy", None),
        check_vma=False,
    )
```

```python
import functools

import jax
import jax.numpy as jnp
from jax import lax
from jax.experimental import pallas as pl
from jax.experimental.pallas import tpu as pltpu
from jax.sharding import PartitionSpec as P

SWEEPS = 2
HALO = 3
COMPONENTS = 5
TILE = 8
CHUNK = 16

heat_ratio = 1.4
step_size = 0.025
density_floor = 0.5
pressure_floor = 0.25
epsilon = 1e-06
radau_weights = [
    [0.112999479323156, -0.040309220723522, 0.025802377420336, -0.009904676507266],
    [0.2343839957474, 0.206892573935359, -0.047857128048541, 0.016047422806516],
    [0.21668178462325, 0.406123263867373, 0.189036518170056, -0.024182104899833],
    [0.220462211176768, 0.388193468843172, 0.32884431998006, 0.0625],
]


def reciprocal(value):
    return pl.reciprocal(value, approx=True)


def primitives(fields):
    inverse = 1.0 / jnp.maximum(fields[0], density_floor)
    velocity = [fields[k] * inverse for k in (1, 2, 3)]
    energy = fields[1] * velocity[0] + fields[2] * velocity[1] + fields[3] * velocity[2]
    pressure = jnp.maximum(0.4 * (fields[4] - 0.5 * energy), pressure_floor)
    return inverse, velocity, pressure


def signal_speeds(fields):
    inverse, velocity, pressure = primitives(fields)
    sound = jnp.sqrt(heat_ratio * pressure * inverse)
    return [jnp.abs(v) + sound for v in velocity]


def half_fluxes(half, speed, half_pressure, direction):
    flux = [half[direction + 1]] + [half[k] * speed for k in (1, 2, 3)]
    flux.append((half[4] + half_pressure) * speed)
    flux[direction + 1] = flux[direction + 1] + half_pressure
    return flux


def splits(fields, alphas, directions=(0, 1, 2)):
    _, velocity, pressure = primitives(fields)
    half = [0.5 * field for field in fields]
    half_pressure = 0.5 * pressure
    out = []
    for direction in directions:
        flux = half_fluxes(half, velocity[direction], half_pressure, direction)
        signal = [alphas[direction] * value for value in half]
        out.append(
            ([f + s for f, s in zip(flux, signal)], [f - s for f, s in zip(flux, signal)])
        )
    return out


def cell_terms(below, above):
    second = above - below
    both = below + above
    square = second * second
    middle = 0.25 * (both * both) + ((13.0 / 12.0) * square + epsilon)
    outer = middle + square
    cross = both * second
    return second, outer + cross, middle, outer - cross


def correction(first, middle, last, third_first, third_last):
    ratio_first = middle * reciprocal(first)
    ratio_last = middle * reciprocal(last)
    weight_first = ratio_first * ratio_first
    weight_last = 1.5 * (ratio_last * ratio_last)
    total = (6.0 + weight_first) + (weight_last + weight_last)
    return (weight_first * third_first + weight_last * third_last) * reciprocal(total)


def stream(load, store, count):
    plus, minus, centre = {}, {}, {}
    terms_plus, terms_minus, third_plus, third_minus, interface = {}, {}, {}, {}, {}
    differences_plus, differences_minus = {}, {}
    plus[0], minus[0] = load(0)
    for j in range(1, count + 2 * HALO):
        plus[j], minus[j] = load(j)
        differences_plus[j] = plus[j] - plus[j - 1]
        differences_minus[j] = minus[j] - minus[j - 1]
        cell = j - 1
        if cell < 1:
            continue
        terms_plus[cell] = cell_terms(differences_plus[cell], differences_plus[j])
        terms_minus[cell] = cell_terms(differences_minus[cell], differences_minus[j])
        if 2 <= cell <= count + 3:
            centre[cell] = 6.0 * (plus[cell] + minus[cell]) - (
                terms_plus[cell][0] + terms_minus[cell][0]
            )
        if cell < 2:
            continue
        third_plus[cell] = terms_plus[cell][0] - terms_plus[cell - 1][0]
        third_minus[cell] = terms_minus[cell][0] - terms_minus[cell - 1][0]
        if cell < 4:
            continue
        at = cell - 2
        right = correction(
            terms_plus[at - 1][1], terms_plus[at][2], terms_plus[at + 1][3], third_plus[at], third_plus[at + 1]
        )
        left = correction(
            terms_minus[at + 2][3], terms_minus[at + 1][2], terms_minus[at][1],
            third_minus[at + 2], third_minus[at + 1],
        )
        interface[at] = (third_plus[at + 1] - third_minus[at + 1]) - 4.0 * (right - left)
        if at >= 3:
            store(at - 3, (centre[at - 1] - centre[at + 1]) + (interface[at - 1] - interface[at]))


def lane_index(shape):
    return lax.broadcasted_iota(jnp.int32, shape, len(shape) - 1)


def turned(value, by):
    size = value.shape[-1]
    if isinstance(by, int):
        by = by % size
        return value if by == 0 else pltpu.roll(value, by, value.ndim - 1)
    return pltpu.roll(value, lax.rem(by + 4 * size, size), value.ndim - 1)


def merged(pieces, slot):
    out = pieces[0]
    for number, piece in enumerate(pieces[1:], 1):
        out = jnp.where(slot == number, piece, out)
    return out


def rows_at(start, size):
    return pl.ds(start if isinstance(start, int) else pl.multiple_of(start, TILE), size)


def by_node(me, values):
    out = jnp.float32(values[0])
    for n, value in enumerate(values[1:], 1):
        out = jnp.where(me == n, jnp.float32(value), out)
    return out


def scaled_weight(row, column):
    return radau_weights[row][column] * (step_size / 12.0)


class Blocks:
    def __init__(self, comps, nx, ny, nz):
        self.comps, self.nx, self.ny, self.nz = comps, nx, ny, nz
        self.per = nz // ny
        self.left = nx - self.per
        assert nz % ny == 0 and ny % TILE == 0 and 2 * self.left == self.per
        self.half = nz // 2
        self.count = comps + (comps + 1) // 2
        self.step = CHUNK + 8

    def pair(self, b):
        first = 2 * (b - self.comps)
        return first, min(first + 1, self.comps - 1) if isinstance(b, int) else jnp.minimum(first + 1, self.comps - 1)

    def whole(self, ref, c):
        return ref[c, pl.ds(0, self.per)].reshape(self.nz, self.nz)

    def leftovers(self, ref, first, second):
        at = pl.ds(self.per, self.left)
        shape = (self.half, self.nz)
        return jnp.concatenate([ref[first, at].reshape(shape), ref[second, at].reshape(shape)], axis=0)

    def natural(self, ref, b):
        return self.whole(ref, b) if b < self.comps else self.leftovers(ref, *self.pair(b))

    def put_whole(self, ref, c, value):
        ref[c, pl.ds(0, self.per)] = value.reshape(self.per, self.ny, self.nz)

    def put_leftovers(self, ref, b, value):
        at = pl.ds(self.per, self.left)
        shape = (self.left, self.ny, self.nz)
        first, second = self.pair(b)
        ref[second, at] = value[self.half :].reshape(shape)
        ref[first, at] = value[: self.half].reshape(shape)

    def put_natural(self, ref, b, value):
        if b < self.comps:
            self.put_whole(ref, b, value)
        else:
            self.put_leftovers(ref, b, value)

    def row(self, c, i, t):
        if i < self.per:
            return c * self.nz + (i * self.ny + t)
        return (self.comps + c // 2) * self.nz + lax.rem(c, 2) * self.half + ((i - self.per) * self.ny + t)


def split_depth(blocks, read, alpha, write):
    comps = blocks.comps
    ((plus, minus),) = splits([read(c) for c in range(comps)], [None, None, alpha], (2,))
    for c in range(comps):
        write(c, plus[c], minus[c])
    shared = [read(b) for b in range(comps, blocks.count)]
    fields = [shared[c // 2] if c % 2 == 0 else turned(shared[c // 2], blocks.half) for c in range(comps)]
    ((plus, minus),) = splits(fields, [None, None, alpha], (2,))
    lower = lane_index(fields[0].shape) < blocks.half
    for b in range(comps, blocks.count):
        first, second = blocks.pair(b)
        write(b, *[jnp.where(lower, v[first], turned(v[second], blocks.half)) for v in (plus, minus)])


def write_edges(read, nx, ny, comps, lo_ref, hi_ref, side_ref):
    rows = side_ref.shape[1] // (2 * HALO)
    for c in range(comps):
        for i in range(HALO):
            lo_ref[0, pl.ds((c * HALO + i) * ny, ny), :] = read(c, i)
            hi_ref[0, pl.ds((c * HALO + i) * ny, ny), :] = read(c, nx - HALO + i)

    def side(i, carry):
        for c in range(comps):
            value = read(c, i)
            side_ref[0, pl.ds(c * nx + i, HALO, stride=rows), :] = value[ny - HALO :]
            side_ref[0, pl.ds(HALO * rows + c * nx + i, HALO, stride=rows), :] = value[:HALO]
        return carry

    lax.fori_loop(0, nx, side, 0, unroll=4)


def faster(best, read, first, count, comps):
    def step(i, best):
        speeds = signal_speeds([read(c, i) for c in range(comps)])
        return tuple(jnp.maximum(b, s) for b, s in zip(best, speeds))

    return lax.fori_loop(first, first + count, step, best, unroll=4 if count % 4 == 0 else count)


def speed_row(best, width):
    rows = [jnp.max(b, axis=0, keepdims=True) for b in best]
    size = width
    while size > TILE:
        size //= 2
        rows = [jnp.maximum(r, turned(r, -size)) for r in rows]
    rows = [turned(r, TILE * k) for k, r in enumerate(rows)]
    return merged(rows, lane_index(rows[0].shape) % width // TILE)


def speed_tile(row, nodes):
    nz = row.shape[-1]
    width = nz // nodes
    shape = (3 * nodes, nz)
    lane = lane_index(shape)
    place = lax.broadcasted_iota(jnp.int32, shape, 0)
    mine = (lane // width == place % nodes) & (lane % width // TILE == place // nodes)
    spots = jnp.max(jnp.where(mine, row, 0.0), axis=1, keepdims=True)
    group = lane_index((1, nz)) // width
    rows = [merged([spots[k * nodes + m : k * nodes + m + 1] for m in range(nodes)], group) for k in range(3)]
    return jnp.concatenate(rows + [jnp.zeros((TILE - 3, nz), jnp.float32)], axis=0)


def send_speeds(row, tiles_ref, out_hbm, sem):
    tiles_ref[...] = jnp.broadcast_to(row[None], tiles_ref.shape)
    copy = pltpu.make_async_copy(tiles_ref, out_hbm, sem)
    copy.start()
    return copy


def open_kernel(u_ref, *refs):
    parts, (speeds_hbm, ring, tiles_ref, sem) = refs[:-4], refs[-4:]
    nodes = len(parts)
    comps, nx, ny, nz = u_ref.shape[1:]
    blocks = Blocks(comps, nx, ny, nz)
    me = lax.axis_index("node")
    best = tuple(jnp.zeros((ny, nz), jnp.float32) for _ in range(3))
    best = faster(best, lambda c, i: u_ref[0, c, i], 0, nx, comps)
    width = nz // nodes
    rows = [jnp.max(b, axis=0, keepdims=True) for b in best]
    rows = [functools.reduce(jnp.maximum, [turned(r, width * k) for k in range(nodes)]) for r in rows]
    row = speed_row(rows, width)
    row = jnp.where(lane_index(row.shape) // width == me, row, 0.0)
    copy = send_speeds(row, tiles_ref, speeds_hbm, sem)
    quarters = [me ^ k for k in range(nodes)]
    for b in range(blocks.count):
        send_quarter(blocks.natural(u_ref.at[0], b).T, ring, b, parts, quarters, width)
    copy.wait()


def send_quarter(value, ring_ref, b, parts, quarters, width):
    nz = value.shape[0]
    base = b * (nz + 2 * TILE)
    ring_ref[rows_at(base + TILE, nz), :] = value
    ring_ref[rows_at(base, TILE), :] = value[nz - TILE :]
    ring_ref[rows_at(base + TILE + nz, TILE), :] = value[:TILE]
    size = width + 8
    for part, quarter in zip(parts, quarters):
        part[rows_at(b * size, size), :] = ring_ref[pl.ds(base + (TILE - HALO) + quarter * width, size), :]


def start_kernel(init_ref, rows_ref, pack_ref, turned_ref, *, nodes):
    comps, nx, ny, nz = init_ref.shape
    blocks = Blocks(comps, nx, ny, nz)
    width = nz // nodes
    me = lax.axis_index("node")
    lanes = lane_index((ny, nz)) // width
    for b in range(blocks.count):
        turned_ref[rows_at(b * nz, nz), :] = blocks.natural(init_ref, b).T
        rows_ref[rows_at(b * width, width), :] = turned_ref[rows_at(b * nz + me * width, width), :]

    def step(c, carry):
        for q in range(nx // nodes):
            pieces = [turned(init_ref[c, q * nodes + i], width * i) for i in range(nodes)]
            out = pieces[0]
            for i in range(1, nodes):
                out = jnp.where(lanes == lax.rem(me + i, nodes), pieces[i], out)
            pack_ref[rows_at((c * (nx // nodes) + q) * ny, ny), :] = out
        return carry

    lax.fori_loop(0, comps, step, 0)


def gather_kernel(*refs):
    parts, (rows_ref, nat_ref, lo_ref, hi_ref, side_ref) = refs[:-5], refs[-5:]
    nodes = len(parts)
    comps, nx, ny, nz = nat_ref.shape
    blocks = Blocks(comps, nx, ny, nz)
    width = nz // nodes
    size = width + 8
    me = lax.axis_index("node")
    for k in range(nodes):
        rows_ref[me ^ k] = parts[k][...]
    for b in range(blocks.count):
        own = pl.ds(b * size + HALO, width)
        state = jnp.concatenate([rows_ref[m, own, :] for m in range(nodes)], axis=0)
        blocks.put_natural(nat_ref, b, state.T)
    write_edges(lambda c, i: nat_ref[c, i], nx, ny, comps, lo_ref, hi_ref, side_ref)


def along_second(u, alphas, side_ref, dims, fy, yp, ym, gp, gm):
    comps, nx, ny, nz = dims
    rows = gp.shape[0] // (2 * HALO)
    every = range(comps)

    def own(i, carry):
        ((p, m),) = splits([u(c, i) for c in every], alphas, (1,))
        for c in every:
            at = rows_at((c * nx + i) * ny, ny)
            yp[at, :] = p[c]
            ym[at, :] = m[c]
        return carry

    lax.fori_loop(0, nx, own, 0, unroll=4)

    def ghost(i, carry):
        ((p, m),) = splits([side_ref[0, pl.ds(i * rows + c * nx, nx), :] for c in every], alphas, (1,))
        for c in every:
            gp[pl.ds(i * rows + c * nx, nx), :] = p[c]
            gm[pl.ds(i * rows + c * nx, nx), :] = m[c]
        return carry

    lax.fori_loop(0, 2 * HALO, ghost, 0, unroll=HALO)

    def along(b, carry):
        first = pl.multiple_of(b * TILE, TILE)

        def load(j):
            if HALO <= j < HALO + ny:
                at = pl.ds(first * ny + (j - HALO), TILE, stride=ny)
                return yp[at, :], ym[at, :]
            at = pl.ds((j if j < HALO else j - ny) * rows + first, TILE)
            return gp[at, :], gm[at, :]

        def store(i, value):
            fy[pl.ds(i * rows + first, TILE), :] = value

        stream(load, store, ny)
        return carry

    lax.fori_loop(0, rows // TILE, along, 0)


def along_last(blocks, zp, zm, fz, after):
    size = blocks.step * TILE

    def along(b, carry):
        def load(j):
            at = pl.ds(b * size + j, TILE, stride=blocks.step)
            return zp[at, :], zm[at, :]

        def store(i, value):
            fz[pl.ds(b * blocks.nz + i, TILE, stride=CHUNK), :] = value

        after(jnp.maximum(b - 1, 0))
        stream(load, store, CHUNK)
        return carry

    lax.fori_loop(0, blocks.count, along, 0)
    after(blocks.count - 1)


def along_first(u, alphas, lo_ref, hi_ref, fy, rate, xp, xm, extra, after):
    comps, nx, ny, nz = rate.shape
    rows = fy.shape[0] // ny
    every = range(comps)

    def split(fields, at):
        ((p, m),) = splits(fields, alphas, (0,))
        for c in every:
            xp[at, c * ny : (c + 1) * ny, :] = p[c]
            xm[at, c * ny : (c + 1) * ny, :] = m[c]

    def own(i, carry):
        split([u(c, i) for c in every], i + HALO)
        return carry

    lax.fori_loop(0, nx, own, 0, unroll=4)
    for ref, start in ((lo_ref, 0), (hi_ref, nx + HALO)):

        def ghost(i, carry, ref=ref, start=start):
            split([ref[0, rows_at((c * HALO + i) * ny, ny), :] for c in every], start + i)
            return carry

        lax.fori_loop(0, HALO, ghost, 0, unroll=HALO)

    def along(c, carry):
        after(jnp.maximum(c - 1, 0))
        for t in range(0, ny, TILE):

            def load(j, t=t):
                at = rows_at(c * ny + t, TILE)
                return xp[j, at, :], xm[j, at, :]

            def store(i, value, t=t):
                value = value + fy[pl.ds(t * rows + c * nx + i, TILE, stride=rows), :]
                rate[c, i, pl.ds(t, TILE), :] = value if extra is None else value + extra(c, i, t)

            stream(load, store, nx)
        return carry

    lax.fori_loop(0, comps, along, 0)
    after(jnp.int32(comps - 1))


def tile_rows(tile):
    return [tile[k : k + 1, :] for k in range(3)]


def along_lanes(nat_ref, rows_ref, side_ref, al_ref, fz, fy, al_out, scratch, after):
    zp, zm, yp, ym, gp, gm = scratch
    nodes = rows_ref.shape[0]
    dims = nat_ref.shape
    blocks = Blocks(*dims)
    nz = blocks.nz
    width = nz // nodes
    tile = speed_tile(jnp.max(al_ref[...], axis=0)[:1], nodes)
    al_out[...] = tile
    alphas = tile_rows(tile)
    along_second(lambda c, i: nat_ref[c, i], alphas, side_ref, dims, fy, yp, ym, gp, gm)
    group = lane_index((1, nz)) // width
    each = width // CHUNK
    for m in range(nodes):
        alpha = jnp.max(jnp.where(group == m, alphas[2], 0.0))

        def depth(n, carry, m=m, alpha=alpha):
            def read(b):
                return rows_ref[m, rows_at(b * (width + 8) + n * CHUNK, blocks.step), :]

            def write(b, plus, minus):
                to = rows_at((b * TILE + m * each + n) * blocks.step, blocks.step)
                zp[to, :] = plus
                zm[to, :] = minus

            split_depth(blocks, read, alpha, write)
            return carry

        lax.fori_loop(0, each, depth, 0, unroll=True)
    along_last(blocks, zp, zm, fz, after)


def first_lanes_kernel(nat_ref, rows_ref, side_ref, al_ref, fz, fy, al_out, *scratch):
    along_lanes(nat_ref, rows_ref, side_ref, al_ref, fz, fy, al_out, scratch, lambda b: None)


def second_lanes_kernel(
    nat_ref, own_ref, before_ref, behind_ref, side_ref, al_ref, fz, fy, al_out, back, rows_ref, *scratch
):
    nodes = own_ref.shape[0]
    blocks = Blocks(*nat_ref.shape)
    nz = blocks.nz
    width = nz // nodes
    size = width + 8
    for m in range(nodes):
        rows_ref[m] = own_ref[m]
        for b in range(blocks.count):
            ghost = pl.ds((m * blocks.count + b) * 4, HALO)
            rows_ref[m, pl.ds(b * size, HALO), :] = before_ref[ghost, :]
            rows_ref[m, pl.ds(b * size + HALO + width, HALO), :] = behind_ref[ghost, :]

    def after(b):
        at = rows_at(b * nz, nz)
        fz[at, :] = back[at, :].T

    along_lanes(nat_ref, rows_ref, side_ref, al_ref, back, fy, al_out, scratch, after)


def first_rows_kernel(nat_in, lo_in, hi_in, al_in, fz, fy, start_ref, *refs):
    rows_ref, nat_ref, lo_ref, hi_ref, side_ref, first_ref, last_ref, speeds_hbm, rate, xp, xm, tiles_ref, sem = refs
    nodes = rows_ref.shape[0]
    comps, nx, ny, nz = nat_ref.shape
    blocks = Blocks(comps, nx, ny, nz)
    width = nz // nodes
    size = width + 8

    def state(value, b):
        rates = value.T + fz[rows_at(b * nz, nz), :]
        start = start_ref[rows_at(b * width, width), :]
        states = []
        for m in range(nodes):
            new = start
            for n in range(nodes):
                new = new + scaled_weight(m, n) * rates[n * width : (n + 1) * width]
            rows_ref[m, pl.ds(b * size + HALO, width), :] = new
            ghost = pl.ds((m * blocks.count + b) * 4, HALO)
            first_ref[ghost, :] = new[:HALO]
            last_ref[ghost, :] = new[width - HALO :]
            states.append(new)
        return jnp.concatenate(states, axis=0).T

    def after(c):
        blocks.put_whole(nat_ref, c, state(blocks.whole(rate, c), c))
        b = blocks.comps + c // 2
        blocks.put_leftovers(nat_ref, b, state(blocks.leftovers(rate, *blocks.pair(b)), b))

    along_first(lambda c, i: nat_in[c, i], tile_rows(al_in), lo_in, hi_in, fy, rate, xp, xm, None, after)

    def read(c, i):
        return nat_ref[c, i]

    best = tuple(jnp.zeros((ny, nz), jnp.float32) for _ in range(3))
    row = speed_row(faster(best, read, 0, nx, comps), width)
    copy = send_speeds(row, tiles_ref, speeds_hbm, sem)
    write_edges(read, nx, ny, comps, lo_ref, hi_ref, side_ref)
    copy.wait()


def second_rows_kernel(nat_ref, lo_ref, hi_ref, al_ref, fz, fy, pack_ref, *refs):
    outs, (rate, xp, xm) = refs[:-3], refs[-3:]
    nodes = len(outs)
    comps, nx, ny, nz = nat_ref.shape
    blocks = Blocks(comps, nx, ny, nz)
    width = nz // nodes
    me = lax.axis_index("node")
    weights = [
        [by_node(me, [scaled_weight(n ^ k, j) for n in range(nodes)]) for j in range(nodes)] for k in range(nodes)
    ]
    lanes = lane_index((TILE, nz)) // width

    def extra(c, i, t):
        return fz[rows_at(blocks.row(c, i, t), TILE), :]

    def after(c):
        for t in range(0, ny, TILE):
            for q in range(nx // nodes):
                at = rows_at((c * (nx // nodes) + q) * ny + t, TILE)
                start = pack_ref[at, :]
                rows = [turned(rate[c, q * nodes + i, pl.ds(t, TILE), :], width * i) for i in range(nodes)]
                rates = [
                    turned(merged([rows[(g - j) % nodes] for g in range(nodes)], lanes), width * (me - j))
                    for j in range(nodes)
                ]
                for k in range(nodes):
                    value = start
                    for j in range(nodes):
                        value = value + weights[k][j] * rates[j]
                    outs[k][at, :] = value

    along_first(lambda c, i: nat_ref[c, i], tile_rows(al_ref), lo_ref, hi_ref, fy, rate, xp, xm, extra, after)


def close_kernel(*refs):
    parts, (out_hbm, out_ref, sems) = refs[:-3], refs[-3:]
    nodes = len(parts)
    comps, nx, ny, nz = out_ref.shape
    width = nz // nodes
    me = lax.axis_index("node")
    lanes = lane_index((ny, nz)) // width
    copies = []
    for c in range(comps):
        for q in range(nx // nodes):
            at = pl.ds((c * (nx // nodes) + q) * ny, ny)
            values = [part[at, :] for part in parts]
            for i in range(nodes):
                out = values[0]
                for k in range(1, nodes):
                    out = jnp.where(lanes == lax.rem((me ^ k) + i, nodes), values[k], out)
                out_ref[c, q * nodes + i] = turned(out, -width * i)
        copies.append(pltpu.make_async_copy(out_ref.at[c], out_hbm.at[0, c], sems.at[c]))
        copies[-1].start()
    for copy in copies:
        copy.wait()


def call(kernel, name, outs, operands, scratch=(), flops=500_000_000, anywhere=False, outside=()):
    vmem, hbm = pl.BlockSpec(memory_space=pltpu.VMEM), pl.BlockSpec(memory_space=pltpu.HBM)
    moved = sum(4 * x.size for x in operands)
    scratch = [pltpu.VMEM(x, jnp.float32) if isinstance(x, tuple) else x for x in scratch]
    return pl.pallas_call(
        kernel,
        out_shape=[jax.ShapeDtypeStruct(shape, jnp.float32) for shape in outs],
        in_specs=[hbm if anywhere else vmem] * len(operands),
        out_specs=[hbm if n in outside else vmem for n in range(len(outs))],
        scratch_shapes=scratch,
        compiler_params=pltpu.CompilerParams(vmem_limit_bytes=32 * 1024 * 1024),
        cost_estimate=pl.CostEstimate(flops=flops, bytes_accessed=2 * moved, transcendentals=0),
        name=name,
    )(*operands)


def shifted(value, axis, by):
    count = lax.axis_size(axis)
    return lax.ppermute(value, axis, [(i, (i + by) % count) for i in range(count)])


def swapped(value, by):
    return lax.ppermute(value, "node", [(i, i ^ by) for i in range(lax.axis_size("node"))])


def beside(side):
    if lax.axis_size("gy") == 2:
        return shifted(side, "gy", 1)
    half = side.shape[1] // 2
    return jnp.concatenate([shifted(side[:, :half], "gy", 1), shifted(side[:, half:], "gy", -1)], axis=1)


def across(lo, hi):
    return shifted(hi, "gx", 1), shifted(lo, "gx", -1)


def exchanged(parts):
    moved = {k: swapped(parts[k], k) for k in sorted(range(1, len(parts)), reverse=True)}
    return [parts[0]] + [moved[k] for k in range(1, len(parts))]


def local(initial, guesses):
    comps, nx, ny, nz = initial.shape
    nodes = lax.axis_size("node")
    everyone = ("node", "gx", "gy")
    devices = nodes * lax.axis_size("gx") * lax.axis_size("gy")
    rows = -(-comps * nx // TILE) * TILE
    blocks = Blocks(comps, nx, ny, nz)
    width = nz // nodes
    assert nz == CHUNK * TILE and width % CHUNK == 0 and nx % nodes == 0
    edge = (1, comps * HALO * ny, nz)
    edges = [edge, edge, (1, 2 * HALO * rows, nz)]
    tile_shape = (TILE, nz)
    speeds_shape = (devices, TILE, nz)
    part = (blocks.count * (width + 8), nz)
    pack = (comps * nx // nodes * ny, nz)
    ghost = (nodes * blocks.count * 4, nz)
    depth_shape = (blocks.count * nz, nz)
    lanes_out = [depth_shape, (ny * rows, nz), tile_shape]
    lanes_scratch = [(blocks.count * TILE * blocks.step, nz)] * 2 + [(ny * rows, nz)] * 2 + [(2 * HALO * rows, nz)] * 2
    slabs = [initial.shape] + [(nx + 2 * HALO, comps * ny, nz)] * 2
    ring = (blocks.count * (nz + 2 * TILE), nz)

    *parts, speeds = call(
        open_kernel,
        "open_kernel",
        [part] * nodes + [speeds_shape],
        [guesses],
        [ring, speeds_shape, pltpu.SemaphoreType.DMA],
        outside=(nodes,),
    )
    speeds = lax.all_to_all(speeds, everyone, 0, 0)
    start, start_pack = call(
        functools.partial(start_kernel, nodes=nodes),
        "start_kernel",
        [(blocks.count * width, nz), pack],
        [initial],
        [depth_shape],
    )
    start, start_pack, *parts = lax.optimization_barrier((start, start_pack, *exchanged(parts)))
    turned_field, field, lo, hi, side = call(
        gather_kernel, "gather_kernel", [(nodes,) + part, initial.shape] + edges, parts
    )
    side = beside(side)
    lower, upper = across(lo, hi)
    depth, rates, tile = call(
        first_lanes_kernel,
        "first_lanes_kernel",
        lanes_out,
        [field, turned_field, side, speeds],
        lanes_scratch,
        4_000_000_000,
    )
    turned_field, field, lo, hi, side, first, last, speeds = call(
        first_rows_kernel,
        "first_rows_kernel",
        [(nodes,) + part, initial.shape] + edges + [ghost, ghost, speeds_shape],
        [field, lower, upper, tile, depth, rates, start],
        slabs + [speeds_shape, pltpu.SemaphoreType.DMA],
        2_500_000_000,
        outside=(7,),
    )
    speeds = lax.all_to_all(speeds, everyone, 0, 0)
    before, behind = shifted(last, "node", 1), shifted(first, "node", -1)
    side = beside(side)
    lower, upper = across(lo, hi)
    depth, rates, tile = call(
        second_lanes_kernel,
        "second_lanes_kernel",
        lanes_out,
        [field, turned_field, before, behind, side, speeds],
        [depth_shape, (nodes,) + part] + lanes_scratch,
        4_000_000_000,
    )
    outs = call(
        second_rows_kernel,
        "second_rows_kernel",
        [pack] * nodes,
        [field, lower, upper, tile, depth, rates, start_pack],
        slabs,
        2_500_000_000,
    )
    (states,) = call(
        close_kernel,
        "close_kernel",
        [(1,) + initial.shape],
        exchanged(outs),
        [initial.shape, pltpu.SemaphoreType.DMA((comps,))],
        outside=(0,),
    )
    return states


def solution(mesh):
    return jax.shard_map(
        local,
        mesh=mesh,
        in_specs=(P(None, "gx", "gy", None), P("node", None, "gx", "gy", None)),
        out_specs=P("node", None, "gx", "gy", None),
        check_vma=False,
    )
```

```python
import functools

import jax
import jax.numpy as jnp
from jax import lax
from jax.experimental import pallas as pl
from jax.experimental.pallas import tpu as pltpu
from jax.sharding import PartitionSpec as P

SWEEPS = 2
HALO = 3
COMPONENTS = 5
TILE = 8
CHUNK = 16

heat_ratio = 1.4
step_size = 0.025
density_floor = 0.5
pressure_floor = 0.25
epsilon = 1e-06
radau_weights = [
    [0.112999479323156, -0.040309220723522, 0.025802377420336, -0.009904676507266],
    [0.2343839957474, 0.206892573935359, -0.047857128048541, 0.016047422806516],
    [0.21668178462325, 0.406123263867373, 0.189036518170056, -0.024182104899833],
    [0.220462211176768, 0.388193468843172, 0.32884431998006, 0.0625],
]


def reciprocal(value):
    return pl.reciprocal(value, approx=True)


def primitives(fields):
    inverse = 1.0 / jnp.maximum(fields[0], density_floor)
    velocity = [fields[k] * inverse for k in (1, 2, 3)]
    energy = fields[1] * velocity[0] + fields[2] * velocity[1] + fields[3] * velocity[2]
    pressure = jnp.maximum(0.4 * (fields[4] - 0.5 * energy), pressure_floor)
    return inverse, velocity, pressure


def signal_speeds(fields):
    inverse, velocity, pressure = primitives(fields)
    sound = jnp.sqrt(heat_ratio * pressure * inverse)
    return [jnp.abs(v) + sound for v in velocity]


def half_fluxes(half, speed, half_pressure, direction):
    flux = [half[direction + 1]] + [half[k] * speed for k in (1, 2, 3)]
    flux.append((half[4] + half_pressure) * speed)
    flux[direction + 1] = flux[direction + 1] + half_pressure
    return flux


def halves(fields, directions):
    _, velocity, pressure = primitives(fields)
    half = [0.5 * field for field in fields]
    half_pressure = 0.5 * pressure
    return [half_fluxes(half, velocity[d], half_pressure, d) for d in directions], half


def split(flux, field, alpha):
    signal = alpha * field
    return flux + signal, flux - signal


def cell_terms(below, above):
    second = above - below
    both = below + above
    square = second * second
    middle = 0.25 * (both * both) + ((13.0 / 12.0) * square + epsilon)
    outer = middle + square
    cross = both * second
    return second, outer + cross, middle, outer - cross


def correction(first, middle, last, third_first, third_last):
    ratio_first = middle * reciprocal(first)
    ratio_last = middle * reciprocal(last)
    weight_first = ratio_first * ratio_first
    weight_last = 1.5 * (ratio_last * ratio_last)
    total = (6.0 + weight_first) + (weight_last + weight_last)
    return (weight_first * third_first + weight_last * third_last) * reciprocal(total)


def stream(load, store, count):
    plus, minus, centre = {}, {}, {}
    terms_plus, terms_minus, third_plus, third_minus, interface = {}, {}, {}, {}, {}
    differences_plus, differences_minus = {}, {}
    plus[0], minus[0] = load(0)
    for j in range(1, count + 2 * HALO):
        plus[j], minus[j] = load(j)
        differences_plus[j] = plus[j] - plus[j - 1]
        differences_minus[j] = minus[j] - minus[j - 1]
        cell = j - 1
        if cell < 1:
            continue
        terms_plus[cell] = cell_terms(differences_plus[cell], differences_plus[j])
        terms_minus[cell] = cell_terms(differences_minus[cell], differences_minus[j])
        if 2 <= cell <= count + 3:
            centre[cell] = 6.0 * (plus[cell] + minus[cell]) - (
                terms_plus[cell][0] + terms_minus[cell][0]
            )
        if cell < 2:
            continue
        third_plus[cell] = terms_plus[cell][0] - terms_plus[cell - 1][0]
        third_minus[cell] = terms_minus[cell][0] - terms_minus[cell - 1][0]
        if cell < 4:
            continue
        at = cell - 2
        right = correction(
            terms_plus[at - 1][1], terms_plus[at][2], terms_plus[at + 1][3], third_plus[at], third_plus[at + 1]
        )
        left = correction(
            terms_minus[at + 2][3], terms_minus[at + 1][2], terms_minus[at][1],
            third_minus[at + 2], third_minus[at + 1],
        )
        interface[at] = (third_plus[at + 1] - third_minus[at + 1]) - 4.0 * (right - left)
        if at >= 3:
            store(at - 3, (centre[at - 1] - centre[at + 1]) + (interface[at - 1] - interface[at]))


def lane_index(shape):
    return lax.broadcasted_iota(jnp.int32, shape, len(shape) - 1)


def turned(value, by):
    size = value.shape[-1]
    if isinstance(by, int):
        by = by % size
        return value if by == 0 else pltpu.roll(value, by, value.ndim - 1)
    return pltpu.roll(value, lax.rem(by + 4 * size, size), value.ndim - 1)


def merged(pieces, slot):
    out = pieces[0]
    for number, piece in enumerate(pieces[1:], 1):
        out = jnp.where(slot == number, piece, out)
    return out


def rows_at(start, size):
    return pl.ds(start if isinstance(start, int) else pl.multiple_of(start, TILE), size)


def by_node(me, values):
    out = jnp.float32(values[0])
    for n, value in enumerate(values[1:], 1):
        out = jnp.where(me == n, jnp.float32(value), out)
    return out


def scaled_weight(row, column):
    return radau_weights[row][column] * (step_size / 12.0)


class Blocks:
    def __init__(self, comps, nx, ny, nz):
        self.comps, self.nx, self.ny, self.nz = comps, nx, ny, nz
        self.per = nz // ny
        self.left = nx - self.per
        assert nz % ny == 0 and ny % TILE == 0 and 2 * self.left == self.per
        self.half = nz // 2
        self.count = comps + (comps + 1) // 2

    def message(self, width):
        span = width + 2 * HALO
        rows = self.count * span - (span // 2 if self.comps % 2 else 0)
        return -(-rows // TILE) * TILE

    def lone(self, b):
        return self.comps % 2 == 1 and b == self.count - 1

    def pair(self, b):
        first = 2 * (b - self.comps)
        return first, min(first + 1, self.comps - 1) if isinstance(b, int) else jnp.minimum(first + 1, self.comps - 1)

    def whole(self, ref, c):
        return ref[c, pl.ds(0, self.per)].reshape(self.nz, self.nz)

    def leftovers(self, ref, first, second):
        at = pl.ds(self.per, self.left)
        shape = (self.half, self.nz)
        return jnp.concatenate([ref[first, at].reshape(shape), ref[second, at].reshape(shape)], axis=0)

    def natural(self, ref, b):
        return self.whole(ref, b) if b < self.comps else self.leftovers(ref, *self.pair(b))

    def put_whole(self, ref, c, value):
        ref[c, pl.ds(0, self.per)] = value.reshape(self.per, self.ny, self.nz)

    def put_leftovers(self, ref, b, value):
        at = pl.ds(self.per, self.left)
        shape = (self.left, self.ny, self.nz)
        first, second = self.pair(b)
        ref[second, at] = value[self.half :].reshape(shape)
        ref[first, at] = value[: self.half].reshape(shape)

    def put_natural(self, ref, b, value):
        if b < self.comps:
            self.put_whole(ref, b, value)
        else:
            self.put_leftovers(ref, b, value)

    def row(self, c, i, t):
        if i < self.per:
            return c * self.nz + (i * self.ny + t)
        return (self.comps + c // 2) * self.nz + lax.rem(c, 2) * self.half + ((i - self.per) * self.ny + t)


def depth_fluxes(blocks, read, write):
    comps = blocks.comps
    (flux,), _ = halves([read(c) for c in range(comps)], (2,))
    for c in range(comps):
        write(c, flux[c])
    shared = [read(b) for b in range(comps, blocks.count)]
    fields = [shared[c // 2] if c % 2 == 0 else turned(shared[c // 2], blocks.half) for c in range(comps)]
    (flux,), _ = halves(fields, (2,))
    lower = lane_index(fields[0].shape) < blocks.half
    for b in range(comps, blocks.count):
        first, second = blocks.pair(b)
        write(b, jnp.where(lower, flux[first], turned(flux[second], blocks.half)))


def write_halves(blocks, nodes, rows_ref, zf):
    size = blocks.nz // nodes + 8

    def node(m, carry):
        def read(b):
            return rows_ref[rows_at((m * blocks.count + b) * size, size), :]

        def write(b, flux):
            zf[rows_at((m * blocks.count + b) * size, size), :] = flux

        depth_fluxes(blocks, read, write)
        return carry

    lax.fori_loop(0, nodes, node, 0, unroll=2)


def write_edges(read, nx, ny, comps, lo_ref, hi_ref, side_ref):
    rows = side_ref.shape[1] // (2 * HALO)
    for c in range(comps):
        for i in range(HALO):
            lo_ref[0, pl.ds((c * HALO + i) * ny, ny), :] = read(c, i)
            hi_ref[0, pl.ds((c * HALO + i) * ny, ny), :] = read(c, nx - HALO + i)

    def side(i, carry):
        for c in range(comps):
            value = read(c, i)
            side_ref[0, pl.ds(c * nx + i, HALO, stride=rows), :] = value[ny - HALO :]
            side_ref[0, pl.ds(HALO * rows + c * nx + i, HALO, stride=rows), :] = value[:HALO]
        return carry

    lax.fori_loop(0, nx, side, 0, unroll=4)


def faster(best, read, first, count, comps):
    def step(i, best):
        speeds = signal_speeds([read(c, i) for c in range(comps)])
        return tuple(jnp.maximum(b, s) for b, s in zip(best, speeds))

    return lax.fori_loop(first, first + count, step, best, unroll=4 if count % 4 == 0 else count)


def speed_row(best, width):
    rows = [jnp.max(b, axis=0, keepdims=True) for b in best]
    size = width
    while size > TILE:
        size //= 2
        rows = [jnp.maximum(r, turned(r, -size)) for r in rows]
    rows = [turned(r, TILE * k) for k, r in enumerate(rows)]
    return merged(rows, lane_index(rows[0].shape) % width // TILE)


def speed_tile(row, nodes):
    nz = row.shape[-1]
    width = nz // nodes
    shape = (3 * nodes, nz)
    lane = lane_index(shape)
    place = lax.broadcasted_iota(jnp.int32, shape, 0)
    mine = (lane // width == place % nodes) & (lane % width // TILE == place // nodes)
    spots = jnp.max(jnp.where(mine, row, 0.0), axis=1, keepdims=True)
    group = lane_index((1, nz)) // width
    rows = [merged([spots[k * nodes + m : k * nodes + m + 1] for m in range(nodes)], group) for k in range(3)]
    return jnp.concatenate(rows + [jnp.zeros((TILE - 3, nz), jnp.float32)], axis=0), spots


def send_speeds(row, tiles_ref, out_hbm, sem):
    tiles_ref[...] = jnp.broadcast_to(row[None], tiles_ref.shape)
    copy = pltpu.make_async_copy(tiles_ref, out_hbm, sem)
    copy.start()
    return copy


def open_kernel(u_ref, *refs):
    parts, (speeds_hbm, ring, tiles_ref, sem) = refs[:-4], refs[-4:]
    nodes = len(parts)
    comps, nx, ny, nz = u_ref.shape[1:]
    blocks = Blocks(comps, nx, ny, nz)
    me = lax.axis_index("node")
    best = tuple(jnp.zeros((ny, nz), jnp.float32) for _ in range(3))
    best = faster(best, lambda c, i: u_ref[0, c, i], 0, nx, comps)
    width = nz // nodes
    rows = [jnp.max(b, axis=0, keepdims=True) for b in best]
    rows = [functools.reduce(jnp.maximum, [turned(r, width * k) for k in range(nodes)]) for r in rows]
    row = speed_row(rows, width)
    row = jnp.where(lane_index(row.shape) // width == me, row, 0.0)
    copy = send_speeds(row, tiles_ref, speeds_hbm, sem)
    quarters = [me ^ k for k in range(nodes)]
    for b in range(blocks.count):
        send_quarter(blocks, blocks.natural(u_ref.at[0], b).T, ring, b, parts, quarters, width)
    copy.wait()


def send_quarter(blocks, value, ring_ref, b, parts, quarters, width):
    nz = value.shape[0]
    base = b * (nz + 2 * TILE)
    ring_ref[pl.ds(base + TILE, nz), :] = value
    ring_ref[pl.ds(base, TILE), :] = value[nz - TILE :]
    ring_ref[pl.ds(base + TILE + nz, TILE), :] = value[:TILE]
    span = width + 2 * HALO
    half = span // 2
    for part, quarter in zip(parts, quarters):
        start = base + (TILE - HALO) + quarter * width
        if blocks.lone(b):
            low, high = ring_ref[pl.ds(start, half), :], ring_ref[pl.ds(start + half, half), :]
            lower = lane_index(low.shape) < blocks.half
            part[pl.ds(b * span, half), :] = jnp.where(lower, low, turned(high, blocks.half))
        else:
            part[pl.ds(b * span, span), :] = ring_ref[pl.ds(start, span), :]


def start_kernel(init_ref, rows_ref, pack_ref, turned_ref, *, nodes):
    comps, nx, ny, nz = init_ref.shape
    blocks = Blocks(comps, nx, ny, nz)
    width = nz // nodes
    me = lax.axis_index("node")
    lanes = lane_index((ny, nz)) // width
    for b in range(blocks.count):
        turned_ref[rows_at(b * nz, nz), :] = blocks.natural(init_ref, b).T
        rows_ref[rows_at(b * width, width), :] = turned_ref[rows_at(b * nz + me * width, width), :]

    def step(c, carry):
        for q in range(nx // nodes):
            pieces = [turned(init_ref[c, q * nodes + i], width * i) for i in range(nodes)]
            out = pieces[0]
            for i in range(1, nodes):
                out = jnp.where(lanes == lax.rem(me + i, nodes), pieces[i], out)
            pack_ref[rows_at((c * (nx // nodes) + q) * ny, ny), :] = out
        return carry

    lax.fori_loop(0, comps, step, 0)


def gather_kernel(*refs):
    parts, (rows_ref, nat_ref, lo_ref, hi_ref, side_ref) = refs[:-5], refs[-5:]
    nodes = len(parts)
    comps, nx, ny, nz = nat_ref.shape
    blocks = Blocks(comps, nx, ny, nz)
    width = nz // nodes
    size = width + 8
    me = lax.axis_index("node")
    whole = blocks.count * size
    span = width + 2 * HALO
    half = span // 2
    for k in range(nodes):
        for b in range(blocks.count):
            start = (me ^ k) * whole + b * size
            if blocks.lone(b):
                both = parts[k][pl.ds(b * span, half), :]
                rows_ref[rows_at(start, half), :] = both
                rows_ref[pl.ds(start + half, half), :] = turned(both, blocks.half)
            else:
                rows_ref[rows_at(start, span), :] = parts[k][pl.ds(b * span, span), :]
    for b in range(blocks.count):
        own = [pl.ds(m * whole + b * size + HALO, width) for m in range(nodes)]
        state = jnp.concatenate([rows_ref[at, :] for at in own], axis=0)
        blocks.put_natural(nat_ref, b, state.T)
    write_edges(lambda c, i: nat_ref[c, i], nx, ny, comps, lo_ref, hi_ref, side_ref)


def along_second(nat_ref, side_ref, alpha, fy, yp, ym, gp, gm):
    comps, nx, ny, nz = nat_ref.shape
    rows = gp.shape[0] // (2 * HALO)

    def prepare(fields, place, plus, minus):
        (flux,), half = halves(fields, (1,))
        for c in range(comps):
            at = place(c)
            plus[at, :], minus[at, :] = split(flux[c], half[c], alpha)

    def own(i, carry):
        prepare([nat_ref[c, i] for c in range(comps)], lambda c: rows_at((c * nx + i) * ny, ny), yp, ym)
        return carry

    lax.fori_loop(0, nx, own, 0, unroll=4)

    def ghost(i, carry):
        def place(c):
            return pl.ds(i * rows + c * nx, nx)

        prepare([side_ref[0, place(c), :] for c in range(comps)], place, gp, gm)
        return carry

    lax.fori_loop(0, 2 * HALO, ghost, 0, unroll=HALO)

    def along(b, carry):
        first = pl.multiple_of(b * TILE, TILE)

        def load(j):
            if HALO <= j < HALO + ny:
                at = pl.ds(first * ny + (j - HALO), TILE, stride=ny)
                return yp[at, :], ym[at, :]
            at = pl.ds((j if j < HALO else j - ny) * rows + first, TILE)
            return gp[at, :], gm[at, :]

        def store(i, value):
            fy[pl.ds(i * rows + first, TILE), :] = value

        stream(load, store, ny)
        return carry

    lax.fori_loop(0, rows // TILE, along, 0)


def along_last(blocks, nodes, zf, zu, alphas):
    width = blocks.nz // nodes
    size = width + 8
    each = width // CHUNK

    def along(n, carry):
        m = n // each
        start = m * (blocks.count * size) + lax.rem(n, each) * CHUNK
        alpha = alphas[pl.ds(m * TILE, TILE), :]

        def load(j):
            at = pl.ds(start + j, TILE, stride=size)
            return split(zf[at, :], zu[at, :], alpha)

        def store(i, value):
            zf[pl.ds(start + i, TILE, stride=size), :] = value

        stream(load, store, CHUNK)
        return carry

    lax.fori_loop(0, nodes * each, along, 0)


def block_rates(blocks, nodes, zf, b):
    width = blocks.nz // nodes
    size = width + 8
    return jnp.concatenate([zf[rows_at((m * blocks.count + b) * size, width), :] for m in range(nodes)], axis=0)


def along_first(u, alphas, lo_ref, hi_ref, fy, rate, xp, xm, extra, after):
    comps, nx, ny, nz = rate.shape
    rows = -(-comps * nx // TILE) * TILE
    every = range(comps)

    def prepare(fields, at):
        (flux,), half = halves(fields, (0,))
        for c in every:
            p, m = split(flux[c], half[c], alphas[0])
            xp[at, c * ny : (c + 1) * ny, :] = p
            xm[at, c * ny : (c + 1) * ny, :] = m

    def own(i, carry):
        prepare([u(c, i) for c in every], i + HALO)
        return carry

    lax.fori_loop(0, nx, own, 0, unroll=4)
    for ref, start in ((lo_ref, 0), (hi_ref, nx + HALO)):

        def ghost(i, carry, ref=ref, start=start):
            prepare([ref[0, rows_at((c * HALO + i) * ny, ny), :] for c in every], start + i)
            return carry

        lax.fori_loop(0, HALO, ghost, 0, unroll=HALO)

    def along(c, carry):
        after(jnp.maximum(c - 1, 0))
        for t in range(0, ny, TILE):

            def load(j, t=t):
                at = rows_at(c * ny + t, TILE)
                return xp[j, at, :], xm[j, at, :]

            def store(i, value, t=t):
                value = value + fy[pl.ds(t * rows + c * nx + i, TILE, stride=rows), :]
                rate[c, i, pl.ds(t, TILE), :] = value if extra is None else value + extra(c, i, t)

            stream(load, store, nx)
        return carry

    lax.fori_loop(0, comps, along, 0)
    after(jnp.int32(comps - 1))


def tile_rows(tile):
    return [tile[k : k + 1, :] for k in range(3)]


def speeds_of(al_ref, al_out, alphas, nodes):
    tile, spots = speed_tile(jnp.max(al_ref[...], axis=0)[:1], nodes)
    al_out[...] = tile
    for m in range(nodes):
        at = 2 * nodes + m
        alphas[m * TILE : (m + 1) * TILE, :] = jnp.broadcast_to(spots[at : at + 1], (TILE, tile.shape[-1])) * 0.5
    return tile


def halves_kernel(rows_ref, zf, *, dims, nodes):
    write_halves(Blocks(*dims), nodes, rows_ref, zf)


def first_lanes_kernel(nat_ref, zu, zf_in, side_ref, al_ref, fy, zf, al_out, *scratch, nodes):
    del zf_in
    *scratch, alphas = scratch
    tile = speeds_of(al_ref, al_out, alphas, nodes)
    along_last(Blocks(*nat_ref.shape), nodes, zf, zu, alphas)
    along_second(nat_ref, side_ref, tile[1:2], fy, *scratch)


def second_lanes_kernel(
    nat_ref, before_ref, behind_ref, side_ref, al_ref, fz, fy, al_out, zu, zf, *scratch, nodes
):
    *scratch, alphas = scratch
    blocks = Blocks(*nat_ref.shape)
    nz = blocks.nz
    size = nz // nodes + 8
    width = nz // nodes
    for b in range(blocks.count):
        value = blocks.natural(nat_ref, b).T
        for m in range(nodes):
            ghost = pl.ds((m * blocks.count + b) * 4, HALO)
            start = (m * blocks.count + b) * size
            zu[pl.ds(start, HALO), :] = before_ref[ghost, :]
            zu[pl.ds(start + HALO, width), :] = value[m * width : (m + 1) * width]
            zu[pl.ds(start + HALO + width, HALO), :] = behind_ref[ghost, :]
    write_halves(blocks, nodes, zu, zf)
    tile = speeds_of(al_ref, al_out, alphas, nodes)
    along_last(blocks, nodes, zf, zu, alphas)
    for b in range(blocks.count):
        fz[pl.ds(b * nz, nz), :] = block_rates(blocks, nodes, zf, b).T
    along_second(nat_ref, side_ref, tile[1:2], fy, *scratch)


def first_rows_kernel(nat_in, lo_in, hi_in, al_in, zf, fy, start_ref, *refs, nodes):
    nat_ref, lo_ref, hi_ref, side_ref, first_ref, last_ref, speeds_hbm, rate, xp, xm, tiles_ref, sem = refs
    comps, nx, ny, nz = nat_ref.shape
    blocks = Blocks(comps, nx, ny, nz)
    width = nz // nodes

    def state(value, b):
        rates = value.T + block_rates(blocks, nodes, zf, b)
        start = start_ref[rows_at(b * width, width), :]
        states = []
        for m in range(nodes):
            new = start
            for n in range(nodes):
                new = new + scaled_weight(m, n) * rates[n * width : (n + 1) * width]
            ghost = pl.ds((m * blocks.count + b) * 4, HALO)
            first_ref[ghost, :] = new[:HALO]
            last_ref[ghost, :] = new[width - HALO :]
            states.append(new)
        return jnp.concatenate(states, axis=0).T

    def after(c):
        blocks.put_whole(nat_ref, c, state(blocks.whole(rate, c), c))
        b = blocks.comps + c // 2
        blocks.put_leftovers(nat_ref, b, state(blocks.leftovers(rate, *blocks.pair(b)), b))

    along_first(lambda c, i: nat_in[c, i], tile_rows(al_in), lo_in, hi_in, fy, rate, xp, xm, None, after)

    def read(c, i):
        return nat_ref[c, i]

    best = tuple(jnp.zeros((ny, nz), jnp.float32) for _ in range(3))
    row = speed_row(faster(best, read, 0, nx, comps), width)
    copy = send_speeds(row, tiles_ref, speeds_hbm, sem)
    write_edges(read, nx, ny, comps, lo_ref, hi_ref, side_ref)
    copy.wait()


def second_rows_kernel(nat_ref, lo_ref, hi_ref, al_ref, fz, fy, pack_ref, *refs):
    outs, (rate, xp, xm) = refs[:-3], refs[-3:]
    nodes = len(outs)
    comps, nx, ny, nz = nat_ref.shape
    blocks = Blocks(comps, nx, ny, nz)
    width = nz // nodes
    me = lax.axis_index("node")
    weights = [
        [by_node(me, [scaled_weight(n ^ k, j) for n in range(nodes)]) for j in range(nodes)] for k in range(nodes)
    ]
    lanes = lane_index((TILE, nz)) // width

    def extra(c, i, t):
        return fz[rows_at(blocks.row(c, i, t), TILE), :]

    def after(c):
        for t in range(0, ny, TILE):
            for q in range(nx // nodes):
                at = rows_at((c * (nx // nodes) + q) * ny + t, TILE)
                start = pack_ref[at, :]
                rows = [turned(rate[c, q * nodes + i, pl.ds(t, TILE), :], width * i) for i in range(nodes)]
                rates = [
                    turned(merged([rows[(g - j) % nodes] for g in range(nodes)], lanes), width * (me - j))
                    for j in range(nodes)
                ]
                for k in range(nodes):
                    value = start
                    for j in range(nodes):
                        value = value + weights[k][j] * rates[j]
                    outs[k][at, :] = value

    along_first(lambda c, i: nat_ref[c, i], tile_rows(al_ref), lo_ref, hi_ref, fy, rate, xp, xm, extra, after)


def close_kernel(*refs):
    parts, (out_hbm, out_ref, sems) = refs[:-3], refs[-3:]
    nodes = len(parts)
    comps, nx, ny, nz = out_ref.shape
    width = nz // nodes
    me = lax.axis_index("node")
    lanes = lane_index((ny, nz)) // width
    copies = []
    for c in range(comps):
        for q in range(nx // nodes):
            at = pl.ds((c * (nx // nodes) + q) * ny, ny)
            values = [part[at, :] for part in parts]
            for i in range(nodes):
                out = values[0]
                for k in range(1, nodes):
                    out = jnp.where(lanes == lax.rem((me ^ k) + i, nodes), values[k], out)
                out_ref[c, q * nodes + i] = turned(out, -width * i)
        copies.append(pltpu.make_async_copy(out_ref.at[c], out_hbm.at[0, c], sems.at[c]))
        copies[-1].start()
    for copy in copies:
        copy.wait()


def call(kernel, name, outs, operands, scratch=(), flops=500_000_000, anywhere=False, outside=(), aliases=None):
    vmem, hbm = pl.BlockSpec(memory_space=pltpu.VMEM), pl.BlockSpec(memory_space=pltpu.HBM)
    moved = sum(4 * x.size for x in operands)
    scratch = [pltpu.VMEM(x, jnp.float32) if isinstance(x, tuple) else x for x in scratch]
    return pl.pallas_call(
        kernel,
        out_shape=[jax.ShapeDtypeStruct(shape, jnp.float32) for shape in outs],
        in_specs=[hbm if anywhere else vmem] * len(operands),
        out_specs=[hbm if n in outside else vmem for n in range(len(outs))],
        scratch_shapes=scratch,
        input_output_aliases=aliases or {},
        compiler_params=pltpu.CompilerParams(vmem_limit_bytes=32 * 1024 * 1024),
        cost_estimate=pl.CostEstimate(flops=flops, bytes_accessed=2 * moved, transcendentals=0),
        name=name,
    )(*operands)


def shifted(value, axis, by):
    count = lax.axis_size(axis)
    return lax.ppermute(value, axis, [(i, (i + by) % count) for i in range(count)])


def swapped(value, by):
    return lax.ppermute(value, "node", [(i, i ^ by) for i in range(lax.axis_size("node"))])


def beside(side):
    if lax.axis_size("gy") == 2:
        return shifted(side, "gy", 1)
    half = side.shape[1] // 2
    return jnp.concatenate([shifted(side[:, :half], "gy", 1), shifted(side[:, half:], "gy", -1)], axis=1)


def across(lo, hi):
    return shifted(hi, "gx", 1), shifted(lo, "gx", -1)


def exchanged(parts):
    moved = {k: swapped(parts[k], k) for k in sorted(range(1, len(parts)), reverse=True)}
    return [parts[0]] + [moved[k] for k in range(1, len(parts))]


def local(initial, guesses):
    comps, nx, ny, nz = initial.shape
    nodes = lax.axis_size("node")
    everyone = ("node", "gx", "gy")
    devices = nodes * lax.axis_size("gx") * lax.axis_size("gy")
    rows = -(-comps * nx // TILE) * TILE
    blocks = Blocks(comps, nx, ny, nz)
    width = nz // nodes
    assert blocks.count == TILE and width % CHUNK == 0 and nx % nodes == 0
    edge = (1, comps * HALO * ny, nz)
    edges = [edge, edge, (1, 2 * HALO * rows, nz)]
    tile_shape = (TILE, nz)
    speeds_shape = (devices, TILE, nz)
    part = (blocks.count * (width + 8), nz)
    pack = (comps * nx // nodes * ny, nz)
    ghost = (nodes * blocks.count * 4, nz)
    depth_shape = (blocks.count * nz, nz)
    lanes_scratch = [(ny * rows, nz)] * 2 + [(2 * HALO * rows, nz)] * 2 + [(nodes * TILE, nz)]
    whole = (nodes * part[0], nz)
    slabs = [initial.shape] + [(nx + 2 * HALO, comps * ny, nz)] * 2
    ring = (blocks.count * (nz + 2 * TILE), nz)

    *parts, speeds = call(
        open_kernel,
        "open_kernel",
        [(blocks.message(width), nz)] * nodes + [speeds_shape],
        [guesses],
        [ring, speeds_shape, pltpu.SemaphoreType.DMA],
        outside=(nodes,),
    )
    speeds = lax.all_to_all(speeds, everyone, 0, 0)
    parts = exchanged(parts)
    turned_field, field, lo, hi, side = call(
        gather_kernel, "gather_kernel", [whole, initial.shape] + edges, parts
    )
    side = beside(side)
    lower, upper = across(lo, hi)
    initial, side = lax.optimization_barrier((initial, side))
    start, start_pack = call(
        functools.partial(start_kernel, nodes=nodes),
        "start_kernel",
        [(blocks.count * width, nz), pack],
        [initial],
        [depth_shape],
    )
    (fluxes,) = call(
        functools.partial(halves_kernel, dims=initial.shape, nodes=nodes), "halves_kernel", [whole], [turned_field]
    )
    fluxes, start, start_pack = lax.optimization_barrier((fluxes, start, start_pack))
    rates, depth, tile = call(
        functools.partial(first_lanes_kernel, nodes=nodes),
        "first_lanes_kernel",
        [(ny * rows, nz), whole, tile_shape],
        [field, turned_field, fluxes, side, speeds],
        lanes_scratch,
        4_000_000_000,
        aliases={2: 1},
    )
    field, lo, hi, side, first, last, speeds = call(
        functools.partial(first_rows_kernel, nodes=nodes),
        "first_rows_kernel",
        [initial.shape] + edges + [ghost, ghost, speeds_shape],
        [field, lower, upper, tile, depth, rates, start],
        slabs + [speeds_shape, pltpu.SemaphoreType.DMA],
        2_500_000_000,
        outside=(6,),
        aliases={0: 0, 1: 1, 2: 2},
    )
    speeds = lax.all_to_all(speeds, everyone, 0, 0)
    before, behind = shifted(last, "node", 1), shifted(first, "node", -1)
    side = beside(side)
    lower, upper = across(lo, hi)
    depth, rates, tile = call(
        functools.partial(second_lanes_kernel, nodes=nodes),
        "second_lanes_kernel",
        [depth_shape, (ny * rows, nz), tile_shape],
        [field, before, behind, side, speeds],
        [whole, whole] + lanes_scratch,
        4_000_000_000,
    )
    outs = call(
        second_rows_kernel,
        "second_rows_kernel",
        [pack] * nodes,
        [field, lower, upper, tile, depth, rates, start_pack],
        slabs,
        2_500_000_000,
    )
    (states,) = call(
        close_kernel,
        "close_kernel",
        [(1,) + initial.shape],
        exchanged(outs),
        [initial.shape, pltpu.SemaphoreType.DMA((comps,))],
        outside=(0,),
    )
    return states


def solution(mesh):
    return jax.shard_map(
        local,
        mesh=mesh,
        in_specs=(P(None, "gx", "gy", None), P("node", None, "gx", "gy", None)),
        out_specs=P("node", None, "gx", "gy", None),
        check_vma=False,
    )
```

```python
import functools

import jax
import jax.numpy as jnp
from jax import lax
from jax.experimental import pallas as pl
from jax.experimental.pallas import tpu as pltpu
from jax.sharding import PartitionSpec as P

SWEEPS = 2
HALO = 3
COMPONENTS = 5
TILE = 8
CHUNK = 16

heat_ratio = 1.4
step_size = 0.025
density_floor = 0.5
pressure_floor = 0.25
epsilon = 1e-06
radau_weights = [
    [0.112999479323156, -0.040309220723522, 0.025802377420336, -0.009904676507266],
    [0.2343839957474, 0.206892573935359, -0.047857128048541, 0.016047422806516],
    [0.21668178462325, 0.406123263867373, 0.189036518170056, -0.024182104899833],
    [0.220462211176768, 0.388193468843172, 0.32884431998006, 0.0625],
]


def reciprocal(value):
    return pl.reciprocal(value, approx=True)


def primitives(fields):
    inverse = 1.0 / jnp.maximum(fields[0], density_floor)
    velocity = [fields[k] * inverse for k in (1, 2, 3)]
    energy = fields[1] * velocity[0] + fields[2] * velocity[1] + fields[3] * velocity[2]
    pressure = jnp.maximum(0.4 * (fields[4] - 0.5 * energy), pressure_floor)
    return inverse, velocity, pressure


def signal_speeds(fields):
    inverse, velocity, pressure = primitives(fields)
    sound = jnp.sqrt(heat_ratio * pressure * inverse)
    return [jnp.abs(v) + sound for v in velocity]


def half_fluxes(half, speed, half_pressure, direction):
    flux = [half[direction + 1]] + [half[k] * speed for k in (1, 2, 3)]
    flux.append((half[4] + half_pressure) * speed)
    flux[direction + 1] = flux[direction + 1] + half_pressure
    return flux


def halves(fields, directions):
    _, velocity, pressure = primitives(fields)
    half = [0.5 * field for field in fields]
    half_pressure = 0.5 * pressure
    return [half_fluxes(half, velocity[d], half_pressure, d) for d in directions], half


def split(flux, field, alpha):
    signal = alpha * field
    return flux + signal, flux - signal


def cell_terms(below, above):
    second = above - below
    both = below + above
    square = second * second
    middle = 0.25 * (both * both) + ((13.0 / 12.0) * square + epsilon)
    outer = middle + square
    cross = both * second
    return second, outer + cross, middle, outer - cross


def correction(first, middle, last, third_first, third_last):
    ratio_first = middle * reciprocal(first)
    ratio_last = middle * reciprocal(last)
    weight_first = ratio_first * ratio_first
    weight_last = 1.5 * (ratio_last * ratio_last)
    total = (6.0 + weight_first) + (weight_last + weight_last)
    return (weight_first * third_first + weight_last * third_last) * reciprocal(total)


def stream(load, store, count):
    plus, minus, centre = {}, {}, {}
    terms_plus, terms_minus, third_plus, third_minus, interface = {}, {}, {}, {}, {}
    differences_plus, differences_minus = {}, {}
    plus[0], minus[0] = load(0)
    for j in range(1, count + 2 * HALO):
        plus[j], minus[j] = load(j)
        differences_plus[j] = plus[j] - plus[j - 1]
        differences_minus[j] = minus[j] - minus[j - 1]
        cell = j - 1
        if cell < 1:
            continue
        terms_plus[cell] = cell_terms(differences_plus[cell], differences_plus[j])
        terms_minus[cell] = cell_terms(differences_minus[cell], differences_minus[j])
        if 2 <= cell <= count + 3:
            centre[cell] = 6.0 * (plus[cell] + minus[cell]) - (
                terms_plus[cell][0] + terms_minus[cell][0]
            )
        if cell < 2:
            continue
        third_plus[cell] = terms_plus[cell][0] - terms_plus[cell - 1][0]
        third_minus[cell] = terms_minus[cell][0] - terms_minus[cell - 1][0]
        if cell < 4:
            continue
        at = cell - 2
        right = correction(
            terms_plus[at - 1][1], terms_plus[at][2], terms_plus[at + 1][3], third_plus[at], third_plus[at + 1]
        )
        left = correction(
            terms_minus[at + 2][3], terms_minus[at + 1][2], terms_minus[at][1],
            third_minus[at + 2], third_minus[at + 1],
        )
        interface[at] = (third_plus[at + 1] - third_minus[at + 1]) - 4.0 * (right - left)
        if at >= 3:
            store(at - 3, (centre[at - 1] - centre[at + 1]) + (interface[at - 1] - interface[at]))


def lane_index(shape):
    return lax.broadcasted_iota(jnp.int32, shape, len(shape) - 1)


def turned(value, by):
    size = value.shape[-1]
    if isinstance(by, int):
        by = by % size
        return value if by == 0 else pltpu.roll(value, by, value.ndim - 1)
    return pltpu.roll(value, lax.rem(by + 4 * size, size), value.ndim - 1)


def merged(pieces, slot):
    out = pieces[0]
    for number, piece in enumerate(pieces[1:], 1):
        out = jnp.where(slot == number, piece, out)
    return out


def rows_at(start, size):
    return pl.ds(start if isinstance(start, int) else pl.multiple_of(start, TILE), size)


def by_node(me, values):
    out = jnp.float32(values[0])
    for n, value in enumerate(values[1:], 1):
        out = jnp.where(me == n, jnp.float32(value), out)
    return out


def scaled_weight(row, column):
    return radau_weights[row][column] * (step_size / 12.0)


class Blocks:
    def __init__(self, comps, nx, ny, nz):
        self.comps, self.nx, self.ny, self.nz = comps, nx, ny, nz
        self.per = nz // ny
        self.left = nx - self.per
        assert nz % ny == 0 and ny % TILE == 0 and 2 * self.left == self.per
        self.half = nz // 2
        self.count = comps + (comps + 1) // 2

    def message(self, width):
        span = width + 2 * HALO
        rows = self.count * span - (span // 2 if self.comps % 2 else 0)
        return -(-rows // TILE) * TILE

    def lone(self, b):
        return self.comps % 2 == 1 and b == self.count - 1

    def pair(self, b):
        first = 2 * (b - self.comps)
        return first, min(first + 1, self.comps - 1) if isinstance(b, int) else jnp.minimum(first + 1, self.comps - 1)

    def whole(self, ref, c):
        return ref[c, pl.ds(0, self.per)].reshape(self.nz, self.nz)

    def leftovers(self, ref, first, second):
        at = pl.ds(self.per, self.left)
        shape = (self.half, self.nz)
        return jnp.concatenate([ref[first, at].reshape(shape), ref[second, at].reshape(shape)], axis=0)

    def natural(self, ref, b):
        return self.whole(ref, b) if b < self.comps else self.leftovers(ref, *self.pair(b))

    def put_whole(self, ref, c, value):
        ref[c, pl.ds(0, self.per)] = value.reshape(self.per, self.ny, self.nz)

    def put_leftovers(self, ref, b, value):
        at = pl.ds(self.per, self.left)
        shape = (self.left, self.ny, self.nz)
        first, second = self.pair(b)
        ref[second, at] = value[self.half :].reshape(shape)
        ref[first, at] = value[: self.half].reshape(shape)

    def put_natural(self, ref, b, value):
        if b < self.comps:
            self.put_whole(ref, b, value)
        else:
            self.put_leftovers(ref, b, value)

    def row(self, c, i, t):
        if i < self.per:
            return c * self.nz + (i * self.ny + t)
        return (self.comps + c // 2) * self.nz + (c % 2) * self.half + ((i - self.per) * self.ny + t)


def depth_fluxes(blocks, read, write):
    comps = blocks.comps
    (flux,), _ = halves([read(c) for c in range(comps)], (2,))
    for c in range(comps):
        write(c, flux[c])
    shared = [read(b) for b in range(comps, blocks.count)]
    fields = [shared[c // 2] if c % 2 == 0 else turned(shared[c // 2], blocks.half) for c in range(comps)]
    (flux,), _ = halves(fields, (2,))
    lower = lane_index(fields[0].shape) < blocks.half
    for b in range(comps, blocks.count):
        first, second = blocks.pair(b)
        write(b, jnp.where(lower, flux[first], turned(flux[second], blocks.half)))


def write_halves(blocks, nodes, rows_ref, zf):
    size = blocks.nz // nodes + 8

    def node(m, carry):
        def read(b):
            return rows_ref[rows_at((m * blocks.count + b) * size, size), :]

        def write(b, flux):
            zf[rows_at((m * blocks.count + b) * size, size), :] = flux

        depth_fluxes(blocks, read, write)
        return carry

    lax.fori_loop(0, nodes, node, 0, unroll=True)


def write_edges(read, nx, ny, comps, lo_ref, hi_ref, side_ref):
    rows = side_ref.shape[1] // (2 * HALO)
    for c in range(comps):
        for i in range(HALO):
            lo_ref[0, pl.ds((c * HALO + i) * ny, ny), :] = read(c, i)
            hi_ref[0, pl.ds((c * HALO + i) * ny, ny), :] = read(c, nx - HALO + i)

    def side(i, carry):
        for c in range(comps):
            value = read(c, i)
            side_ref[0, pl.ds(c * nx + i, HALO, stride=rows), :] = value[ny - HALO :]
            side_ref[0, pl.ds(HALO * rows + c * nx + i, HALO, stride=rows), :] = value[:HALO]
        return carry

    lax.fori_loop(0, nx, side, 0, unroll=4)


def faster(best, read, first, count, comps):
    def step(i, best):
        speeds = signal_speeds([read(c, i) for c in range(comps)])
        return tuple(jnp.maximum(b, s) for b, s in zip(best, speeds))

    return lax.fori_loop(first, first + count, step, best, unroll=True)


def speed_row(best, width):
    rows = [jnp.max(b, axis=0, keepdims=True) for b in best]
    size = width
    while size > TILE:
        size //= 2
        rows = [jnp.maximum(r, turned(r, -size)) for r in rows]
    rows = [turned(r, TILE * k) for k, r in enumerate(rows)]
    return merged(rows, lane_index(rows[0].shape) % width // TILE)


def speed_tile(row, nodes):
    nz = row.shape[-1]
    width = nz // nodes
    shape = (3 * nodes, nz)
    lane = lane_index(shape)
    place = lax.broadcasted_iota(jnp.int32, shape, 0)
    mine = (lane // width == place % nodes) & (lane % width // TILE == place // nodes)
    spots = jnp.max(jnp.where(mine, row, 0.0), axis=1, keepdims=True)
    group = lane_index((1, nz)) // width
    rows = [merged([spots[k * nodes + m : k * nodes + m + 1] for m in range(nodes)], group) for k in range(3)]
    return jnp.concatenate(rows + [jnp.zeros((TILE - 3, nz), jnp.float32)], axis=0), spots


def send_speeds(row, tiles_ref, out_hbm, sem):
    tiles_ref[...] = jnp.broadcast_to(row[None], tiles_ref.shape)
    copy = pltpu.make_async_copy(tiles_ref, out_hbm, sem)
    copy.start()
    return copy


def open_kernel(u_ref, *refs):
    parts, (speeds_hbm, ring, tiles_ref, sem) = refs[:-4], refs[-4:]
    nodes = len(parts)
    comps, nx, ny, nz = u_ref.shape[1:]
    blocks = Blocks(comps, nx, ny, nz)
    me = lax.axis_index("node")
    best = tuple(jnp.zeros((ny, nz), jnp.float32) for _ in range(3))
    best = faster(best, lambda c, i: u_ref[0, c, i], 0, nx, comps)
    width = nz // nodes
    rows = [jnp.max(b, axis=0, keepdims=True) for b in best]
    rows = [functools.reduce(jnp.maximum, [turned(r, width * k) for k in range(nodes)]) for r in rows]
    row = speed_row(rows, width)
    row = jnp.where(lane_index(row.shape) // width == me, row, 0.0)
    copy = send_speeds(row, tiles_ref, speeds_hbm, sem)
    quarters = [me ^ k for k in range(nodes)]
    for b in range(blocks.count):
        send_quarter(blocks, blocks.natural(u_ref.at[0], b).T, ring, b, parts, quarters, width)
    copy.wait()


def send_quarter(blocks, value, ring_ref, b, parts, quarters, width):
    nz = value.shape[0]
    base = b * (nz + 2 * TILE)
    ring_ref[pl.ds(base + TILE, nz), :] = value
    ring_ref[pl.ds(base, TILE), :] = value[nz - TILE :]
    ring_ref[pl.ds(base + TILE + nz, TILE), :] = value[:TILE]
    span = width + 2 * HALO
    half = span // 2
    for part, quarter in zip(parts, quarters):
        start = base + (TILE - HALO) + quarter * width
        if blocks.lone(b):
            low, high = ring_ref[pl.ds(start, half), :], ring_ref[pl.ds(start + half, half), :]
            lower = lane_index(low.shape) < blocks.half
            part[pl.ds(b * span, half), :] = jnp.where(lower, low, turned(high, blocks.half))
        else:
            part[pl.ds(b * span, span), :] = ring_ref[pl.ds(start, span), :]


def start_kernel(init_ref, rows_ref, pack_ref, turned_ref, *, nodes):
    comps, nx, ny, nz = init_ref.shape
    blocks = Blocks(comps, nx, ny, nz)
    width = nz // nodes
    me = lax.axis_index("node")
    lanes = lane_index((ny, nz)) // width
    for b in range(blocks.count):
        turned_ref[rows_at(b * nz, nz), :] = blocks.natural(init_ref, b).T
        rows_ref[rows_at(b * width, width), :] = turned_ref[rows_at(b * nz + me * width, width), :]

    def step(c, carry):
        for q in range(nx // nodes):
            pieces = [turned(init_ref[c, q * nodes + i], width * i) for i in range(nodes)]
            out = pieces[0]
            for i in range(1, nodes):
                out = jnp.where(lanes == lax.rem(me + i, nodes), pieces[i], out)
            pack_ref[rows_at((c * (nx // nodes) + q) * ny, ny), :] = out
        return carry

    lax.fori_loop(0, comps, step, 0)


def gather_kernel(*refs):
    parts, (rows_ref, nat_ref, lo_ref, hi_ref, side_ref) = refs[:-5], refs[-5:]
    nodes = len(parts)
    comps, nx, ny, nz = nat_ref.shape
    blocks = Blocks(comps, nx, ny, nz)
    width = nz // nodes
    size = width + 8
    me = lax.axis_index("node")
    whole = blocks.count * size
    span = width + 2 * HALO
    half = span // 2
    for k in range(nodes):
        for b in range(blocks.count):
            start = (me ^ k) * whole + b * size
            if blocks.lone(b):
                both = parts[k][pl.ds(b * span, half), :]
                rows_ref[rows_at(start, half), :] = both
                rows_ref[pl.ds(start + half, half), :] = turned(both, blocks.half)
            else:
                rows_ref[rows_at(start, span), :] = parts[k][pl.ds(b * span, span), :]
    for b in range(blocks.count):
        own = [pl.ds(m * whole + b * size + HALO, width) for m in range(nodes)]
        state = jnp.concatenate([rows_ref[at, :] for at in own], axis=0)
        blocks.put_natural(nat_ref, b, state.T)
    write_edges(lambda c, i: nat_ref[c, i], nx, ny, comps, lo_ref, hi_ref, side_ref)


def along_second(nat_ref, side_ref, alpha, fy, yp, ym, gp, gm, beside=None):
    comps, nx, ny, nz = nat_ref.shape
    rows = gp.shape[0] // (2 * HALO)

    def prepare(fields, place, plus, minus):
        (flux,), half = halves(fields, (1,))
        for c in range(comps):
            at = place(c)
            plus[at, :], minus[at, :] = split(flux[c], half[c], alpha)

    def own(i, carry):
        prepare([nat_ref[c, i] for c in range(comps)], lambda c: rows_at((c * nx + i) * ny, ny), yp, ym)
        return carry

    lax.fori_loop(0, nx, own, 0, unroll=4)

    def ghost(i, carry):
        def place(c):
            return pl.ds(i * rows + c * nx, nx)

        prepare([side_ref[0, place(c), :] for c in range(comps)], place, gp, gm)
        return carry

    lax.fori_loop(0, 2 * HALO, ghost, 0, unroll=HALO)

    def along(b, carry):
        first = pl.multiple_of(b * TILE, TILE)

        def load(j):
            if HALO <= j < HALO + ny:
                at = pl.ds(first * ny + (j - HALO), TILE, stride=ny)
                return yp[at, :], ym[at, :]
            at = pl.ds((j if j < HALO else j - ny) * rows + first, TILE)
            return gp[at, :], gm[at, :]

        def store(i, value):
            fy[pl.ds(i * rows + first, TILE), :] = value

        if beside is not None:
            beside(b)
        stream(load, store, ny)
        return carry

    lax.fori_loop(0, rows // TILE, along, 0)


def along_last(blocks, nodes, zf, zu, alphas):
    width = blocks.nz // nodes
    size = width + 8
    each = width // CHUNK

    def along(n, carry):
        m = n // each
        start = m * (blocks.count * size) + lax.rem(n, each) * CHUNK
        alpha = alphas[pl.ds(m * TILE, TILE), :]

        def load(j):
            at = pl.ds(start + j, TILE, stride=size)
            return split(zf[at, :], zu[at, :], alpha)

        def store(i, value):
            zf[pl.ds(start + i, TILE, stride=size), :] = value

        stream(load, store, CHUNK)
        return carry

    lax.fori_loop(0, nodes * each, along, 0)


def block_rates(blocks, nodes, zf, b):
    width = blocks.nz // nodes
    size = width + 8
    return jnp.concatenate([zf[rows_at((m * blocks.count + b) * size, width), :] for m in range(nodes)], axis=0)


def along_first(u, alphas, lo_ref, hi_ref, fy, rate, xp, xm, extra, after, unrolled=False):
    comps, nx, ny, nz = rate.shape
    rows = -(-comps * nx // TILE) * TILE
    every = range(comps)

    def prepare(fields, at):
        (flux,), half = halves(fields, (0,))
        for c in every:
            p, m = split(flux[c], half[c], alphas[0])
            xp[at, c * ny : (c + 1) * ny, :] = p
            xm[at, c * ny : (c + 1) * ny, :] = m

    def own(i, carry):
        prepare([u(c, i) for c in every], i + HALO)
        return carry

    lax.fori_loop(0, nx, own, 0, unroll=4)
    for ref, start in ((lo_ref, 0), (hi_ref, nx + HALO)):

        def ghost(i, carry, ref=ref, start=start):
            prepare([ref[0, rows_at((c * HALO + i) * ny, ny), :] for c in every], start + i)
            return carry

        lax.fori_loop(0, HALO, ghost, 0, unroll=HALO)

    def component(c):
        for t in range(0, ny, TILE):

            def load(j, t=t):
                at = rows_at(c * ny + t, TILE)
                return xp[j, at, :], xm[j, at, :]

            def store(i, value, t=t):
                value = value + fy[pl.ds(t * rows + c * nx + i, TILE, stride=rows), :]
                rate[c, i, pl.ds(t, TILE), :] = value if extra is None else value + extra(c, i, t)

            stream(load, store, nx)

    def along(c, carry):
        after(jnp.maximum(c - 1, 0))
        component(c)
        return carry

    if unrolled:
        for c in every:
            if c:
                after(c - 1)
            component(c)
        after(comps - 1)
    else:
        lax.fori_loop(0, comps, along, 0)
        after(jnp.int32(comps - 1))


def tile_rows(tile):
    return [tile[k : k + 1, :] for k in range(3)]


def speeds_of(al_ref, al_out, alphas, nodes):
    tile, spots = speed_tile(jnp.max(al_ref[...], axis=0)[:1], nodes)
    al_out[...] = tile
    for m in range(nodes):
        at = 2 * nodes + m
        alphas[m * TILE : (m + 1) * TILE, :] = jnp.broadcast_to(spots[at : at + 1], (TILE, tile.shape[-1])) * 0.5
    return tile


def halves_kernel(rows_ref, zf, *, dims, nodes):
    write_halves(Blocks(*dims), nodes, rows_ref, zf)


def first_lanes_kernel(nat_ref, zu, zf_in, side_ref, al_ref, fy, zf, al_out, *scratch, nodes):
    del zf_in
    *scratch, alphas = scratch
    tile = speeds_of(al_ref, al_out, alphas, nodes)
    along_last(Blocks(*nat_ref.shape), nodes, zf, zu, alphas)
    along_second(nat_ref, side_ref, tile[1:2], fy, *scratch)


def second_lanes_kernel(
    nat_ref, before_ref, behind_ref, side_ref, al_ref, fz, fy, al_out, zu, zf, *scratch, nodes
):
    *scratch, alphas = scratch
    blocks = Blocks(*nat_ref.shape)
    nz = blocks.nz
    size = nz // nodes + 8
    width = nz // nodes
    for b in range(blocks.count):
        value = blocks.natural(nat_ref, b).T
        for m in range(nodes):
            ghost = pl.ds((m * blocks.count + b) * 4, HALO)
            start = (m * blocks.count + b) * size
            zu[pl.ds(start, HALO), :] = before_ref[ghost, :]
            zu[pl.ds(start + HALO, width), :] = value[m * width : (m + 1) * width]
            zu[pl.ds(start + HALO + width, HALO), :] = behind_ref[ghost, :]
    write_halves(blocks, nodes, zu, zf)
    tile = speeds_of(al_ref, al_out, alphas, nodes)
    along_last(blocks, nodes, zf, zu, alphas)

    def turn(b):
        fz[rows_at(b * nz, nz), :] = block_rates(blocks, nodes, zf, b).T

    assert blocks.count == scratch[2].shape[0] // (2 * HALO) // TILE
    along_second(nat_ref, side_ref, tile[1:2], fy, *scratch, beside=turn)


def first_rows_kernel(nat_in, lo_in, hi_in, al_in, zf, fy, start_ref, *refs, nodes):
    nat_ref, lo_ref, hi_ref, side_ref, first_ref, last_ref, speeds_hbm, rate, xp, xm, tiles_ref, sem = refs
    comps, nx, ny, nz = nat_ref.shape
    blocks = Blocks(comps, nx, ny, nz)
    width = nz // nodes

    def state(value, b):
        rates = value.T + block_rates(blocks, nodes, zf, b)
        start = start_ref[rows_at(b * width, width), :]
        states = []
        for m in range(nodes):
            new = start
            for n in range(nodes):
                new = new + scaled_weight(m, n) * rates[n * width : (n + 1) * width]
            ghost = pl.ds((m * blocks.count + b) * 4, HALO)
            first_ref[ghost, :] = new[:HALO]
            last_ref[ghost, :] = new[width - HALO :]
            states.append(new)
        return jnp.concatenate(states, axis=0).T

    def after(c):
        blocks.put_whole(nat_ref, c, state(blocks.whole(rate, c), c))
        if c % 2 == 1 or c == comps - 1:
            b = comps + c // 2
            blocks.put_leftovers(nat_ref, b, state(blocks.leftovers(rate, *blocks.pair(b)), b))

    along_first(lambda c, i: nat_in[c, i], tile_rows(al_in), lo_in, hi_in, fy, rate, xp, xm, None, after, True)

    def read(c, i):
        return nat_ref[c, i]

    best = tuple(jnp.zeros((ny, nz), jnp.float32) for _ in range(3))
    row = speed_row(faster(best, read, 0, nx, comps), width)
    copy = send_speeds(row, tiles_ref, speeds_hbm, sem)
    write_edges(read, nx, ny, comps, lo_ref, hi_ref, side_ref)
    copy.wait()


def second_rows_kernel(nat_ref, lo_ref, hi_ref, al_ref, fz, fy, pack_ref, *refs):
    outs, (rate, xp, xm) = refs[:-3], refs[-3:]
    nodes = len(outs)
    comps, nx, ny, nz = nat_ref.shape
    blocks = Blocks(comps, nx, ny, nz)
    width = nz // nodes
    me = lax.axis_index("node")
    weights = [
        [by_node(me, [scaled_weight(n ^ k, j) for n in range(nodes)]) for j in range(nodes)] for k in range(nodes)
    ]
    lanes = lane_index((TILE, nz)) // width

    def extra(c, i, t):
        return fz[rows_at(blocks.row(c, i, t), TILE), :]

    def after(c):
        for t in range(0, ny, TILE):
            for q in range(nx // nodes):
                at = rows_at((c * (nx // nodes) + q) * ny + t, TILE)
                start = pack_ref[at, :]
                rows = [turned(rate[c, q * nodes + i, pl.ds(t, TILE), :], width * i) for i in range(nodes)]
                rates = [
                    turned(merged([rows[(g - j) % nodes] for g in range(nodes)], lanes), width * (me - j))
                    for j in range(nodes)
                ]
                for k in range(nodes):
                    value = start
                    for j in range(nodes):
                        value = value + weights[k][j] * rates[j]
                    outs[k][at, :] = value

    along_first(lambda c, i: nat_ref[c, i], tile_rows(al_ref), lo_ref, hi_ref, fy, rate, xp, xm, extra, after, True)


def close_kernel(*refs):
    parts, (out_hbm, out_ref, sems) = refs[:-3], refs[-3:]
    nodes = len(parts)
    comps, nx, ny, nz = out_ref.shape
    width = nz // nodes
    me = lax.axis_index("node")
    lanes = lane_index((ny, nz)) // width
    copies = []
    for c in range(comps):
        for q in range(nx // nodes):
            at = pl.ds((c * (nx // nodes) + q) * ny, ny)
            values = [part[at, :] for part in parts]
            for i in range(nodes):
                out = values[0]
                for k in range(1, nodes):
                    out = jnp.where(lanes == lax.rem((me ^ k) + i, nodes), values[k], out)
                out_ref[c, q * nodes + i] = turned(out, -width * i)
        copies.append(pltpu.make_async_copy(out_ref.at[c], out_hbm.at[0, c], sems.at[c]))
        copies[-1].start()
    for copy in copies:
        copy.wait()


def call(kernel, name, outs, operands, scratch=(), flops=500_000_000, anywhere=False, outside=(), aliases=None):
    vmem, hbm = pl.BlockSpec(memory_space=pltpu.VMEM), pl.BlockSpec(memory_space=pltpu.HBM)
    moved = sum(4 * x.size for x in operands)
    scratch = [pltpu.VMEM(x, jnp.float32) if isinstance(x, tuple) else x for x in scratch]
    return pl.pallas_call(
        kernel,
        out_shape=[jax.ShapeDtypeStruct(shape, jnp.float32) for shape in outs],
        in_specs=[hbm if anywhere else vmem] * len(operands),
        out_specs=[hbm if n in outside else vmem for n in range(len(outs))],
        scratch_shapes=scratch,
        input_output_aliases=aliases or {},
        compiler_params=pltpu.CompilerParams(vmem_limit_bytes=32 * 1024 * 1024),
        cost_estimate=pl.CostEstimate(flops=flops, bytes_accessed=2 * moved, transcendentals=0),
        name=name,
    )(*operands)


def shifted(value, axis, by):
    count = lax.axis_size(axis)
    return lax.ppermute(value, axis, [(i, (i + by) % count) for i in range(count)])


def swapped(value, by):
    return lax.ppermute(value, "node", [(i, i ^ by) for i in range(lax.axis_size("node"))])


def beside(side):
    if lax.axis_size("gy") == 2:
        return shifted(side, "gy", 1)
    half = side.shape[1] // 2
    return jnp.concatenate([shifted(side[:, :half], "gy", 1), shifted(side[:, half:], "gy", -1)], axis=1)


def across(lo, hi):
    return shifted(hi, "gx", 1), shifted(lo, "gx", -1)


def exchanged(parts):
    moved = {k: swapped(parts[k], k) for k in sorted(range(1, len(parts)), reverse=True)}
    return [parts[0]] + [moved[k] for k in range(1, len(parts))]


def local(initial, guesses):
    comps, nx, ny, nz = initial.shape
    nodes = lax.axis_size("node")
    everyone = ("node", "gx", "gy")
    devices = nodes * lax.axis_size("gx") * lax.axis_size("gy")
    rows = -(-comps * nx // TILE) * TILE
    blocks = Blocks(comps, nx, ny, nz)
    width = nz // nodes
    assert blocks.count == TILE and width % CHUNK == 0 and nx % nodes == 0
    edge = (1, comps * HALO * ny, nz)
    edges = [edge, edge, (1, 2 * HALO * rows, nz)]
    tile_shape = (TILE, nz)
    speeds_shape = (devices, TILE, nz)
    part = (blocks.count * (width + 8), nz)
    pack = (comps * nx // nodes * ny, nz)
    ghost = (nodes * blocks.count * 4, nz)
    depth_shape = (blocks.count * nz, nz)
    lanes_scratch = [(ny * rows, nz)] * 2 + [(2 * HALO * rows, nz)] * 2 + [(nodes * TILE, nz)]
    whole = (nodes * part[0], nz)
    slabs = [initial.shape] + [(nx + 2 * HALO, comps * ny, nz)] * 2
    ring = (blocks.count * (nz + 2 * TILE), nz)

    *parts, speeds = call(
        open_kernel,
        "open_kernel",
        [(blocks.message(width), nz)] * nodes + [speeds_shape],
        [guesses],
        [ring, speeds_shape, pltpu.SemaphoreType.DMA],
        outside=(nodes,),
    )
    speeds = lax.all_to_all(speeds, everyone, 0, 0)
    parts = exchanged(parts)
    turned_field, field, lo, hi, side = call(
        gather_kernel, "gather_kernel", [whole, initial.shape] + edges, parts
    )
    side = beside(side)
    lower, upper = across(lo, hi)
    initial, side = lax.optimization_barrier((initial, side))
    start, start_pack = call(
        functools.partial(start_kernel, nodes=nodes),
        "start_kernel",
        [(blocks.count * width, nz), pack],
        [initial],
        [depth_shape],
    )
    (fluxes,) = call(
        functools.partial(halves_kernel, dims=initial.shape, nodes=nodes), "halves_kernel", [whole], [turned_field]
    )
    fluxes, start, start_pack = lax.optimization_barrier((fluxes, start, start_pack))
    rates, depth, tile = call(
        functools.partial(first_lanes_kernel, nodes=nodes),
        "first_lanes_kernel",
        [(ny * rows, nz), whole, tile_shape],
        [field, turned_field, fluxes, side, speeds],
        lanes_scratch,
        4_000_000_000,
        aliases={2: 1},
    )
    field, lo, hi, side, first, last, speeds = call(
        functools.partial(first_rows_kernel, nodes=nodes),
        "first_rows_kernel",
        [initial.shape] + edges + [ghost, ghost, speeds_shape],
        [field, lower, upper, tile, depth, rates, start],
        slabs + [speeds_shape, pltpu.SemaphoreType.DMA],
        2_500_000_000,
        outside=(6,),
        aliases={0: 0, 1: 1, 2: 2},
    )
    speeds = lax.all_to_all(speeds, everyone, 0, 0)
    before, behind = shifted(last, "node", 1), shifted(first, "node", -1)
    side = beside(side)
    lower, upper = across(lo, hi)
    depth, rates, tile = call(
        functools.partial(second_lanes_kernel, nodes=nodes),
        "second_lanes_kernel",
        [depth_shape, (ny * rows, nz), tile_shape],
        [field, before, behind, side, speeds],
        [whole, whole] + lanes_scratch,
        4_000_000_000,
    )
    outs = call(
        second_rows_kernel,
        "second_rows_kernel",
        [pack] * nodes,
        [field, lower, upper, tile, depth, rates, start_pack],
        slabs,
        2_500_000_000,
    )
    (states,) = call(
        close_kernel,
        "close_kernel",
        [(1,) + initial.shape],
        exchanged(outs),
        [initial.shape, pltpu.SemaphoreType.DMA((comps,))],
        outside=(0,),
    )
    return states


def solution(mesh):
    return jax.shard_map(
        local,
        mesh=mesh,
        in_specs=(P(None, "gx", "gy", None), P("node", None, "gx", "gy", None)),
        out_specs=P("node", None, "gx", "gy", None),
        check_vma=False,
    )
```

```python
import functools

import jax
import jax.numpy as jnp
from jax import lax
from jax.experimental import pallas as pl
from jax.experimental.pallas import tpu as pltpu
from jax.sharding import PartitionSpec as P

SWEEPS = 2
HALO = 3
COMPONENTS = 5
TILE = 8
CHUNK = 16

heat_ratio = 1.4
step_size = 0.025
density_floor = 0.5
pressure_floor = 0.25
epsilon = 1e-06
radau_weights = [
    [0.112999479323156, -0.040309220723522, 0.025802377420336, -0.009904676507266],
    [0.2343839957474, 0.206892573935359, -0.047857128048541, 0.016047422806516],
    [0.21668178462325, 0.406123263867373, 0.189036518170056, -0.024182104899833],
    [0.220462211176768, 0.388193468843172, 0.32884431998006, 0.0625],
]


def reciprocal(value):
    return pl.reciprocal(value, approx=True)


def primitives(fields):
    inverse = 1.0 / jnp.maximum(fields[0], density_floor)
    velocity = [fields[k] * inverse for k in (1, 2, 3)]
    energy = fields[1] * velocity[0] + fields[2] * velocity[1] + fields[3] * velocity[2]
    pressure = jnp.maximum(0.4 * (fields[4] - 0.5 * energy), pressure_floor)
    return inverse, velocity, pressure


def signal_speeds(fields):
    inverse, velocity, pressure = primitives(fields)
    sound = jnp.sqrt(heat_ratio * pressure * inverse)
    return [jnp.abs(v) + sound for v in velocity]


def half_fluxes(half, speed, half_pressure, direction):
    flux = [half[direction + 1]] + [half[k] * speed for k in (1, 2, 3)]
    flux.append((half[4] + half_pressure) * speed)
    flux[direction + 1] = flux[direction + 1] + half_pressure
    return flux


def halves(fields, directions):
    _, velocity, pressure = primitives(fields)
    half = [0.5 * field for field in fields]
    half_pressure = 0.5 * pressure
    return [half_fluxes(half, velocity[d], half_pressure, d) for d in directions], half


def split(flux, field, alpha):
    signal = alpha * field
    return flux + signal, flux - signal


def cell_terms(below, above):
    second = above - below
    both = below + above
    square = second * second
    middle = 0.25 * (both * both) + ((13.0 / 12.0) * square + epsilon)
    outer = middle + square
    cross = both * second
    return second, outer + cross, middle, outer - cross


def correction(first, middle, last, third_first, third_last):
    ratio_first = middle * reciprocal(first)
    ratio_last = middle * reciprocal(last)
    weight_first = ratio_first * ratio_first
    weight_last = 1.5 * (ratio_last * ratio_last)
    total = (6.0 + weight_first) + (weight_last + weight_last)
    return (weight_first * third_first + weight_last * third_last) * reciprocal(total)


def stream(load, store, count):
    plus, minus, centre = {}, {}, {}
    terms_plus, terms_minus, third_plus, third_minus, interface = {}, {}, {}, {}, {}
    differences_plus, differences_minus = {}, {}
    plus[0], minus[0] = load(0)
    for j in range(1, count + 2 * HALO):
        plus[j], minus[j] = load(j)
        differences_plus[j] = plus[j] - plus[j - 1]
        differences_minus[j] = minus[j] - minus[j - 1]
        cell = j - 1
        if cell < 1:
            continue
        terms_plus[cell] = cell_terms(differences_plus[cell], differences_plus[j])
        terms_minus[cell] = cell_terms(differences_minus[cell], differences_minus[j])
        if 2 <= cell <= count + 3:
            centre[cell] = 6.0 * (plus[cell] + minus[cell]) - (
                terms_plus[cell][0] + terms_minus[cell][0]
            )
        if cell < 2:
            continue
        third_plus[cell] = terms_plus[cell][0] - terms_plus[cell - 1][0]
        third_minus[cell] = terms_minus[cell][0] - terms_minus[cell - 1][0]
        if cell < 4:
            continue
        at = cell - 2
        right = correction(
            terms_plus[at - 1][1], terms_plus[at][2], terms_plus[at + 1][3], third_plus[at], third_plus[at + 1]
        )
        left = correction(
            terms_minus[at + 2][3], terms_minus[at + 1][2], terms_minus[at][1],
            third_minus[at + 2], third_minus[at + 1],
        )
        interface[at] = (third_plus[at + 1] - third_minus[at + 1]) - 4.0 * (right - left)
        if at >= 3:
            store(at - 3, (centre[at - 1] - centre[at + 1]) + (interface[at - 1] - interface[at]))


def lane_index(shape):
    return lax.broadcasted_iota(jnp.int32, shape, len(shape) - 1)


def turned(value, by):
    size = value.shape[-1]
    if isinstance(by, int):
        by = by % size
        return value if by == 0 else pltpu.roll(value, by, value.ndim - 1)
    return pltpu.roll(value, lax.rem(by + 4 * size, size), value.ndim - 1)


def merged(pieces, slot):
    out = pieces[0]
    for number, piece in enumerate(pieces[1:], 1):
        out = jnp.where(slot == number, piece, out)
    return out


def rows_at(start, size):
    return pl.ds(start if isinstance(start, int) else pl.multiple_of(start, TILE), size)


def by_node(me, values):
    out = jnp.float32(values[0])
    for n, value in enumerate(values[1:], 1):
        out = jnp.where(me == n, jnp.float32(value), out)
    return out


def scaled_weight(row, column):
    return radau_weights[row][column] * (step_size / 12.0)


class Blocks:
    def __init__(self, comps, nx, ny, nz):
        self.comps, self.nx, self.ny, self.nz = comps, nx, ny, nz
        self.per = nz // ny
        self.left = nx - self.per
        assert nz % ny == 0 and ny % TILE == 0 and 2 * self.left == self.per
        self.half = nz // 2
        self.count = comps + (comps + 1) // 2

    def message(self, width):
        span = width + 2 * HALO
        rows = self.count * span - (span // 2 if self.comps % 2 else 0)
        return -(-rows // TILE) * TILE

    def lone(self, b):
        return self.comps % 2 == 1 and b == self.count - 1

    def pair(self, b):
        first = 2 * (b - self.comps)
        return first, min(first + 1, self.comps - 1) if isinstance(b, int) else jnp.minimum(first + 1, self.comps - 1)

    def whole(self, ref, c):
        return ref[c, pl.ds(0, self.per)].reshape(self.nz, self.nz)

    def leftovers(self, ref, first, second):
        at = pl.ds(self.per, self.left)
        shape = (self.half, self.nz)
        return jnp.concatenate([ref[first, at].reshape(shape), ref[second, at].reshape(shape)], axis=0)

    def natural(self, ref, b):
        return self.whole(ref, b) if b < self.comps else self.leftovers(ref, *self.pair(b))

    def put_whole(self, ref, c, value):
        ref[c, pl.ds(0, self.per)] = value.reshape(self.per, self.ny, self.nz)

    def put_leftovers(self, ref, b, value):
        at = pl.ds(self.per, self.left)
        shape = (self.left, self.ny, self.nz)
        first, second = self.pair(b)
        ref[second, at] = value[self.half :].reshape(shape)
        ref[first, at] = value[: self.half].reshape(shape)

    def put_natural(self, ref, b, value):
        if b < self.comps:
            self.put_whole(ref, b, value)
        else:
            self.put_leftovers(ref, b, value)

    def row(self, c, i, t):
        if i < self.per:
            return c * self.nz + (i * self.ny + t)
        return (self.comps + c // 2) * self.nz + (c % 2) * self.half + ((i - self.per) * self.ny + t)


def depth_fluxes(blocks, read, write):
    comps = blocks.comps
    (flux,), _ = halves([read(c) for c in range(comps)], (2,))
    for c in range(comps):
        write(c, flux[c])
    shared = [read(b) for b in range(comps, blocks.count)]
    fields = [shared[c // 2] if c % 2 == 0 else turned(shared[c // 2], blocks.half) for c in range(comps)]
    (flux,), _ = halves(fields, (2,))
    lower = lane_index(fields[0].shape) < blocks.half
    for b in range(comps, blocks.count):
        first, second = blocks.pair(b)
        write(b, jnp.where(lower, flux[first], turned(flux[second], blocks.half)))


def write_halves(blocks, nodes, rows_ref, zf):
    size = blocks.nz // nodes + 8

    def node(m, carry):
        def read(b):
            return rows_ref[rows_at((m * blocks.count + b) * size, size), :]

        def write(b, flux):
            zf[rows_at((m * blocks.count + b) * size, size), :] = flux

        depth_fluxes(blocks, read, write)
        return carry

    lax.fori_loop(0, nodes, node, 0, unroll=True)


def write_edges(read, nx, ny, comps, lo_ref, hi_ref, side_ref):
    rows = side_ref.shape[1] // (2 * HALO)
    for c in range(comps):
        for i in range(HALO):
            lo_ref[0, pl.ds((c * HALO + i) * ny, ny), :] = read(c, i)
            hi_ref[0, pl.ds((c * HALO + i) * ny, ny), :] = read(c, nx - HALO + i)

    def side(i, carry):
        for c in range(comps):
            value = read(c, i)
            side_ref[0, pl.ds(c * nx + i, HALO, stride=rows), :] = value[ny - HALO :]
            side_ref[0, pl.ds(HALO * rows + c * nx + i, HALO, stride=rows), :] = value[:HALO]
        return carry

    lax.fori_loop(0, nx, side, 0, unroll=4)


def faster(best, read, first, count, comps):
    def step(i, best):
        speeds = signal_speeds([read(c, i) for c in range(comps)])
        return tuple(jnp.maximum(b, s) for b, s in zip(best, speeds))

    return lax.fori_loop(first, first + count, step, best, unroll=True)


def speed_tile(best, nodes):
    nz = best.shape[-1]
    width = nz // nodes
    shape = (3 * nodes, nz)
    place = lax.broadcasted_iota(jnp.int32, shape, 0)
    rows = jnp.where(place < nodes, best[:1], jnp.where(place < 2 * nodes, best[1:2], best[2:3]))
    spots = jnp.max(jnp.where(lane_index(shape) // width == place % nodes, rows, 0.0), axis=1, keepdims=True)
    group = lane_index((1, nz)) // width
    rows = [merged([spots[k * nodes + m : k * nodes + m + 1] for m in range(nodes)], group) for k in range(3)]
    return jnp.concatenate(rows + [jnp.zeros((TILE - 3, nz), jnp.float32)], axis=0), spots


def send_speeds(rows, tiles_ref, out_hbm, sem):
    tile = jnp.concatenate(rows + [jnp.zeros((TILE - 3, rows[0].shape[-1]), jnp.float32)], axis=0)
    tiles_ref[...] = jnp.broadcast_to(tile[None], tiles_ref.shape)
    copy = pltpu.make_async_copy(tiles_ref, out_hbm, sem)
    copy.start()
    return copy


def open_kernel(u_ref, *refs):
    parts, (speeds_hbm, ring, tiles_ref, sem) = refs[:-4], refs[-4:]
    nodes = len(parts)
    comps, nx, ny, nz = u_ref.shape[1:]
    blocks = Blocks(comps, nx, ny, nz)
    me = lax.axis_index("node")
    best = tuple(jnp.zeros((ny, nz), jnp.float32) for _ in range(3))
    best = faster(best, lambda c, i: u_ref[0, c, i], 0, nx, comps)
    width = nz // nodes
    rows = [jnp.max(b, axis=0, keepdims=True) for b in best]
    rows = [functools.reduce(jnp.maximum, [turned(r, width * k) for k in range(nodes)]) for r in rows]
    mine = lane_index(rows[0].shape) // width == me
    copy = send_speeds([jnp.where(mine, r, 0.0) for r in rows], tiles_ref, speeds_hbm, sem)
    quarters = [me ^ k for k in range(nodes)]
    for b in range(blocks.count):
        send_quarter(blocks, blocks.natural(u_ref.at[0], b).T, ring, b, parts, quarters, width)
    copy.wait()


def send_quarter(blocks, value, ring_ref, b, parts, quarters, width):
    nz = value.shape[0]
    base = b * (nz + 2 * TILE)
    ring_ref[pl.ds(base + TILE, nz), :] = value
    ring_ref[pl.ds(base, TILE), :] = value[nz - TILE :]
    ring_ref[pl.ds(base + TILE + nz, TILE), :] = value[:TILE]
    span = width + 2 * HALO
    half = span // 2
    for part, quarter in zip(parts, quarters):
        start = base + (TILE - HALO) + quarter * width
        if blocks.lone(b):
            low, high = ring_ref[pl.ds(start, half), :], ring_ref[pl.ds(start + half, half), :]
            lower = lane_index(low.shape) < blocks.half
            part[pl.ds(b * span, half), :] = jnp.where(lower, low, turned(high, blocks.half))
        else:
            part[pl.ds(b * span, span), :] = ring_ref[pl.ds(start, span), :]


def start_kernel(init_ref, rows_ref, pack_ref, turned_ref, *, nodes):
    comps, nx, ny, nz = init_ref.shape
    blocks = Blocks(comps, nx, ny, nz)
    width = nz // nodes
    me = lax.axis_index("node")
    lanes = lane_index((ny, nz)) // width
    for b in range(blocks.count):
        turned_ref[rows_at(b * nz, nz), :] = blocks.natural(init_ref, b).T
        rows_ref[rows_at(b * width, width), :] = turned_ref[rows_at(b * nz + me * width, width), :]

    def step(c, carry):
        for q in range(nx // nodes):
            pieces = [turned(init_ref[c, q * nodes + i], width * i) for i in range(nodes)]
            out = pieces[0]
            for i in range(1, nodes):
                out = jnp.where(lanes == lax.rem(me + i, nodes), pieces[i], out)
            pack_ref[rows_at((c * (nx // nodes) + q) * ny, ny), :] = out
        return carry

    lax.fori_loop(0, comps, step, 0)


def gather_kernel(*refs):
    parts, (rows_ref, nat_ref, lo_ref, hi_ref, side_ref) = refs[:-5], refs[-5:]
    nodes = len(parts)
    comps, nx, ny, nz = nat_ref.shape
    blocks = Blocks(comps, nx, ny, nz)
    width = nz // nodes
    size = width + 8
    me = lax.axis_index("node")
    whole = blocks.count * size
    span = width + 2 * HALO
    half = span // 2
    for k in range(nodes):
        for b in range(blocks.count):
            start = (me ^ k) * whole + b * size
            if blocks.lone(b):
                both = parts[k][pl.ds(b * span, half), :]
                rows_ref[rows_at(start, half), :] = both
                rows_ref[pl.ds(start + half, half), :] = turned(both, blocks.half)
            else:
                rows_ref[rows_at(start, span), :] = parts[k][pl.ds(b * span, span), :]
    for b in range(blocks.count):
        own = [pl.ds(m * whole + b * size + HALO, width) for m in range(nodes)]
        state = jnp.concatenate([rows_ref[at, :] for at in own], axis=0)
        blocks.put_natural(nat_ref, b, state.T)
    write_edges(lambda c, i: nat_ref[c, i], nx, ny, comps, lo_ref, hi_ref, side_ref)


def along_second(nat_ref, side_ref, alpha, fy, yp, ym, gp, gm, beside=None):
    comps, nx, ny, nz = nat_ref.shape
    rows = gp.shape[0] // (2 * HALO)

    def prepare(fields, place, plus, minus):
        (flux,), half = halves(fields, (1,))
        for c in range(comps):
            at = place(c)
            plus[at, :], minus[at, :] = split(flux[c], half[c], alpha)

    def own(i, carry):
        prepare([nat_ref[c, i] for c in range(comps)], lambda c: rows_at((c * nx + i) * ny, ny), yp, ym)
        return carry

    lax.fori_loop(0, nx, own, 0, unroll=4)

    def ghost(i, carry):
        def place(c):
            return pl.ds(i * rows + c * nx, nx)

        prepare([side_ref[0, place(c), :] for c in range(comps)], place, gp, gm)
        return carry

    lax.fori_loop(0, 2 * HALO, ghost, 0, unroll=HALO)

    def along(b, carry):
        first = pl.multiple_of(b * TILE, TILE)

        def load(j):
            if HALO <= j < HALO + ny:
                at = pl.ds(first * ny + (j - HALO), TILE, stride=ny)
                return yp[at, :], ym[at, :]
            at = pl.ds((j if j < HALO else j - ny) * rows + first, TILE)
            return gp[at, :], gm[at, :]

        def store(i, value):
            fy[pl.ds(i * rows + first, TILE), :] = value

        if beside is not None:
            beside(b)
        stream(load, store, ny)
        return carry

    lax.fori_loop(0, rows // TILE, along, 0)


def along_last(blocks, nodes, zf, zu, alphas):
    width = blocks.nz // nodes
    size = width + 8
    each = width // CHUNK

    def along(n, carry):
        m = n // each
        start = m * (blocks.count * size) + lax.rem(n, each) * CHUNK
        alpha = alphas[pl.ds(m * TILE, TILE), :]

        def load(j):
            at = pl.ds(start + j, TILE, stride=size)
            return split(zf[at, :], zu[at, :], alpha)

        def store(i, value):
            zf[pl.ds(start + i, TILE, stride=size), :] = value

        stream(load, store, CHUNK)
        return carry

    lax.fori_loop(0, nodes * each, along, 0)


def block_rates(blocks, nodes, zf, b):
    width = blocks.nz // nodes
    size = width + 8
    return jnp.concatenate([zf[rows_at((m * blocks.count + b) * size, width), :] for m in range(nodes)], axis=0)


def along_first(u, alphas, lo_ref, hi_ref, fy, rate, xp, xm, extra, after, unrolled=False):
    comps, nx, ny, nz = rate.shape
    rows = -(-comps * nx // TILE) * TILE
    every = range(comps)

    def prepare(fields, at):
        (flux,), half = halves(fields, (0,))
        for c in every:
            p, m = split(flux[c], half[c], alphas[0])
            xp[at, c * ny : (c + 1) * ny, :] = p
            xm[at, c * ny : (c + 1) * ny, :] = m

    def own(i, carry):
        prepare([u(c, i) for c in every], i + HALO)
        return carry

    lax.fori_loop(0, nx, own, 0, unroll=4)
    for ref, start in ((lo_ref, 0), (hi_ref, nx + HALO)):

        def ghost(i, carry, ref=ref, start=start):
            prepare([ref[0, rows_at((c * HALO + i) * ny, ny), :] for c in every], start + i)
            return carry

        lax.fori_loop(0, HALO, ghost, 0, unroll=HALO)

    def component(c):
        for t in range(0, ny, TILE):

            def load(j, t=t):
                at = rows_at(c * ny + t, TILE)
                return xp[j, at, :], xm[j, at, :]

            def store(i, value, t=t):
                value = value + fy[pl.ds(t * rows + c * nx + i, TILE, stride=rows), :]
                rate[c, i, pl.ds(t, TILE), :] = value if extra is None else value + extra(c, i, t)

            stream(load, store, nx)

    def along(c, carry):
        after(jnp.maximum(c - 1, 0))
        component(c)
        return carry

    if unrolled:
        for c in every:
            if c:
                after(c - 1)
            component(c)
        after(comps - 1)
    else:
        lax.fori_loop(0, comps, along, 0)
        after(jnp.int32(comps - 1))


def tile_rows(tile):
    return [tile[k : k + 1, :] for k in range(3)]


def speeds_of(al_ref, al_out, alphas, nodes):
    tile, spots = speed_tile(jnp.max(al_ref[...], axis=0), nodes)
    al_out[...] = tile
    for m in range(nodes):
        at = 2 * nodes + m
        alphas[m * TILE : (m + 1) * TILE, :] = jnp.broadcast_to(spots[at : at + 1], (TILE, tile.shape[-1])) * 0.5
    return tile


def halves_kernel(rows_ref, zf, *, dims, nodes):
    write_halves(Blocks(*dims), nodes, rows_ref, zf)


def first_lanes_kernel(nat_ref, zu, zf_in, side_ref, al_ref, fy, zf, al_out, *scratch, nodes):
    del zf_in
    *scratch, alphas = scratch
    tile = speeds_of(al_ref, al_out, alphas, nodes)
    along_last(Blocks(*nat_ref.shape), nodes, zf, zu, alphas)
    along_second(nat_ref, side_ref, tile[1:2], fy, *scratch)


def second_lanes_kernel(
    nat_ref, before_ref, behind_ref, side_ref, al_ref, fz, fy, al_out, zu, zf, *scratch, nodes
):
    *scratch, alphas = scratch
    blocks = Blocks(*nat_ref.shape)
    nz = blocks.nz
    size = nz // nodes + 8
    width = nz // nodes
    for b in range(blocks.count):
        value = blocks.natural(nat_ref, b).T
        for m in range(nodes):
            ghost = pl.ds((m * blocks.count + b) * 4, HALO)
            start = (m * blocks.count + b) * size
            zu[pl.ds(start, HALO), :] = before_ref[ghost, :]
            zu[pl.ds(start + HALO, width), :] = value[m * width : (m + 1) * width]
            zu[pl.ds(start + HALO + width, HALO), :] = behind_ref[ghost, :]
    write_halves(blocks, nodes, zu, zf)
    tile = speeds_of(al_ref, al_out, alphas, nodes)
    along_last(blocks, nodes, zf, zu, alphas)

    def turn(b):
        fz[rows_at(b * nz, nz), :] = block_rates(blocks, nodes, zf, b).T

    assert blocks.count == scratch[2].shape[0] // (2 * HALO) // TILE
    along_second(nat_ref, side_ref, tile[1:2], fy, *scratch, beside=turn)


def first_rows_kernel(nat_in, lo_in, hi_in, al_in, zf, fy, start_ref, *refs, nodes):
    nat_ref, lo_ref, hi_ref, side_ref, first_ref, last_ref, speeds_hbm, rate, xp, xm, tiles_ref, sem = refs
    comps, nx, ny, nz = nat_ref.shape
    blocks = Blocks(comps, nx, ny, nz)
    width = nz // nodes

    def state(value, b):
        rates = value.T + block_rates(blocks, nodes, zf, b)
        start = start_ref[rows_at(b * width, width), :]
        states = []
        for m in range(nodes):
            new = start
            for n in range(nodes):
                new = new + scaled_weight(m, n) * rates[n * width : (n + 1) * width]
            ghost = pl.ds((m * blocks.count + b) * 4, HALO)
            first_ref[ghost, :] = new[:HALO]
            last_ref[ghost, :] = new[width - HALO :]
            states.append(new)
        return jnp.concatenate(states, axis=0).T

    def after(c):
        blocks.put_whole(nat_ref, c, state(blocks.whole(rate, c), c))
        if c % 2 == 1 or c == comps - 1:
            b = comps + c // 2
            blocks.put_leftovers(nat_ref, b, state(blocks.leftovers(rate, *blocks.pair(b)), b))

    along_first(lambda c, i: nat_in[c, i], tile_rows(al_in), lo_in, hi_in, fy, rate, xp, xm, None, after, True)

    def read(c, i):
        return nat_ref[c, i]

    best = tuple(jnp.zeros((ny, nz), jnp.float32) for _ in range(3))
    best = faster(best, read, 0, nx, comps)
    copy = send_speeds([jnp.max(b, axis=0, keepdims=True) for b in best], tiles_ref, speeds_hbm, sem)
    write_edges(read, nx, ny, comps, lo_ref, hi_ref, side_ref)
    copy.wait()


def second_rows_kernel(nat_ref, lo_ref, hi_ref, al_ref, fz, fy, pack_ref, *refs):
    outs, (rate, xp, xm) = refs[:-3], refs[-3:]
    nodes = len(outs)
    comps, nx, ny, nz = nat_ref.shape
    blocks = Blocks(comps, nx, ny, nz)
    width = nz // nodes
    me = lax.axis_index("node")
    weights = [
        [by_node(me, [scaled_weight(n ^ k, j) for n in range(nodes)]) for j in range(nodes)] for k in range(nodes)
    ]
    lanes = lane_index((TILE, nz)) // width

    def extra(c, i, t):
        return fz[rows_at(blocks.row(c, i, t), TILE), :]

    def after(c):
        for t in range(0, ny, TILE):
            for q in range(nx // nodes):
                at = rows_at((c * (nx // nodes) + q) * ny + t, TILE)
                start = pack_ref[at, :]
                rows = [turned(rate[c, q * nodes + i, pl.ds(t, TILE), :], width * i) for i in range(nodes)]
                rates = [
                    turned(merged([rows[(g - j) % nodes] for g in range(nodes)], lanes), width * (me - j))
                    for j in range(nodes)
                ]
                for k in range(nodes):
                    value = start
                    for j in range(nodes):
                        value = value + weights[k][j] * rates[j]
                    outs[k][at, :] = value

    along_first(lambda c, i: nat_ref[c, i], tile_rows(al_ref), lo_ref, hi_ref, fy, rate, xp, xm, extra, after, True)


def close_kernel(*refs):
    parts, (out_hbm, out_ref, sems) = refs[:-3], refs[-3:]
    nodes = len(parts)
    comps, nx, ny, nz = out_ref.shape
    width = nz // nodes
    me = lax.axis_index("node")
    lanes = lane_index((ny, nz)) // width
    copies = []
    for c in range(comps):
        for q in range(nx // nodes):
            at = pl.ds((c * (nx // nodes) + q) * ny, ny)
            values = [part[at, :] for part in parts]
            for i in range(nodes):
                out = values[0]
                for k in range(1, nodes):
                    out = jnp.where(lanes == lax.rem((me ^ k) + i, nodes), values[k], out)
                out_ref[c, q * nodes + i] = turned(out, -width * i)
        copies.append(pltpu.make_async_copy(out_ref.at[c], out_hbm.at[0, c], sems.at[c]))
        copies[-1].start()
    for copy in copies:
        copy.wait()


def call(kernel, name, outs, operands, scratch=(), flops=500_000_000, anywhere=False, outside=(), aliases=None):
    vmem, hbm = pl.BlockSpec(memory_space=pltpu.VMEM), pl.BlockSpec(memory_space=pltpu.HBM)
    moved = sum(4 * x.size for x in operands)
    scratch = [pltpu.VMEM(x, jnp.float32) if isinstance(x, tuple) else x for x in scratch]
    return pl.pallas_call(
        kernel,
        out_shape=[jax.ShapeDtypeStruct(shape, jnp.float32) for shape in outs],
        in_specs=[hbm if anywhere else vmem] * len(operands),
        out_specs=[hbm if n in outside else vmem for n in range(len(outs))],
        scratch_shapes=scratch,
        input_output_aliases=aliases or {},
        compiler_params=pltpu.CompilerParams(vmem_limit_bytes=32 * 1024 * 1024),
        cost_estimate=pl.CostEstimate(flops=flops, bytes_accessed=2 * moved, transcendentals=0),
        name=name,
    )(*operands)


def shifted(value, axis, by):
    count = lax.axis_size(axis)
    return lax.ppermute(value, axis, [(i, (i + by) % count) for i in range(count)])


def swapped(value, by):
    return lax.ppermute(value, "node", [(i, i ^ by) for i in range(lax.axis_size("node"))])


def beside(side):
    if lax.axis_size("gy") == 2:
        return shifted(side, "gy", 1)
    half = side.shape[1] // 2
    return jnp.concatenate([shifted(side[:, :half], "gy", 1), shifted(side[:, half:], "gy", -1)], axis=1)


def across(lo, hi):
    return shifted(hi, "gx", 1), shifted(lo, "gx", -1)


def exchanged(parts):
    moved = {k: swapped(parts[k], k) for k in sorted(range(1, len(parts)), reverse=True)}
    return [parts[0]] + [moved[k] for k in range(1, len(parts))]


def local(initial, guesses):
    comps, nx, ny, nz = initial.shape
    nodes = lax.axis_size("node")
    everyone = ("node", "gx", "gy")
    devices = nodes * lax.axis_size("gx") * lax.axis_size("gy")
    rows = -(-comps * nx // TILE) * TILE
    blocks = Blocks(comps, nx, ny, nz)
    width = nz // nodes
    assert blocks.count == TILE and width % CHUNK == 0 and nx % nodes == 0
    edge = (1, comps * HALO * ny, nz)
    edges = [edge, edge, (1, 2 * HALO * rows, nz)]
    tile_shape = (TILE, nz)
    speeds_shape = (devices, TILE, nz)
    part = (blocks.count * (width + 8), nz)
    pack = (comps * nx // nodes * ny, nz)
    ghost = (nodes * blocks.count * 4, nz)
    depth_shape = (blocks.count * nz, nz)
    lanes_scratch = [(ny * rows, nz)] * 2 + [(2 * HALO * rows, nz)] * 2 + [(nodes * TILE, nz)]
    whole = (nodes * part[0], nz)
    slabs = [initial.shape] + [(nx + 2 * HALO, comps * ny, nz)] * 2
    ring = (blocks.count * (nz + 2 * TILE), nz)

    *parts, speeds = call(
        open_kernel,
        "open_kernel",
        [(blocks.message(width), nz)] * nodes + [speeds_shape],
        [guesses],
        [ring, speeds_shape, pltpu.SemaphoreType.DMA],
        outside=(nodes,),
    )
    speeds = lax.all_to_all(speeds, everyone, 0, 0)
    parts = exchanged(parts)
    turned_field, field, lo, hi, side = call(
        gather_kernel, "gather_kernel", [whole, initial.shape] + edges, parts
    )
    side = beside(side)
    lower, upper = across(lo, hi)
    initial, side = lax.optimization_barrier((initial, side))
    start, start_pack = call(
        functools.partial(start_kernel, nodes=nodes),
        "start_kernel",
        [(blocks.count * width, nz), pack],
        [initial],
        [depth_shape],
    )
    (fluxes,) = call(
        functools.partial(halves_kernel, dims=initial.shape, nodes=nodes), "halves_kernel", [whole], [turned_field]
    )
    fluxes, start, start_pack = lax.optimization_barrier((fluxes, start, start_pack))
    rates, depth, tile = call(
        functools.partial(first_lanes_kernel, nodes=nodes),
        "first_lanes_kernel",
        [(ny * rows, nz), whole, tile_shape],
        [field, turned_field, fluxes, side, speeds],
        lanes_scratch,
        4_000_000_000,
        aliases={2: 1},
    )
    field, lo, hi, side, first, last, speeds = call(
        functools.partial(first_rows_kernel, nodes=nodes),
        "first_rows_kernel",
        [initial.shape] + edges + [ghost, ghost, speeds_shape],
        [field, lower, upper, tile, depth, rates, start],
        slabs + [speeds_shape, pltpu.SemaphoreType.DMA],
        2_500_000_000,
        outside=(6,),
        aliases={0: 0, 1: 1, 2: 2},
    )
    speeds = lax.all_to_all(speeds, everyone, 0, 0)
    before, behind = shifted(last, "node", 1), shifted(first, "node", -1)
    side = beside(side)
    lower, upper = across(lo, hi)
    depth, rates, tile = call(
        functools.partial(second_lanes_kernel, nodes=nodes),
        "second_lanes_kernel",
        [depth_shape, (ny * rows, nz), tile_shape],
        [field, before, behind, side, speeds],
        [whole, whole] + lanes_scratch,
        4_000_000_000,
    )
    outs = call(
        second_rows_kernel,
        "second_rows_kernel",
        [pack] * nodes,
        [field, lower, upper, tile, depth, rates, start_pack],
        slabs,
        2_500_000_000,
    )
    (states,) = call(
        close_kernel,
        "close_kernel",
        [(1,) + initial.shape],
        exchanged(outs),
        [initial.shape, pltpu.SemaphoreType.DMA((comps,))],
        outside=(0,),
    )
    return states


def solution(mesh):
    return jax.shard_map(
        local,
        mesh=mesh,
        in_specs=(P(None, "gx", "gy", None), P("node", None, "gx", "gy", None)),
        out_specs=P("node", None, "gx", "gy", None),
        check_vma=False,
    )
```

```python
import functools

import jax
import jax.numpy as jnp
from jax import lax
from jax.experimental import pallas as pl
from jax.experimental.pallas import tpu as pltpu
from jax.sharding import PartitionSpec as P

SWEEPS = 2
HALO = 3
COMPONENTS = 5
TILE = 8
CHUNK = 16

heat_ratio = 1.4
step_size = 0.025
density_floor = 0.5
pressure_floor = 0.25
epsilon = 1e-06
radau_weights = [
    [0.112999479323156, -0.040309220723522, 0.025802377420336, -0.009904676507266],
    [0.2343839957474, 0.206892573935359, -0.047857128048541, 0.016047422806516],
    [0.21668178462325, 0.406123263867373, 0.189036518170056, -0.024182104899833],
    [0.220462211176768, 0.388193468843172, 0.32884431998006, 0.0625],
]


def reciprocal(value):
    return pl.reciprocal(value, approx=True)


def primitives(fields):
    inverse = 1.0 / jnp.maximum(fields[0], density_floor)
    velocity = [fields[k] * inverse for k in (1, 2, 3)]
    energy = fields[1] * velocity[0] + fields[2] * velocity[1] + fields[3] * velocity[2]
    pressure = jnp.maximum(0.4 * (fields[4] - 0.5 * energy), pressure_floor)
    return inverse, velocity, pressure


def signal_speeds(fields):
    inverse, velocity, pressure = primitives(fields)
    sound = jnp.sqrt(heat_ratio * pressure * inverse)
    return [jnp.abs(v) + sound for v in velocity]


def half_fluxes(half, speed, half_pressure, direction):
    flux = [half[direction + 1]] + [half[k] * speed for k in (1, 2, 3)]
    flux.append((half[4] + half_pressure) * speed)
    flux[direction + 1] = flux[direction + 1] + half_pressure
    return flux


def halves(fields, directions):
    _, velocity, pressure = primitives(fields)
    half = [0.5 * field for field in fields]
    half_pressure = 0.5 * pressure
    return [half_fluxes(half, velocity[d], half_pressure, d) for d in directions], half


def split(flux, field, alpha):
    signal = alpha * field
    return flux + signal, flux - signal


def cell_terms(below, above):
    second = above - below
    both = below + above
    square = second * second
    middle = 0.25 * (both * both) + ((13.0 / 12.0) * square + epsilon)
    outer = middle + square
    cross = both * second
    return second, outer + cross, middle, outer - cross


def correction(first, middle, last, third_first, third_last):
    ratio_first = middle * reciprocal(first)
    ratio_last = middle * reciprocal(last)
    weight_first = ratio_first * ratio_first
    weight_last = 1.5 * (ratio_last * ratio_last)
    total = (6.0 + weight_first) + (weight_last + weight_last)
    return (weight_first * third_first + weight_last * third_last) * reciprocal(total)


def stream(load, store, count):
    plus, minus, centre = {}, {}, {}
    terms_plus, terms_minus, third_plus, third_minus, interface = {}, {}, {}, {}, {}
    differences_plus, differences_minus = {}, {}
    plus[0], minus[0] = load(0)
    for j in range(1, count + 2 * HALO):
        plus[j], minus[j] = load(j)
        differences_plus[j] = plus[j] - plus[j - 1]
        differences_minus[j] = minus[j] - minus[j - 1]
        cell = j - 1
        if cell < 1:
            continue
        terms_plus[cell] = cell_terms(differences_plus[cell], differences_plus[j])
        terms_minus[cell] = cell_terms(differences_minus[cell], differences_minus[j])
        if 2 <= cell <= count + 3:
            centre[cell] = 6.0 * (plus[cell] + minus[cell]) - (
                terms_plus[cell][0] + terms_minus[cell][0]
            )
        if cell < 2:
            continue
        third_plus[cell] = terms_plus[cell][0] - terms_plus[cell - 1][0]
        third_minus[cell] = terms_minus[cell][0] - terms_minus[cell - 1][0]
        if cell < 4:
            continue
        at = cell - 2
        right = correction(
            terms_plus[at - 1][1], terms_plus[at][2], terms_plus[at + 1][3], third_plus[at], third_plus[at + 1]
        )
        left = correction(
            terms_minus[at + 2][3], terms_minus[at + 1][2], terms_minus[at][1],
            third_minus[at + 2], third_minus[at + 1],
        )
        interface[at] = (third_plus[at + 1] - third_minus[at + 1]) - 4.0 * (right - left)
        if at >= 3:
            store(at - 3, (centre[at - 1] - centre[at + 1]) + (interface[at - 1] - interface[at]))


def lane_index(shape):
    return lax.broadcasted_iota(jnp.int32, shape, len(shape) - 1)


def turned(value, by):
    size = value.shape[-1]
    if isinstance(by, int):
        by = by % size
        return value if by == 0 else pltpu.roll(value, by, value.ndim - 1)
    return pltpu.roll(value, lax.rem(by + 4 * size, size), value.ndim - 1)


def merged(pieces, slot):
    out = pieces[0]
    for number, piece in enumerate(pieces[1:], 1):
        out = jnp.where(slot == number, piece, out)
    return out


def rows_at(start, size):
    return pl.ds(start if isinstance(start, int) else pl.multiple_of(start, TILE), size)


def by_node(me, values):
    out = jnp.float32(values[0])
    for n, value in enumerate(values[1:], 1):
        out = jnp.where(me == n, jnp.float32(value), out)
    return out


def scaled_weight(row, column):
    return radau_weights[row][column] * (step_size / 12.0)


class Blocks:
    def __init__(self, comps, nx, ny, nz):
        self.comps, self.nx, self.ny, self.nz = comps, nx, ny, nz
        self.per = nz // ny
        self.left = nx - self.per
        assert nz % ny == 0 and ny % TILE == 0 and 2 * self.left == self.per
        self.half = nz // 2
        self.count = comps + (comps + 1) // 2

    def message(self, width):
        span = width + 2 * HALO
        rows = self.count * span - (span // 2 if self.comps % 2 else 0)
        return -(-rows // TILE) * TILE

    def lone(self, b):
        return self.comps % 2 == 1 and b == self.count - 1

    def pair(self, b):
        first = 2 * (b - self.comps)
        return first, min(first + 1, self.comps - 1) if isinstance(b, int) else jnp.minimum(first + 1, self.comps - 1)

    def whole(self, ref, c):
        return ref[c, pl.ds(0, self.per)].reshape(self.nz, self.nz)

    def leftovers(self, ref, first, second):
        at = pl.ds(self.per, self.left)
        shape = (self.half, self.nz)
        return jnp.concatenate([ref[first, at].reshape(shape), ref[second, at].reshape(shape)], axis=0)

    def natural(self, ref, b):
        return self.whole(ref, b) if b < self.comps else self.leftovers(ref, *self.pair(b))

    def put_whole(self, ref, c, value):
        ref[c, pl.ds(0, self.per)] = value.reshape(self.per, self.ny, self.nz)

    def put_leftovers(self, ref, b, value):
        at = pl.ds(self.per, self.left)
        shape = (self.left, self.ny, self.nz)
        first, second = self.pair(b)
        ref[second, at] = value[self.half :].reshape(shape)
        ref[first, at] = value[: self.half].reshape(shape)

    def put_natural(self, ref, b, value):
        if b < self.comps:
            self.put_whole(ref, b, value)
        else:
            self.put_leftovers(ref, b, value)

    def row(self, c, i, t):
        if i < self.per:
            return c * self.nz + (i * self.ny + t)
        return (self.comps + c // 2) * self.nz + (c % 2) * self.half + ((i - self.per) * self.ny + t)


def depth_fluxes(blocks, read, write):
    comps = blocks.comps
    (flux,), _ = halves([read(c) for c in range(comps)], (2,))
    for c in range(comps):
        write(c, flux[c])
    shared = [read(b) for b in range(comps, blocks.count)]
    fields = [shared[c // 2] if c % 2 == 0 else turned(shared[c // 2], blocks.half) for c in range(comps)]
    (flux,), _ = halves(fields, (2,))
    lower = lane_index(fields[0].shape) < blocks.half
    for b in range(comps, blocks.count):
        first, second = blocks.pair(b)
        write(b, jnp.where(lower, flux[first], turned(flux[second], blocks.half)))


def write_halves(blocks, nodes, rows_ref, zf):
    size = blocks.nz // nodes + 8

    def node(m, carry):
        def read(b):
            return rows_ref[rows_at((m * blocks.count + b) * size, size), :]

        def write(b, flux):
            zf[rows_at((m * blocks.count + b) * size, size), :] = flux

        depth_fluxes(blocks, read, write)
        return carry

    lax.fori_loop(0, nodes, node, 0, unroll=True)


def write_edges(read, nx, ny, comps, lo_ref, hi_ref, side_ref):
    rows = side_ref.shape[1] // (2 * HALO)
    for c in range(comps):
        for i in range(HALO):
            lo_ref[0, pl.ds((c * HALO + i) * ny, ny), :] = read(c, i)
            hi_ref[0, pl.ds((c * HALO + i) * ny, ny), :] = read(c, nx - HALO + i)

    def side(i, carry):
        for c in range(comps):
            value = read(c, i)
            side_ref[0, pl.ds(c * nx + i, HALO, stride=rows), :] = value[ny - HALO :]
            side_ref[0, pl.ds(HALO * rows + c * nx + i, HALO, stride=rows), :] = value[:HALO]
        return carry

    lax.fori_loop(0, nx, side, 0, unroll=4)


def faster(best, read, first, count, comps):
    def step(i, best):
        speeds = signal_speeds([read(c, i) for c in range(comps)])
        return tuple(jnp.maximum(b, s) for b, s in zip(best, speeds))

    return lax.fori_loop(first, first + count, step, best, unroll=True)


def speed_tile(best, nodes):
    nz = best.shape[-1]
    width = nz // nodes
    shape = (3 * nodes, nz)
    place = lax.broadcasted_iota(jnp.int32, shape, 0)
    rows = jnp.where(place < nodes, best[:1], jnp.where(place < 2 * nodes, best[1:2], best[2:3]))
    spots = jnp.max(jnp.where(lane_index(shape) // width == place % nodes, rows, 0.0), axis=1, keepdims=True)
    group = lane_index((1, nz)) // width
    rows = [merged([spots[k * nodes + m : k * nodes + m + 1] for m in range(nodes)], group) for k in range(3)]
    return jnp.concatenate(rows + [jnp.zeros((TILE - 3, nz), jnp.float32)], axis=0), spots


def send_speeds(rows, tiles_ref, out_hbm, sem):
    tile = jnp.concatenate(rows + [jnp.zeros((TILE - 3, rows[0].shape[-1]), jnp.float32)], axis=0)
    tiles_ref[...] = jnp.broadcast_to(tile[None], tiles_ref.shape)
    copy = pltpu.make_async_copy(tiles_ref, out_hbm, sem)
    copy.start()
    return copy


def open_kernel(u_ref, *refs):
    parts, (speeds_hbm, ring, tiles_ref, sem) = refs[:-4], refs[-4:]
    nodes = len(parts)
    comps, nx, ny, nz = u_ref.shape[1:]
    blocks = Blocks(comps, nx, ny, nz)
    me = lax.axis_index("node")
    best = tuple(jnp.zeros((ny, nz), jnp.float32) for _ in range(3))
    best = faster(best, lambda c, i: u_ref[0, c, i], 0, nx, comps)
    width = nz // nodes
    rows = [jnp.max(b, axis=0, keepdims=True) for b in best]
    rows = [functools.reduce(jnp.maximum, [turned(r, width * k) for k in range(nodes)]) for r in rows]
    mine = lane_index(rows[0].shape) // width == me
    copy = send_speeds([jnp.where(mine, r, 0.0) for r in rows], tiles_ref, speeds_hbm, sem)
    quarters = [me ^ k for k in range(nodes)]
    for b in range(blocks.count):
        send_quarter(blocks, blocks.natural(u_ref.at[0], b).T, ring, b, parts, quarters, width)
    copy.wait()


def send_quarter(blocks, value, ring_ref, b, parts, quarters, width):
    nz = value.shape[0]
    base = b * (nz + 2 * TILE)
    ring_ref[pl.ds(base + TILE, nz), :] = value
    ring_ref[pl.ds(base, TILE), :] = value[nz - TILE :]
    ring_ref[pl.ds(base + TILE + nz, TILE), :] = value[:TILE]
    span = width + 2 * HALO
    half = span // 2
    for part, quarter in zip(parts, quarters):
        start = base + (TILE - HALO) + quarter * width
        if blocks.lone(b):
            low, high = ring_ref[pl.ds(start, half), :], ring_ref[pl.ds(start + half, half), :]
            lower = lane_index(low.shape) < blocks.half
            part[pl.ds(b * span, half), :] = jnp.where(lower, low, turned(high, blocks.half))
        else:
            part[pl.ds(b * span, span), :] = ring_ref[pl.ds(start, span), :]


def start_kernel(init_ref, rows_ref, pack_ref, turned_ref, *, nodes):
    comps, nx, ny, nz = init_ref.shape
    blocks = Blocks(comps, nx, ny, nz)
    width = nz // nodes
    me = lax.axis_index("node")
    lanes = lane_index((ny, nz)) // width
    for b in range(blocks.count):
        turned_ref[rows_at(b * nz, nz), :] = blocks.natural(init_ref, b).T
        rows_ref[rows_at(b * width, width), :] = turned_ref[rows_at(b * nz + me * width, width), :]

    def step(c, carry):
        for q in range(nx // nodes):
            pieces = [turned(init_ref[c, q * nodes + i], width * i) for i in range(nodes)]
            out = pieces[0]
            for i in range(1, nodes):
                out = jnp.where(lanes == lax.rem(me + i, nodes), pieces[i], out)
            pack_ref[rows_at((c * (nx // nodes) + q) * ny, ny), :] = out
        return carry

    lax.fori_loop(0, comps, step, 0)


def gather_kernel(*refs):
    parts, (rows_ref, nat_ref, lo_ref, hi_ref, side_ref) = refs[:-5], refs[-5:]
    nodes = len(parts)
    comps, nx, ny, nz = nat_ref.shape
    blocks = Blocks(comps, nx, ny, nz)
    width = nz // nodes
    size = width + 8
    me = lax.axis_index("node")
    whole = blocks.count * size
    span = width + 2 * HALO
    half = span // 2
    for k in range(nodes):
        for b in range(blocks.count):
            start = (me ^ k) * whole + b * size
            if blocks.lone(b):
                both = parts[k][pl.ds(b * span, half), :]
                rows_ref[rows_at(start, half), :] = both
                rows_ref[pl.ds(start + half, half), :] = turned(both, blocks.half)
            else:
                rows_ref[rows_at(start, span), :] = parts[k][pl.ds(b * span, span), :]
    for b in range(blocks.count):
        own = [pl.ds(m * whole + b * size + HALO, width) for m in range(nodes)]
        state = jnp.concatenate([rows_ref[at, :] for at in own], axis=0)
        blocks.put_natural(nat_ref, b, state.T)
    write_edges(lambda c, i: nat_ref[c, i], nx, ny, comps, lo_ref, hi_ref, side_ref)


def along_second(nat_ref, side_ref, alpha, fy, yp, ym, gp, gm, beside=None):
    comps, nx, ny, nz = nat_ref.shape
    rows = gp.shape[0] // (2 * HALO)

    def prepare(fields, place, plus, minus):
        (flux,), half = halves(fields, (1,))
        for c in range(comps):
            at = place(c)
            plus[at, :], minus[at, :] = split(flux[c], half[c], alpha)

    def own(i, carry):
        prepare([nat_ref[c, i] for c in range(comps)], lambda c: rows_at((c * nx + i) * ny, ny), yp, ym)
        return carry

    lax.fori_loop(0, nx, own, 0, unroll=4)

    def ghost(i, carry):
        def place(c):
            return pl.ds(i * rows + c * nx, nx)

        prepare([side_ref[0, place(c), :] for c in range(comps)], place, gp, gm)
        return carry

    lax.fori_loop(0, 2 * HALO, ghost, 0, unroll=HALO)

    def along(b, carry):
        first = pl.multiple_of(b * TILE, TILE)

        def load(j):
            if HALO <= j < HALO + ny:
                at = pl.ds(first * ny + (j - HALO), TILE, stride=ny)
                return yp[at, :], ym[at, :]
            at = pl.ds((j if j < HALO else j - ny) * rows + first, TILE)
            return gp[at, :], gm[at, :]

        def store(i, value):
            fy[pl.ds(i * rows + first, TILE), :] = value

        if beside is not None:
            beside(b)
        stream(load, store, ny)
        return carry

    lax.fori_loop(0, rows // TILE, along, 0)


def along_last(blocks, nodes, flux, zu, alphas, zf):
    width = blocks.nz // nodes
    size = width + 8
    each = width // CHUNK

    def along(n, carry):
        m = n // each
        start = m * (blocks.count * size) + lax.rem(n, each) * CHUNK
        alpha = alphas[pl.ds(m * TILE, TILE), :]

        def load(j):
            at = pl.ds(start + j, TILE, stride=size)
            return split(flux[at, :], zu[at, :], alpha)

        def store(i, value):
            zf[pl.ds(start + i, TILE, stride=size), :] = value

        stream(load, store, CHUNK)
        return carry

    lax.fori_loop(0, nodes * each, along, 0)


def block_rates(blocks, nodes, zf, b):
    width = blocks.nz // nodes
    size = width + 8
    return jnp.concatenate([zf[rows_at((m * blocks.count + b) * size, width), :] for m in range(nodes)], axis=0)


def along_first(u, alphas, lo_ref, hi_ref, fy, rate, xp, xm, extra, after, unrolled=False):
    comps, nx, ny, nz = rate.shape
    rows = -(-comps * nx // TILE) * TILE
    every = range(comps)

    def prepare(fields, at):
        (flux,), half = halves(fields, (0,))
        for c in every:
            p, m = split(flux[c], half[c], alphas[0])
            xp[at, c * ny : (c + 1) * ny, :] = p
            xm[at, c * ny : (c + 1) * ny, :] = m

    def own(i, carry):
        prepare([u(c, i) for c in every], i + HALO)
        return carry

    lax.fori_loop(0, nx, own, 0, unroll=4)
    for ref, start in ((lo_ref, 0), (hi_ref, nx + HALO)):

        def ghost(i, carry, ref=ref, start=start):
            prepare([ref[0, rows_at((c * HALO + i) * ny, ny), :] for c in every], start + i)
            return carry

        lax.fori_loop(0, HALO, ghost, 0, unroll=HALO)

    def component(c):
        for t in range(0, ny, TILE):

            def load(j, t=t):
                at = rows_at(c * ny + t, TILE)
                return xp[j, at, :], xm[j, at, :]

            def store(i, value, t=t):
                value = value + fy[pl.ds(t * rows + c * nx + i, TILE, stride=rows), :]
                rate[c, i, pl.ds(t, TILE), :] = value if extra is None else value + extra(c, i, t)

            stream(load, store, nx)

    def along(c, carry):
        after(jnp.maximum(c - 1, 0))
        component(c)
        return carry

    if unrolled:
        for c in every:
            if c:
                after(c - 1)
            component(c)
        after(comps - 1)
    else:
        lax.fori_loop(0, comps, along, 0)
        after(jnp.int32(comps - 1))


def tile_rows(tile):
    return [tile[k : k + 1, :] for k in range(3)]


def speeds_of(al_ref, al_out, alphas, nodes):
    tile, spots = speed_tile(jnp.max(al_ref[...], axis=0), nodes)
    al_out[...] = tile
    for m in range(nodes):
        at = 2 * nodes + m
        alphas[m * TILE : (m + 1) * TILE, :] = jnp.broadcast_to(spots[at : at + 1], (TILE, tile.shape[-1])) * 0.5
    return tile


def halves_kernel(rows_ref, zf, *, dims, nodes):
    write_halves(Blocks(*dims), nodes, rows_ref, zf)


def first_lanes_kernel(nat_ref, zu, zf_in, side_ref, al_ref, fy, zf, al_out, *scratch, nodes):
    *scratch, alphas = scratch
    tile = speeds_of(al_ref, al_out, alphas, nodes)
    along_last(Blocks(*nat_ref.shape), nodes, zf_in, zu, alphas, zf)
    along_second(nat_ref, side_ref, tile[1:2], fy, *scratch)


def second_lanes_kernel(
    nat_ref, before_ref, behind_ref, side_ref, al_ref, fz, fy, al_out, zu, zf, *scratch, nodes
):
    *scratch, alphas = scratch
    blocks = Blocks(*nat_ref.shape)
    nz = blocks.nz
    size = nz // nodes + 8
    width = nz // nodes
    for b in range(blocks.count):
        value = blocks.natural(nat_ref, b).T
        for m in range(nodes):
            ghost = pl.ds((m * blocks.count + b) * 4, HALO)
            start = (m * blocks.count + b) * size
            zu[pl.ds(start, HALO), :] = before_ref[ghost, :]
            zu[pl.ds(start + HALO, width), :] = value[m * width : (m + 1) * width]
            zu[pl.ds(start + HALO + width, HALO), :] = behind_ref[ghost, :]
    write_halves(blocks, nodes, zu, zf)
    tile = speeds_of(al_ref, al_out, alphas, nodes)
    along_last(blocks, nodes, zf, zu, alphas, zf)

    def turn(b):
        fz[rows_at(b * nz, nz), :] = block_rates(blocks, nodes, zf, b).T

    assert blocks.count == scratch[2].shape[0] // (2 * HALO) // TILE
    along_second(nat_ref, side_ref, tile[1:2], fy, *scratch, beside=turn)


def first_rows_kernel(nat_in, lo_in, hi_in, al_in, zf, fy, start_ref, *refs, nodes):
    nat_ref, lo_ref, hi_ref, side_ref, first_ref, last_ref, speeds_hbm, rate, xp, xm, tiles_ref, sem = refs
    comps, nx, ny, nz = nat_ref.shape
    blocks = Blocks(comps, nx, ny, nz)
    width = nz // nodes

    def state(value, b):
        rates = value.T + block_rates(blocks, nodes, zf, b)
        start = start_ref[rows_at(b * width, width), :]
        states = []
        for m in range(nodes):
            new = start
            for n in range(nodes):
                new = new + scaled_weight(m, n) * rates[n * width : (n + 1) * width]
            ghost = pl.ds((m * blocks.count + b) * 4, HALO)
            first_ref[ghost, :] = new[:HALO]
            last_ref[ghost, :] = new[width - HALO :]
            states.append(new)
        return jnp.concatenate(states, axis=0).T

    def after(c):
        blocks.put_whole(nat_ref, c, state(blocks.whole(rate, c), c))
        if c % 2 == 1 or c == comps - 1:
            b = comps + c // 2
            blocks.put_leftovers(nat_ref, b, state(blocks.leftovers(rate, *blocks.pair(b)), b))

    along_first(lambda c, i: nat_in[c, i], tile_rows(al_in), lo_in, hi_in, fy, rate, xp, xm, None, after, True)

    def read(c, i):
        return nat_ref[c, i]

    best = tuple(jnp.zeros((ny, nz), jnp.float32) for _ in range(3))
    best = faster(best, read, 0, nx, comps)
    copy = send_speeds([jnp.max(b, axis=0, keepdims=True) for b in best], tiles_ref, speeds_hbm, sem)
    write_edges(read, nx, ny, comps, lo_ref, hi_ref, side_ref)
    copy.wait()


def second_rows_kernel(nat_ref, lo_ref, hi_ref, al_ref, fz, fy, pack_ref, *refs):
    outs, (rate, xp, xm) = refs[:-3], refs[-3:]
    nodes = len(outs)
    comps, nx, ny, nz = nat_ref.shape
    blocks = Blocks(comps, nx, ny, nz)
    width = nz // nodes
    me = lax.axis_index("node")
    weights = [
        [by_node(me, [scaled_weight(n ^ k, j) for n in range(nodes)]) for j in range(nodes)] for k in range(nodes)
    ]
    lanes = lane_index((TILE, nz)) // width

    def extra(c, i, t):
        return fz[rows_at(blocks.row(c, i, t), TILE), :]

    def after(c):
        for t in range(0, ny, TILE):
            for q in range(nx // nodes):
                at = rows_at((c * (nx // nodes) + q) * ny + t, TILE)
                start = pack_ref[at, :]
                rows = [turned(rate[c, q * nodes + i, pl.ds(t, TILE), :], width * i) for i in range(nodes)]
                rates = [
                    turned(merged([rows[(g - j) % nodes] for g in range(nodes)], lanes), width * (me - j))
                    for j in range(nodes)
                ]
                for k in range(nodes):
                    value = start
                    for j in range(nodes):
                        value = value + weights[k][j] * rates[j]
                    outs[k][at, :] = value

    along_first(lambda c, i: nat_ref[c, i], tile_rows(al_ref), lo_ref, hi_ref, fy, rate, xp, xm, extra, after, True)


def close_kernel(*refs):
    parts, (out_hbm, out_ref, sems) = refs[:-3], refs[-3:]
    nodes = len(parts)
    comps, nx, ny, nz = out_ref.shape
    width = nz // nodes
    me = lax.axis_index("node")
    lanes = lane_index((ny, nz)) // width
    copies = []
    for c in range(comps):
        for q in range(nx // nodes):
            at = pl.ds((c * (nx // nodes) + q) * ny, ny)
            values = [part[at, :] for part in parts]
            for i in range(nodes):
                out = values[0]
                for k in range(1, nodes):
                    out = jnp.where(lanes == lax.rem((me ^ k) + i, nodes), values[k], out)
                out_ref[c, q * nodes + i] = turned(out, -width * i)
        copies.append(pltpu.make_async_copy(out_ref.at[c], out_hbm.at[0, c], sems.at[c]))
        copies[-1].start()
    for copy in copies:
        copy.wait()


def call(kernel, name, outs, operands, scratch=(), flops=500_000_000, anywhere=False, outside=(), aliases=None):
    vmem, hbm = pl.BlockSpec(memory_space=pltpu.VMEM), pl.BlockSpec(memory_space=pltpu.HBM)
    moved = sum(4 * x.size for x in operands)
    scratch = [pltpu.VMEM(x, jnp.float32) if isinstance(x, tuple) else x for x in scratch]
    return pl.pallas_call(
        kernel,
        out_shape=[jax.ShapeDtypeStruct(shape, jnp.float32) for shape in outs],
        in_specs=[hbm if anywhere else vmem] * len(operands),
        out_specs=[hbm if n in outside else vmem for n in range(len(outs))],
        scratch_shapes=scratch,
        input_output_aliases=aliases or {},
        compiler_params=pltpu.CompilerParams(vmem_limit_bytes=32 * 1024 * 1024),
        cost_estimate=pl.CostEstimate(flops=flops, bytes_accessed=2 * moved, transcendentals=0),
        name=name,
    )(*operands)


def shifted(value, axis, by):
    count = lax.axis_size(axis)
    return lax.ppermute(value, axis, [(i, (i + by) % count) for i in range(count)])


def swapped(value, by):
    return lax.ppermute(value, "node", [(i, i ^ by) for i in range(lax.axis_size("node"))])


def beside(side):
    if lax.axis_size("gy") == 2:
        return shifted(side, "gy", 1)
    half = side.shape[1] // 2
    return jnp.concatenate([shifted(side[:, :half], "gy", 1), shifted(side[:, half:], "gy", -1)], axis=1)


def across(lo, hi):
    return shifted(hi, "gx", 1), shifted(lo, "gx", -1)


def exchanged(parts):
    moved = {k: swapped(parts[k], k) for k in sorted(range(1, len(parts)), reverse=True)}
    return [parts[0]] + [moved[k] for k in range(1, len(parts))]


def local(initial, guesses):
    comps, nx, ny, nz = initial.shape
    nodes = lax.axis_size("node")
    everyone = ("node", "gx", "gy")
    devices = nodes * lax.axis_size("gx") * lax.axis_size("gy")
    rows = -(-comps * nx // TILE) * TILE
    blocks = Blocks(comps, nx, ny, nz)
    width = nz // nodes
    assert blocks.count == TILE and width % CHUNK == 0 and nx % nodes == 0
    edge = (1, comps * HALO * ny, nz)
    edges = [edge, edge, (1, 2 * HALO * rows, nz)]
    tile_shape = (TILE, nz)
    speeds_shape = (devices, TILE, nz)
    part = (blocks.count * (width + 8), nz)
    pack = (comps * nx // nodes * ny, nz)
    ghost = (nodes * blocks.count * 4, nz)
    depth_shape = (blocks.count * nz, nz)
    lanes_scratch = [(ny * rows, nz)] * 2 + [(2 * HALO * rows, nz)] * 2 + [(nodes * TILE, nz)]
    whole = (nodes * part[0], nz)
    slabs = [initial.shape] + [(nx + 2 * HALO, comps * ny, nz)] * 2
    ring = (blocks.count * (nz + 2 * TILE), nz)

    *parts, speeds = call(
        open_kernel,
        "open_kernel",
        [(blocks.message(width), nz)] * nodes + [speeds_shape],
        [guesses],
        [ring, speeds_shape, pltpu.SemaphoreType.DMA],
        outside=(nodes,),
    )
    speeds = lax.all_to_all(speeds, everyone, 0, 0)
    parts = exchanged(parts)
    turned_field, field, lo, hi, side = call(
        gather_kernel, "gather_kernel", [whole, initial.shape] + edges, parts
    )
    side = beside(side)
    lower, upper = across(lo, hi)
    initial, side = lax.optimization_barrier((initial, side))
    start, start_pack = call(
        functools.partial(start_kernel, nodes=nodes),
        "start_kernel",
        [(blocks.count * width, nz), pack],
        [initial],
        [depth_shape],
    )
    (fluxes,) = call(
        functools.partial(halves_kernel, dims=initial.shape, nodes=nodes), "halves_kernel", [whole], [turned_field]
    )
    fluxes, start, start_pack = lax.optimization_barrier((fluxes, start, start_pack))
    rates, depth, tile = call(
        functools.partial(first_lanes_kernel, nodes=nodes),
        "first_lanes_kernel",
        [(ny * rows, nz), whole, tile_shape],
        [field, turned_field, fluxes, side, speeds],
        lanes_scratch,
        4_000_000_000,
        aliases={2: 1},
    )
    field, lo, hi, side, first, last, speeds = call(
        functools.partial(first_rows_kernel, nodes=nodes),
        "first_rows_kernel",
        [initial.shape] + edges + [ghost, ghost, speeds_shape],
        [field, lower, upper, tile, depth, rates, start],
        slabs + [speeds_shape, pltpu.SemaphoreType.DMA],
        2_500_000_000,
        outside=(6,),
        aliases={0: 0, 1: 1, 2: 2},
    )
    speeds = lax.all_to_all(speeds, everyone, 0, 0)
    before, behind = shifted(last, "node", 1), shifted(first, "node", -1)
    side = beside(side)
    lower, upper = across(lo, hi)
    depth, rates, tile = call(
        functools.partial(second_lanes_kernel, nodes=nodes),
        "second_lanes_kernel",
        [depth_shape, (ny * rows, nz), tile_shape],
        [field, before, behind, side, speeds],
        [whole, whole] + lanes_scratch,
        4_000_000_000,
    )
    outs = call(
        second_rows_kernel,
        "second_rows_kernel",
        [pack] * nodes,
        [field, lower, upper, tile, depth, rates, start_pack],
        slabs,
        2_500_000_000,
    )
    (states,) = call(
        close_kernel,
        "close_kernel",
        [(1,) + initial.shape],
        exchanged(outs),
        [initial.shape, pltpu.SemaphoreType.DMA((comps,))],
        outside=(0,),
    )
    return states


def solution(mesh):
    return jax.shard_map(
        local,
        mesh=mesh,
        in_specs=(P(None, "gx", "gy", None), P("node", None, "gx", "gy", None)),
        out_specs=P("node", None, "gx", "gy", None),
        check_vma=False,
    )
```
